32 devices in a mesh: dp: 4 (over y, x), blk: 8 (over z, core).
Axes of the slice: x: 2, y: 2, z: 4, core: 2. Of those that a mesh axis runs over, the one named last changes fastest.
Arguments:
- tokens: bfloat16 [7168, 2048], P(('dp', 'blk')), may hold values from -6 to 6
- cotangent: bfloat16 [7168, 2048], P(('dp', 'blk')), may hold values from -6 to 6
- document_length_list: int32 [4, 3], P('dp'), may hold values from 1 to 1790, as said below
- attention_norm_gain: float32 [2048], replicated, may hold values from 0.5 to 1.5
- feedforward_norm_gain: float32 [2048], replicated, may hold values from 0.5 to 1.5
- frozen_query_key_value: bfloat16 [3, 2048, 2048], P(None, None, 'blk'), may hold values from -0.125 to 0.125
- query_key_value_downmap: float32 [3, 2048, 16], replicated, may hold values from -0.125 to 0.125
- query_key_value_upmap: float32 [3, 16, 2048], replicated, may hold values from -0.3 to 0.3
- query_key_value_norm: float32 [3, 2048], replicated, may hold values from 0.8 to 2
- frozen_output_weight: bfloat16 [2048, 2048], P(None, 'blk'), may hold values from -0.125 to 0.125
- output_adapter_downmap: float32 [2048, 16], replicated, may hold values from -0.125 to 0.125
- output_adapter_upmap: float32 [16, 2048], replicated, may hold values from -0.3 to 0.3
- output_column_norm: float32 [2048], replicated, may hold values from 3 to 12
- frozen_gate_up_weight: bfloat16 [2, 2048, 5632], P(None, None, 'blk'), may hold values from -0.125 to 0.125
- gate_up_adapter_downmap: float32 [2, 2048, 16], replicated, may hold values from -0.125 to 0.125
- gate_up_adapter_upmap: float32 [2, 16, 5632], replicated, may hold values from -0.3 to 0.3
- gate_up_column_norm: float32 [2, 5632], replicated, may hold values from 0.8 to 2
- frozen_down_weight: bfloat16 [5632, 2048], P(None, 'blk'), may hold values from -0.078125 to 0.078125
- down_adapter_downmap: float32 [5632, 16], replicated, may hold values from -0.078125 to 0.078125
- down_adapter_upmap: float32 [16, 2048], replicated, may hold values from -0.3 to 0.3
- down_column_norm: float32 [2048], replicated, may hold values from 1 to 3
Outputs:
- result: bfloat16 [7168, 2048], P(('dp', 'blk'))
- grad_input: float32 [7168, 2048], P(('dp', 'blk'))
- grad_gain_attn: float32 [2048], replicated
- grad_gain_ffn: float32 [2048], replicated
- grad_a_qkv: float32 [3, 2048, 16], replicated
- grad_b_qkv: float32 [3, 16, 2048], replicated
- grad_mag_qkv: float32 [3, 2048], replicated
- grad_a_out: float32 [2048, 16], replicated
- grad_b_out: float32 [16, 2048], replicated
- grad_mag_out: float32 [2048], replicated
- grad_a_gu: float32 [2, 2048, 16], replicated
- grad_b_gu: float32 [2, 16, 5632], replicated
- grad_mag_gu: float32 [2, 5632], replicated
- grad_a_down: float32 [5632, 16], replicated
- grad_b_down: float32 [16, 2048], replicated
- grad_mag_down: float32 [2048], replicated
The draws below stay inside these ranges and needn't reach their ends.
Inputs may be any that keep to these rules, and one draw needn't show every extreme that they name: `document_length_list`: each row lists the lengths of the 3 documents packed in order into one slot of 1792 positions; a row sums to at most 1792, and the positions after its documents are padding.
All inputs are finite; a program needn't handle non-finite values.
Results may differ from the reference program's by a relative error of at most 0.03.
Values may be sent and summed in bfloat16 or wider, within the bound.
No kernel may reach another device: no remote copies, remote signals or barrier semaphores. Data moves between devices by JAX's collectives and lax.ppermute only.
A program may use at most 448 MiB of HBM per device.

```python
import math
from functools import partial
import jax
import jax.numpy as jnp
from jax import lax

MODEL_WIDTH = 2048
HEADS = 16
HIDDEN_UNITS = 5632
ADAPTER_RANK = 16
ALPHA = 32
NDOC = 3
TOK_DEV = 224
HDIM = 128
SEQ = 1792
SLOTS = 4
TOKENS = 7168


def draw_document_length_list(key, part):
    key = jax.random.fold_in(key, 11)
    quarter = max(TOK_DEV // 4, 1)
    short_key, pad_key, long_key, slot_key = jax.random.split(key, 4)
    full_slot = jax.random.randint(slot_key, (), 0, SLOTS, dtype=jnp.int32)
    is_full = jnp.arange(SLOTS, dtype=jnp.int32) == full_slot
    shorts = jax.random.randint(short_key, (SLOTS, NDOC), 1, quarter + 1, dtype=jnp.int32)
    shorts = jnp.where(is_full[:, None], 1, shorts)
    padding = jax.random.randint(pad_key, (SLOTS,), 0, quarter + 1, dtype=jnp.int32)
    padding = jnp.where(is_full, 0, padding)
    chosen = jax.random.randint(long_key, (SLOTS,), 0, NDOC, dtype=jnp.int32)
    is_long = jnp.arange(NDOC, dtype=jnp.int32)[None, :] == chosen[:, None]
    others = jnp.sum(jnp.where(is_long, 0, shorts), axis=1, dtype=jnp.int32)
    longest = SEQ - others - padding
    return jnp.where(is_long, longest[:, None], shorts).astype(jnp.int32)


def shard_levels(rng, shape, shards, smallest, largest):
    def one(position, blocks):
        heights = jax.random.uniform(jax.random.fold_in(jax.random.fold_in(rng, 6), position), (blocks,), jnp.float32, smallest / len(shards), largest / len(shards))
        return jnp.repeat(jnp.exp(heights), shape[position] // blocks).reshape((-1,) + (1,) * (len(shape) - position - 1))

    level = one(*shards[0])
    for cut in shards[1:]:
        level = level * one(*cut)
    return level


def scatter_about(rng, dims, deviation, bound, cuts=(), kind=jnp.bfloat16):
    drawn = jax.random.normal(rng, dims, jnp.float32) * deviation
    if len(cuts) > 0:
        drawn = shard_levels(rng, dims, cuts, -0.22, 0.18) * drawn
    return jnp.clip(drawn, min=-bound, max=bound).astype(kind)


def setup_inputs(seed: int = 0) -> dict:
    key_list = jax.random.split(jax.random.key(seed), 22)
    return {
        "tokens": scatter_about(key_list[0], (TOKENS, MODEL_WIDTH), 1.0, 6.0, ((0, 32),)),
        "cotangent": scatter_about(key_list[1], (TOKENS, MODEL_WIDTH), 1.0, 6.0, ((0, 32),)),
        "document_length_list": draw_document_length_list(jax.random.fold_in(key_list[21], 71), 0),
        "attention_norm_gain": jnp.clip(1.0 + 0.1 * jax.random.normal(key_list[3], (MODEL_WIDTH,), jnp.float32), 0.5, 1.5),
        "feedforward_norm_gain": jnp.clip(1.0 + 0.1 * jax.random.normal(key_list[4], (MODEL_WIDTH,), jnp.float32), 0.5, 1.5),
        "frozen_query_key_value": scatter_about(key_list[5], (3, MODEL_WIDTH, MODEL_WIDTH), MODEL_WIDTH ** -0.5, 0.125, ((2, 8),)),
        "query_key_value_downmap": scatter_about(key_list[6], (3, MODEL_WIDTH, ADAPTER_RANK), MODEL_WIDTH ** -0.5, 0.125, (), jnp.float32),
        "query_key_value_upmap": scatter_about(key_list[7], (3, ADAPTER_RANK, MODEL_WIDTH), 0.05, 0.3, (), jnp.float32),
        "query_key_value_norm": jnp.clip(jnp.exp(jax.random.uniform(key_list[8], (3, MODEL_WIDTH), jnp.float32, math.log(0.8), math.log(2.0))), 0.8, 2.0),
        "frozen_output_weight": scatter_about(key_list[9], (MODEL_WIDTH, MODEL_WIDTH), MODEL_WIDTH ** -0.5, 0.125, ((1, 8),)),
        "output_adapter_downmap": scatter_about(key_list[10], (MODEL_WIDTH, ADAPTER_RANK), MODEL_WIDTH ** -0.5, 0.125, (), jnp.float32),
        "output_adapter_upmap": scatter_about(key_list[11], (ADAPTER_RANK, MODEL_WIDTH), 0.05, 0.3, (), jnp.float32),
        "output_column_norm": jnp.clip(jnp.exp(jax.random.uniform(key_list[12], (MODEL_WIDTH,), jnp.float32, math.log(3.0), math.log(12.0))), 3.0, 12.0),
        "frozen_gate_up_weight": scatter_about(key_list[13], (2, MODEL_WIDTH, HIDDEN_UNITS), MODEL_WIDTH ** -0.5, 0.125, ((2, 8),)),
        "gate_up_adapter_downmap": scatter_about(key_list[14], (2, MODEL_WIDTH, ADAPTER_RANK), MODEL_WIDTH ** -0.5, 0.125, (), jnp.float32),
        "gate_up_adapter_upmap": scatter_about(key_list[15], (2, ADAPTER_RANK, HIDDEN_UNITS), 0.05, 0.3, (), jnp.float32),
        "gate_up_column_norm": jnp.clip(jnp.exp(jax.random.uniform(key_list[16], (2, HIDDEN_UNITS), jnp.float32, math.log(0.8), math.log(2.0))), 0.8, 2.0),
        "frozen_down_weight": scatter_about(key_list[17], (HIDDEN_UNITS, MODEL_WIDTH), HIDDEN_UNITS ** -0.5, 0.078125, ((1, 8),)),
        "down_adapter_downmap": scatter_about(key_list[18], (HIDDEN_UNITS, ADAPTER_RANK), HIDDEN_UNITS ** -0.5, 0.078125, (), jnp.float32),
        "down_adapter_upmap": scatter_about(key_list[19], (ADAPTER_RANK, MODEL_WIDTH), 0.05, 0.3, (), jnp.float32),
        "down_column_norm": jnp.clip(jnp.exp(jax.random.uniform(key_list[20], (MODEL_WIDTH,), jnp.float32, math.log(1.0), math.log(3.0))), 1.0, 3.0),
    }


norm_eps = 1e-05
column_eps = 1e-06
rope_base = 10000.0
far_negative = -1e+30

@jax.custom_vjp
def low(v):
    return lax.optimization_barrier(v.astype(jnp.bfloat16)).astype(jnp.float32)

@jax.custom_vjp
def low_back(v):
    return v

def low_keep(v):
    return (low(v), None)

def low_pass(kept, grad):
    return (grad,)

def back_keep(v):
    return (v, None)

def back_low(kept, grad):
    return (low(grad),)
low.defvjp(low_keep, low_pass)
low_back.defvjp(back_keep, back_low)

def layout(lens_row, first, count):
    places = first + jnp.arange(count, dtype=jnp.int32)
    ends = jnp.cumsum(lens_row, dtype=jnp.int32)
    after = (places[:, None] >= ends[None, :]).astype(jnp.int32)
    segment = lax.optimization_barrier(jnp.sum(after, axis=1, dtype=jnp.int32))
    begins = lax.optimization_barrier(jnp.sum(after * lens_row[None, :], axis=1, dtype=jnp.int32))
    offset = (places - begins).astype(jnp.float32)
    return (places, segment, offset, places < ends[-1])

def angles(offset):
    half = HDIM // 2
    freq = rope_base ** (-(jnp.arange(half, dtype=jnp.float32) * 2.0 / HDIM))
    turn = offset[:, None] * freq[None, :]
    return (jnp.cos(turn)[:, None, :], jnp.sin(turn)[:, None, :])

def rotate(values, cosine, sine):
    count = values.shape[0]
    split = values.reshape(count, HEADS, HDIM)
    half = HDIM // 2
    first, second = (split[..., :half], split[..., half:])
    turned = jnp.concatenate([first * cosine - second * sine, second * cosine + first * sine], axis=2)
    return turned.reshape(count, MODEL_WIDTH)

def normalize(values, gain):
    inverse = lax.rsqrt(lax.optimization_barrier(jnp.mean(values * values, axis=-1, keepdims=True)) + norm_eps)
    return values * inverse * gain

def combine_weight(frozen_matrix, adapter_downmap, adapter_upmap, column_magnitude):
    adapter_factor_scale = ALPHA / ADAPTER_RANK
    unit_direction = frozen_matrix + adapter_factor_scale * jnp.einsum('meg,mgt->met', adapter_downmap, adapter_upmap, precision=lax.Precision.HIGHEST)
    column_norms = jnp.sqrt(lax.optimization_barrier(jnp.sum(unit_direction * unit_direction, axis=1)) + column_eps)
    return low(unit_direction * (column_magnitude / column_norms)[:, None, :])

def attend(allowed, trio):
    head_q, head_k, head_v = trio
    scores = low_back(jnp.dot(head_q, head_k.T, precision=lax.Precision.HIGHEST) * HDIM ** (-0.5))
    masked = jnp.where(allowed, scores, far_negative)
    top = lax.optimization_barrier(jnp.max(masked, axis=-1, keepdims=True))
    total = lax.optimization_barrier(jnp.sum(jnp.where(allowed, jnp.exp(masked - top), 0.0), axis=-1, keepdims=True))
    lse = top + jnp.log(total)
    probs = jnp.where(allowed, jnp.exp(masked - lse), 0.0)
    return jnp.dot(low(probs), head_v, precision=lax.Precision.HIGHEST)

def by_heads(values):
    return jnp.transpose(values.reshape(SEQ, HEADS, HDIM), (1, 0, 2))

def layer(weights, attention_norm_gain, feedforward_norm_gain, input_rows, lens_row):
    w_qkv, w_out, w_gu, w_down = weights
    places, segment, offset, valid = layout(lens_row, 0, SEQ)
    allowed = (segment[None, :] == segment[:, None]) & (places[None, :] <= places[:, None])
    cosine, sine = angles(offset)
    h_one = low(normalize(input_rows, attention_norm_gain))
    triple = jnp.einsum('ti,kio->kto', h_one, w_qkv, precision=lax.Precision.HIGHEST)
    queries = low(rotate(low_back(triple[0]), cosine, sine))
    keys = low(rotate(low_back(triple[1]), cosine, sine))
    values = low(low_back(triple[2]))
    mixed = lax.map(jax.checkpoint(partial(attend, allowed)), (by_heads(queries), by_heads(keys), by_heads(values)))
    attended = low(low_back(jnp.transpose(mixed, (1, 0, 2)).reshape(SEQ, MODEL_WIDTH)))
    residual = input_rows + low_back(jnp.dot(attended, w_out[0], precision=lax.Precision.HIGHEST))
    h_two = low(normalize(residual, feedforward_norm_gain))
    pair = jnp.einsum('ti,kio->kto', h_two, w_gu, precision=lax.Precision.HIGHEST)
    gate = low_back(pair[0])
    upward = low_back(pair[1])
    act = low(jax.nn.silu(gate) * upward)
    return residual + low_back(jnp.dot(act, w_down[0], precision=lax.Precision.HIGHEST))

def reference(tokens, cotangent, document_length_list, attention_norm_gain, feedforward_norm_gain, frozen_query_key_value, query_key_value_downmap, query_key_value_upmap, query_key_value_norm, frozen_output_weight, output_adapter_downmap, output_adapter_upmap, output_column_norm, frozen_gate_up_weight, gate_up_adapter_downmap, gate_up_adapter_upmap, gate_up_column_norm, frozen_down_weight, down_adapter_downmap, down_adapter_upmap, down_column_norm):
    frozen = (frozen_query_key_value.astype(jnp.float32), frozen_output_weight.astype(jnp.float32)[None], frozen_gate_up_weight.astype(jnp.float32), frozen_down_weight.astype(jnp.float32)[None])
    trainable_params = (attention_norm_gain, feedforward_norm_gain, query_key_value_downmap, query_key_value_upmap, query_key_value_norm, output_adapter_downmap, output_adapter_upmap, output_column_norm, gate_up_adapter_downmap, gate_up_adapter_upmap, gate_up_column_norm, down_adapter_downmap, down_adapter_upmap, down_column_norm)
    x_all = tokens.astype(jnp.float32).reshape(SLOTS, SEQ, MODEL_WIDTH)
    valid_all = jax.vmap(lambda row: layout(row, 0, SEQ)[3])(document_length_list)

    def forward(params, inputs_all):
        g_attn, g_ffn, a_qkv, b_qkv, m_qkv, a_out, b_out, m_out, a_gu, b_gu, m_gu, a_down, b_down, m_down = params
        weights = (combine_weight(frozen[0], a_qkv, b_qkv, m_qkv), combine_weight(frozen[1], a_out[None], b_out[None], m_out[None]), combine_weight(frozen[2], a_gu, b_gu, m_gu), combine_weight(frozen[3], a_down[None], b_down[None], m_down[None]))

        def one(running_state, slot):
            return (running_state, jax.checkpoint(layer)(weights, g_attn, g_ffn, slot[0], slot[1]))
        return lax.scan(one, jnp.zeros((), jnp.float32), (inputs_all, document_length_list))[1]
    final, pullback = jax.vjp(forward, trainable_params, x_all)
    d_final = cotangent.astype(jnp.float32).reshape(SLOTS, SEQ, MODEL_WIDTH) * valid_all.astype(jnp.float32)[:, :, None]
    gradient_tuple, d_inputs = pullback(d_final)
    return (final.reshape(TOKENS, MODEL_WIDTH).astype(jnp.bfloat16), d_inputs.reshape(TOKENS, MODEL_WIDTH), gradient_tuple[0], gradient_tuple[1], gradient_tuple[2], gradient_tuple[3], gradient_tuple[4], gradient_tuple[5], gradient_tuple[6], gradient_tuple[7], gradient_tuple[8], gradient_tuple[9], gradient_tuple[10], gradient_tuple[11], gradient_tuple[12], gradient_tuple[13])
```

```python
import functools

import jax
import jax.numpy as jnp
from jax import lax
from jax.experimental import pallas as pl
from jax.experimental.pallas import tpu as pltpu
from jax.sharding import PartitionSpec as P

MODEL_WIDTH = 2048
HEADS = 16
ADAPTER_RANK = 16
ALPHA = 32
HDIM = 128
TILE = 256
QUAD = 4

norm_eps = 1e-05
column_eps = 1e-06
rope_base = 10000.0
far_negative = -1e30
adapter_scale = ALPHA / ADAPTER_RANK
bf16 = jnp.bfloat16
f32 = jnp.float32
NT = (((1,), (1,)), ((), ()))
TN = (((0,), (0,)), ((), ()))
NN = (((1,), (0,)), ((), ()))


def dot(a, b, dims=NN):
    return lax.dot_general(a, b, dims, preferred_element_type=f32)


def after(array, *earlier):
    return lax.optimization_barrier((array, *earlier))[0]


def blank(shape, dtype):
    return pl.pallas_call(
        lambda out: None,
        out_shape=jax.ShapeDtypeStruct(shape, dtype),
        out_specs=pl.BlockSpec(memory_space=pl.ANY),
        name="blank",
    )()


def swap(array, axis, bit):
    return lax.ppermute(array, axis, [(i, i ^ bit) for i in range(lax.axis_size(axis))])


def axis_sum(array, axis):
    bit = 1
    while bit < lax.axis_size(axis):
        array = array + swap(array, axis, bit)
        bit *= 2
    return array


def begins_of(lens_row, count):
    places = jnp.arange(count, dtype=jnp.int32)
    ends = jnp.cumsum(lens_row, dtype=jnp.int32)
    after = (places[:, None] >= ends[None, :]).astype(jnp.int32)
    return places, jnp.sum(after * lens_row[None, :], axis=1, dtype=jnp.int32), ends[-1]


def split_three(a):
    one = lax.reduce_precision(a, 8, 7)
    rest = a - one
    two = lax.reduce_precision(rest, 8, 7)
    return one.astype(bf16), two.astype(bf16), (rest - two).astype(bf16)


def parts_of(a, b):
    a1, a2, a3 = split_three(a * adapter_scale)
    b1, b2, b3 = split_three(b)
    return (
        jnp.concatenate([a1, a1, a2, a1, a2, a3], axis=-2),
        jnp.concatenate([b1, b2, b1, b3, b2, b1], axis=-2),
    )


def merge_kernel(w_ref, a_ref, b_ref, m_ref, out_ref, n_ref, v_ref):
    rows = w_ref.shape[1]

    def add(i, acc):
        at = pl.ds(pl.multiple_of(i * TILE, TILE), TILE)
        v = w_ref[0, at, :].astype(f32) + dot(a_ref[0, :, at], b_ref[0], TN)
        v_ref[at, :] = v
        return acc + jnp.sum(v * v, axis=0, keepdims=True)

    total = lax.fori_loop(0, rows // TILE, add, jnp.zeros(m_ref.shape, f32), unroll=2)
    norms = jnp.sqrt(total + column_eps)
    n_ref[...] = norms
    s = m_ref[...] / norms

    def put(i, carry):
        at = pl.ds(pl.multiple_of(i * TILE, TILE), TILE)
        out_ref[at, :] = (v_ref[at, :] * s).astype(bf16)
        return carry

    lax.fori_loop(0, rows // TILE, put, 0, unroll=2)


def merge(w, a, b, m):
    k, rows, cols = w.shape
    a_cat, b_cat = parts_of(a, b)
    wide = a_cat.shape[1]
    place = lambda i, h: (0, h * k + i)
    return pl.pallas_call(
        merge_kernel,
        grid=(k, cols // HDIM),
        in_specs=[
            pl.BlockSpec((1, rows, HDIM), lambda i, h: (i, 0, h)),
            pl.BlockSpec((1, wide, rows), lambda i, h: (i, 0, 0)),
            pl.BlockSpec((1, wide, HDIM), lambda i, h: (i, 0, h)),
            pl.BlockSpec((1, HDIM), place),
        ],
        out_specs=[pl.BlockSpec((rows, HDIM), place), pl.BlockSpec((1, HDIM), place)],
        out_shape=[
            jax.ShapeDtypeStruct((rows, k * cols), bf16),
            jax.ShapeDtypeStruct((1, k * cols), f32),
        ],
        scratch_shapes=[pltpu.VMEM((rows, HDIM), f32)],
        compiler_params=pltpu.CompilerParams(vmem_limit_bytes=48 * 2**20),
        cost_estimate=pl.CostEstimate(
            flops=2 * k * rows * cols * wide, bytes_accessed=4 * k * rows * cols, transcendentals=0
        ),
        name="merge",
    )(w, a_cat, b_cat, m)


def merge_rows_kernel(w_ref, a_ref, b_ref, m_ref, out_ref, n_ref):
    out_ref = out_ref.at[0]
    v = w_ref[0].astype(f32) + dot(b_ref[0], a_ref[0], TN)
    norms = jnp.sqrt(jnp.sum(v * v, axis=1, keepdims=True) + column_eps)
    n_ref[0] = norms
    out_ref[0] = (v * (m_ref[0] / norms)).astype(bf16)


def merge_rows(w, a, b, m, mates):
    k, cols, rows = w.shape
    a_cat, b_cat = parts_of(a, b)
    wide = a_cat.shape[1]
    return pl.pallas_call(
        merge_rows_kernel,
        grid=(k,),
        in_specs=[
            pl.BlockSpec((1, cols, rows), lambda i: (i, 0, 0)),
            pl.BlockSpec((1, wide, rows), lambda i: (i, 0, 0)),
            pl.BlockSpec((1, wide, cols), lambda i: (i, 0, 0)),
            pl.BlockSpec((1, cols, 1), lambda i: (i, 0, 0)),
        ],
        out_specs=[
            pl.BlockSpec((1, 1, cols, rows), lambda i: (0, i, 0, 0)),
            pl.BlockSpec((1, cols, 1), lambda i: (i, 0, 0)),
        ],
        out_shape=[
            jax.ShapeDtypeStruct((mates, k, cols, rows), bf16),
            jax.ShapeDtypeStruct((k, cols, 1), f32),
        ],
        compiler_params=pltpu.CompilerParams(vmem_limit_bytes=56 * 2**20),
        cost_estimate=pl.CostEstimate(
            flops=2 * k * rows * cols * wide, bytes_accessed=4 * k * rows * cols, transcendentals=0
        ),
        name="merge_rows",
    )(w, a_cat, b_cat, m)


def turned(u, cosine, sine):
    return u * cosine + pltpu.roll(u, HDIM // 2, 1) * sine


def forward_kernel(
    pre, cosine, sine, begin, q_out, k_out, v_out, att_out, mixed_t, lse_out, v_t
):
    count = pre.shape[0]
    scale = HDIM**-0.5
    for i in range(count // TILE):
        at = pl.ds(i * TILE, TILE)
        cos, sin = cosine[at, :], sine[at, :]
        q_out[at, :] = turned(pre[at, :HDIM], cos, sin).astype(bf16)
        k_out[at, :] = turned(pre[at, HDIM : 2 * HDIM], cos, sin).astype(bf16)
        v = pre[at, 2 * HDIM :]
        v_out[at, :] = v.astype(bf16)
        v_t[:, at] = v.T.astype(bf16)
    for i in range(count // TILE):
        rows = pl.ds(i * TILE, TILE)
        q = q_out[rows, :]
        start = begin[:, rows]

        def visit(j, state, diagonal):
            top, total, mixed = state
            keys = pl.ds(pl.multiple_of(j * TILE, TILE), TILE)
            s = dot(k_out[keys, :], q, NT) * scale
            place = j * TILE + lax.broadcasted_iota(jnp.int32, (TILE, TILE), 0)
            allowed = place >= start
            if diagonal:
                mine = i * TILE + lax.broadcasted_iota(jnp.int32, (TILE, TILE), 1)
                allowed = allowed & (place <= mine)
            s = jnp.where(allowed, s, far_negative)
            high = jnp.maximum(top, jnp.max(s, axis=0, keepdims=True))
            keep = jnp.exp(top - high)
            p = jnp.where(allowed, jnp.exp(s - high), 0.0)
            total = total * keep + jnp.sum(p, axis=0, keepdims=True)
            mixed = mixed * keep + dot(v_t[:, keys], p.astype(bf16))
            return high, total, mixed

        state = (
            jnp.full((1, TILE), far_negative, f32),
            jnp.zeros((1, TILE), f32),
            jnp.zeros((HDIM, TILE), f32),
        )
        state = visit(i, state, True)
        for j in range(i):
            state = visit(j, state, False)
        top, total, mixed = state
        mixed = mixed / total
        mixed_t[:, rows] = mixed
        att_out[rows, :] = mixed.T.astype(bf16)
        lse_out[0, :, rows] = top + jnp.log(total)


def backward_kernel(
    q_ref, k_ref, v_ref, pre, cosine, sine, begin, grad_att, mixed_t, lse,
    g_out, gm_out, dk, dv, k_t,
):
    count = q_ref.shape[0]
    scale = HDIM**-0.5
    dk[...] = jnp.zeros_like(dk)
    dv[...] = jnp.zeros_like(dv)
    for i in range(count // TILE):
        at = pl.ds(i * TILE, TILE)
        k_t[:, at] = k_ref[at, :].astype(f32).T.astype(bf16)
    gm_q = jnp.zeros((1, HDIM), f32)
    for i in range(count // TILE):
        rows = pl.ds(i * TILE, TILE)
        q = q_ref[rows, :]
        d_mixed = grad_att[rows, :]
        delta = jnp.sum(d_mixed.astype(f32).T * mixed_t[:, rows], axis=0, keepdims=True)
        start = begin[:, rows]
        high = lse[0, :, rows]
        dq_t = jnp.zeros((HDIM, TILE), f32)
        for j in range(i + 1):
            keys = pl.ds(j * TILE, TILE)
            s = dot(k_ref[keys, :], q, NT) * scale
            place = j * TILE + lax.broadcasted_iota(jnp.int32, (TILE, TILE), 0)
            allowed = place >= start
            if j == i:
                mine = i * TILE + lax.broadcasted_iota(jnp.int32, (TILE, TILE), 1)
                allowed = allowed & (place <= mine)
            p = jnp.where(allowed, jnp.exp(s - high), 0.0)
            dp = dot(v_ref[keys, :], d_mixed, NT)
            ds = (p * (dp - delta)).astype(bf16)
            dv[keys, :] += dot(p.astype(bf16), d_mixed)
            dk[keys, :] += dot(ds, q)
            dq_t = dq_t + dot(k_t[:, keys], ds)
        gq = turned(dq_t.T * scale, cosine[rows, :], -sine[rows, :]).astype(bf16)
        g_out[rows, :HDIM] = gq
        gm_q = gm_q + jnp.sum(gq.astype(f32) * pre[rows, :HDIM], axis=0, keepdims=True)
    gm_k = jnp.zeros((1, HDIM), f32)
    gm_v = jnp.zeros((1, HDIM), f32)
    for i in range(count // TILE):
        at = pl.ds(i * TILE, TILE)
        gk = turned(dk[at, :] * scale, cosine[at, :], -sine[at, :]).astype(bf16)
        g_out[at, HDIM : 2 * HDIM] = gk
        gm_k = gm_k + jnp.sum(gk.astype(f32) * pre[at, HDIM : 2 * HDIM], axis=0, keepdims=True)
        gv = dv[at, :].astype(bf16)
        g_out[at, 2 * HDIM :] = gv
        gm_v = gm_v + jnp.sum(gv.astype(f32) * pre[at, 2 * HDIM :], axis=0, keepdims=True)
    gm_out[0:1, :HDIM] = gm_q
    gm_out[0:1, HDIM : 2 * HDIM] = gm_k
    gm_out[0:1, 2 * HDIM :] = gm_v


def attention_forward(triple, cosine, sine, begin):
    count, width = triple.shape[0], triple.shape[1] // 3
    heads = width // HDIM
    whole = lambda h: (0, 0)
    head = lambda h: (0, h)
    tall = lambda at: pl.BlockSpec((count, HDIM), at)
    return pl.pallas_call(
        forward_kernel,
        grid=(heads,),
        in_specs=[
            pl.BlockSpec((count, 3 * HDIM), head),
            tall(whole),
            tall(whole),
            pl.BlockSpec((1, count), whole),
        ],
        out_specs=[
            tall(head),
            tall(head),
            tall(head),
            tall(head),
            pl.BlockSpec((HDIM, count), lambda h: (h, 0)),
            pl.BlockSpec((1, 1, count), lambda h: (h, 0, 0)),
        ],
        out_shape=[jax.ShapeDtypeStruct((count, width), bf16)] * 4
        + [
            jax.ShapeDtypeStruct((width, count), f32),
            jax.ShapeDtypeStruct((heads, 1, count), f32),
        ],
        scratch_shapes=[pltpu.VMEM((HDIM, count), bf16)],
        compiler_params=pltpu.CompilerParams(vmem_limit_bytes=48 * 2**20),
        cost_estimate=pl.CostEstimate(
            flops=2 * count * count * width, bytes_accessed=30 * count * width, transcendentals=0
        ),
        name="attend",
    )(triple, cosine, sine, begin)


def attention_backward(q, k, v, triple, cosine, sine, begin, grad_att, mixed_t, lse):
    count, width = q.shape
    heads = width // HDIM
    whole = lambda h: (0, 0)
    head = lambda h: (0, h)
    tall = lambda at: pl.BlockSpec((count, HDIM), at)
    return pl.pallas_call(
        backward_kernel,
        grid=(heads,),
        in_specs=[
            tall(head),
            tall(head),
            tall(head),
            pl.BlockSpec((count, 3 * HDIM), head),
            tall(whole),
            tall(whole),
            pl.BlockSpec((1, count), whole),
            tall(head),
            pl.BlockSpec((HDIM, count), lambda h: (h, 0)),
            pl.BlockSpec((1, 1, count), lambda h: (h, 0, 0)),
        ],
        out_specs=[pl.BlockSpec((count, 3 * HDIM), head), pl.BlockSpec((8, 3 * HDIM), head)],
        out_shape=[
            jax.ShapeDtypeStruct((count, 3 * width), bf16),
            jax.ShapeDtypeStruct((8, 3 * width), f32),
        ],
        scratch_shapes=[
            pltpu.VMEM((count, HDIM), f32),
            pltpu.VMEM((count, HDIM), f32),
            pltpu.VMEM((HDIM, count), bf16),
        ],
        compiler_params=pltpu.CompilerParams(vmem_limit_bytes=48 * 2**20),
        cost_estimate=pl.CostEstimate(
            flops=5 * count * count * width, bytes_accessed=40 * count * width, transcendentals=0
        ),
        name="attend_back",
    )(q, k, v, triple, cosine, sine, begin, grad_att, mixed_t, lse)


def feed_kernel(gu_ref, down_ref, h_ref, d_ref, acts_out, g_out, gm_out):
    h = h_ref[...]
    gate = dot(gu_ref[0, 0], h, NT)
    upward = dot(gu_ref[0, 1], h, NT)
    d_act = dot(down_ref[...], d_ref[...], NT)
    sigmoid_gate = jax.nn.sigmoid(gate)
    silu = gate * sigmoid_gate
    acts_out[...] = (silu * upward).astype(bf16)
    d_gate = (d_act * upward * sigmoid_gate * (1.0 + gate * (1.0 - sigmoid_gate))).astype(bf16)
    d_upward = (d_act * silu).astype(bf16)
    g_out[0, 0] = d_gate
    g_out[0, 1] = d_upward
    gm_out[0, 0] = jnp.sum(d_gate.astype(f32) * gate, axis=1, keepdims=True)
    gm_out[0, 1] = jnp.sum(d_upward.astype(f32) * upward, axis=1, keepdims=True)


def feed_forward(gu, down, h, d, mates):
    rows, width = h.shape
    hidden = down.shape[0] // mates
    unit = hidden // max(1, hidden // 176)
    steps = hidden // unit
    flat = lambda k, j: (k * steps + j, 0)
    deep = lambda k, j: (k, 0, j, 0)
    whole = lambda k, j: (0, 0)
    acts, g, gm = pl.pallas_call(
        feed_kernel,
        grid=(mates, steps),
        in_specs=[
            pl.BlockSpec((1, 2, unit, width), deep),
            pl.BlockSpec((unit, width), flat),
            pl.BlockSpec((rows, width), whole),
            pl.BlockSpec((rows, width), whole),
        ],
        out_specs=[
            pl.BlockSpec((unit, rows), flat),
            pl.BlockSpec((1, 2, unit, rows), deep),
            pl.BlockSpec((1, 2, unit, 1), deep),
        ],
        out_shape=[
            jax.ShapeDtypeStruct((mates * hidden, rows), bf16),
            jax.ShapeDtypeStruct((mates, 2, hidden, rows), bf16),
            jax.ShapeDtypeStruct((mates, 2, hidden, 1), f32),
        ],
        compiler_params=pltpu.CompilerParams(vmem_limit_bytes=48 * 2**20),
        cost_estimate=pl.CostEstimate(
            flops=6 * mates * hidden * rows * width,
            bytes_accessed=6 * mates * hidden * width + 4 * rows * width,
            transcendentals=0,
        ),
        name="feed_forward",
    )(gu.reshape(mates, 2, hidden, width), down, h, d)
    return acts, g.reshape(2 * mates * hidden, rows), gm


def normalize(values, gain):
    inverse = lax.rsqrt(jnp.mean(values * values, axis=-1, keepdims=True) + norm_eps)
    return (values * inverse * gain, inverse)


def normalize_back(values, inverse, gain, grad):
    unit = values * inverse
    scaled = grad * gain
    return inverse * (scaled - unit * jnp.mean(scaled * unit, axis=-1, keepdims=True))


def quad_gather(block):
    pair = jnp.concatenate([block, swap(block, "blk", 2)], axis=0)
    return jnp.concatenate([pair, swap(pair, "blk", 1)], axis=0)


def quad_halve(parts):
    half = parts.shape[0] // 2
    return parts[:half].astype(f32) + swap(parts[half:], "blk", 1).astype(f32)


def quad_finish(mine):
    half = mine.shape[0] // 2
    return mine[:half] + swap(mine[half:].astype(bf16), "blk", 2).astype(f32)


def step_chips(array, first, last, by):
    pairs = [(2 * i + c, 2 * (i + by) + c) for i in range(first, last + 1) for c in range(2)]
    return lax.ppermute(array, "blk", pairs)


def core_scatter(parts):
    chips = lax.axis_size("blk") // 2
    core = lax.axis_index("blk") % 2
    parts = parts.reshape(chips, 2, parts.shape[0] // (2 * chips), parts.shape[1])
    take = lambda c: lax.dynamic_index_in_dim(parts, c, 1, keepdims=False)
    return (take(core).astype(f32) + swap(take(1 - core), "blk", 1).astype(f32)).astype(bf16)


def chips_step(total, t, state):
    chips = total.shape[0]
    chip = lax.axis_index("blk") // 2
    pick = lambda c: lax.dynamic_index_in_dim(
        total, jnp.clip(c, 0, chips - 1), 0, keepdims=False
    )
    up, down = pick(chips - t + chip), pick(t - chips + chip)
    if t > 1:
        up = (up.astype(f32) + state[0].astype(f32)).astype(bf16)
        down = (down.astype(f32) + state[1].astype(f32)).astype(bf16)
    up, down = after((up, down))
    return step_chips(up, 0, t - 1, 1), step_chips(down, chips - t, chips - 1, -1)


def chips_end(total, state):
    chip = lax.axis_index("blk") // 2
    own = lax.dynamic_index_in_dim(total, chip, 0, keepdims=False)
    return own.astype(f32) + state[0].astype(f32) + state[1].astype(f32)


def dp_start(piece):
    half = piece.shape[0] // 2
    return piece[None, :half], piece[None, half:]


def dp_steps(state, first=None, last=None):
    bits = [1 << i for i in range(lax.axis_size("dp").bit_length() - 1)]
    one, two = state
    for step in range(len(bits))[first:last]:
        one = jnp.concatenate([one, swap(one, "dp", bits[step])], axis=0)
        two = jnp.concatenate([two, swap(two, "dp", bits[::-1][step])], axis=0)
    return one, two


def dp_places():
    groups = lax.axis_size("dp")
    bits = groups.bit_length() - 1
    who = jnp.arange(groups, dtype=jnp.int32) ^ lax.axis_index("dp")
    turned = sum(((who >> i) & 1) << (bits - 1 - i) for i in range(bits))
    return jnp.stack([who, turned]).astype(jnp.int32)


def lay_kernel(places, one, two, into, out):
    place = out.at[0, 0] if len(out.shape) == 5 else out.at[0, 0, 0]
    place[0] = one[0]
    place[1] = two[0]


def dp_lay(state, into, at):
    one, two = state
    groups, half, width = one.shape
    shape = into.shape
    if isinstance(at, tuple):
        split = into.reshape(shape[0], shape[1], groups, 2, half, width)
        block = (1, 1, 1, 2, half, width)
        where = lambda c, places: (at[0], at[1], c, 0, 0, 0)
        second = jnp.zeros((1, groups), jnp.int32)
    else:
        split = into.reshape(groups, 2, 2, half, width)
        block = (1, 1, 2, half, width)
        where = lambda c, places: (c, places[2, c], 0, 0, 0)
        second = jnp.full((1, groups), at, jnp.int32)
    out = pl.pallas_call(
        lay_kernel,
        grid_spec=pltpu.PrefetchScalarGridSpec(
            num_scalar_prefetch=1,
            grid=(groups,),
            in_specs=[
                pl.BlockSpec((1, half, width), lambda c, places: (places[0, c], 0, 0)),
                pl.BlockSpec((1, half, width), lambda c, places: (places[1, c], 0, 0)),
                pl.BlockSpec(memory_space=pl.ANY),
            ],
            out_specs=pl.BlockSpec(block, where),
        ),
        out_shape=jax.ShapeDtypeStruct(split.shape, into.dtype),
        input_output_aliases={3: 0},
        name="lay",
    )(jnp.concatenate([dp_places(), second]), one, two, split)
    return out.reshape(shape)


def total_sum(buffer, between):
    stages = [("blk", 2, 1), ("dp", lax.axis_size("dp"), 1), ("blk", lax.axis_size("blk") // 2, 2)]
    for number, (axis, ways, unit) in enumerate(stages):
        part = buffer.shape[1] // ways
        mine = (lax.axis_index(axis) // unit) % ways
        cut = lambda d: lax.dynamic_slice_in_dim(buffer, (mine ^ d) * part, part, 1)
        arrived = [swap(cut(d), axis, d * unit) for d in range(1, ways)]
        buffer = between(functools.reduce(jnp.add, arrived, cut(0)), number)
    for number, (axis, ways, unit) in enumerate(stages[::-1]):
        part = buffer.shape[1]
        mine = (lax.axis_index(axis) // unit) % ways
        whole = blank((buffer.shape[0], ways * part), f32)
        for d in range(ways):
            piece = swap(buffer, axis, d * unit) if d else buffer
            whole = lax.dynamic_update_slice_in_dim(whole, piece, (mine ^ d) * part, 1)
        buffer = between(whole, 3 + number)
    return buffer


def sum_all(tables, vectors, between):
    devices = lax.axis_size("dp") * lax.axis_size("blk")
    flat = jnp.concatenate(vectors)
    extra = -flat.shape[0] % 1024
    flat = jnp.pad(flat, (0, extra)).reshape(8, -1)
    joined = jnp.concatenate(
        [t[i * 8 : (i + 1) * 8] for t in tables for i in range(2)] + [flat], axis=1
    )
    width = joined.shape[1]
    joined = jnp.pad(joined, ((0, 0), (0, -width % (128 * devices))))
    joined = total_sum(joined, between)
    out, at = [], 0
    for t in tables:
        size = t.shape[1]
        out.append(
            jnp.concatenate([joined[:, at : at + size], joined[:, at + size : at + 2 * size]], axis=0)
        )
        at += 2 * size
    flat = joined[:, at:width].reshape(-1)
    vecs, at = [], 0
    for v in vectors:
        vecs.append(flat[at : at + v.shape[0]])
        at += v.shape[0]
    return out, vecs


def per_device(
    tokens,
    cotangent,
    document_length_list,
    attention_norm_gain,
    feedforward_norm_gain,
    frozen_query_key_value,
    query_key_value_downmap,
    query_key_value_upmap,
    query_key_value_norm,
    frozen_output_weight,
    output_adapter_downmap,
    output_adapter_upmap,
    output_column_norm,
    frozen_gate_up_weight,
    gate_up_adapter_downmap,
    gate_up_adapter_upmap,
    gate_up_column_norm,
    frozen_down_weight,
    down_adapter_downmap,
    down_adapter_upmap,
    down_column_norm,
):
    length = tokens.shape[0]
    members, groups = lax.axis_size("blk"), lax.axis_size("dp")
    me, line = lax.axis_index("blk"), lax.axis_index("dp")
    count = length * members
    mates = members // QUAD
    wide = frozen_output_weight.shape[1]
    heads = wide // HDIM
    hidden = frozen_gate_up_weight.shape[2]
    lens_row = document_length_list[0]
    rank = ADAPTER_RANK
    flip = lambda a: jnp.swapaxes(a, -1, -2)

    def home(array, axis, width, who=None):
        return lax.dynamic_slice_in_dim(array, (me if who is None else who) * width, width, axis)

    def by_head(array):
        split = array.reshape(3, array.shape[1], heads, HDIM)
        return jnp.transpose(split, (1, 2, 0, 3)).reshape(array.shape[1], 3 * wide)

    def by_three(array):
        split = array.reshape(array.shape[0], heads, 3, HDIM)
        return jnp.transpose(split, (2, 0, 1, 3)).reshape(3, array.shape[0], wide)

    x_full = tokens.astype(f32)
    normed_one, inverse_one = normalize(x_full, attention_norm_gain)
    h_one = normed_one.astype(bf16)
    h_all = lax.all_gather(h_one, "blk", axis=0, tiled=True)

    w_out, n_out = merge(
        after(frozen_output_weight, h_one)[None],
        flip(output_adapter_downmap)[None],
        home(output_adapter_upmap, 1, wide)[None],
        home(output_column_norm, 0, wide)[None],
    )
    gu, n_gu = merge_rows(
        flip(frozen_gate_up_weight),
        flip(gate_up_adapter_downmap),
        home(gate_up_adapter_upmap, 2, hidden),
        home(gate_up_column_norm, 1, hidden)[:, :, None],
        mates,
    )
    b_qkv = home(query_key_value_upmap, 2, wide)
    m_qkv = by_head(home(query_key_value_norm, 1, wide)[:, None, :])
    w_qkv, n_qkv = merge(frozen_query_key_value, flip(query_key_value_downmap), b_qkv, m_qkv)
    w_down, n_down = merge(
        frozen_down_weight[None],
        flip(down_adapter_downmap)[None],
        home(down_adapter_upmap, 1, wide)[None],
        home(down_column_norm, 0, wide)[None],
    )
    places, begins, end = begins_of(lens_row, count)
    half = HDIM // 2
    freq = rope_base ** (-(jnp.arange(half, dtype=f32) * 2.0 / HDIM))
    angle = (places - begins).astype(f32)[:, None] * freq[None, :]
    cosine, sine = jnp.cos(angle), jnp.sin(angle)
    cosine = jnp.concatenate([cosine, cosine], axis=1)
    sine = jnp.concatenate([-sine, sine], axis=1)
    begin = begins[None, :]
    valid = (me * length + jnp.arange(length, dtype=jnp.int32)) < end
    d_final = cotangent.astype(f32) * valid.astype(f32)[:, None]
    d_final_low = d_final.astype(bf16)

    def spread_rows(chunks):
        got = lax.all_to_all(chunks, "blk", 0, 0, tiled=True)
        return jnp.transpose(got, (1, 0, 2)).reshape(chunks.shape[1], members * wide)

    def spread_rows(chunks):
        got = lax.all_to_all(chunks, "blk", 0, 0, tiled=True)
        return jnp.transpose(got, (1, 0, 2)).reshape(chunks.shape[1], members * wide)

    w_out, gu = after((w_out, gu), w_qkv, w_down, cosine, sine)
    piece = MODEL_WIDTH // (2 * groups)
    core = me % 2
    pair = lax.dynamic_slice_in_dim(w_out, 2 * line * piece, 2 * piece, 0)
    pair = pair.reshape(1, 2, piece, wide)
    mine = spread_rows(jnp.tile(pair, (members // 2, 1, 1, 1)).reshape(members, piece, wide))
    mine = dp_steps(dp_start(mine), 0, 1)
    piece = mates * hidden // groups
    per_shard = groups // mates
    turn = line // per_shard
    shards = lax.dynamic_slice_in_dim(
        after(w_down, w_out).reshape(mates, QUAD, hidden, wide),
        (line % per_shard) * piece,
        piece,
        2,
    )
    chosen = jnp.stack(
        [
            functools.reduce(
                lambda rest, k: jnp.where(turn == k, shards[q ^ k], rest),
                range(1, mates),
                shards[q],
            )
            for q in range(mates)
        ]
    ).reshape(members, piece, wide)
    own = jnp.concatenate([n_out[0], n_gu[0, :, 0], n_gu[1, :, 0], n_down[0]])
    own = jnp.pad(own, (0, -own.shape[0] % wide)).reshape(-1, wide)
    own_high = lax.reduce_precision(own, 8, 7)
    riders = jnp.concatenate([own_high, own - own_high], axis=0).astype(bf16)
    extra = -riders.shape[0] % 16
    riders = jnp.pad(riders, ((0, extra), (0, 0)))
    riders = jnp.broadcast_to(riders[None], (members, *riders.shape))
    rows_down = spread_rows(jnp.concatenate([chosen, riders], axis=1))
    norm_rows = rows_down[piece:].astype(f32)
    norms = norm_rows[: own.shape[0]] + norm_rows[own.shape[0] : 2 * own.shape[0]]
    norms = jnp.transpose(norms.reshape(own.shape[0], members, wide), (1, 0, 2))
    norms = norms.reshape(members, own.shape[0] * wide)
    rows_down = rows_down[:piece]
    piece_gu = hidden // groups
    gu_part = lax.dynamic_slice(
        gu, (0, 0, line * piece_gu, 0), (1, 2, piece_gu, MODEL_WIDTH)
    ).reshape(2, piece_gu, MODEL_WIDTH)
    gate_part = after(gu_part[0], rows_down)
    gate_parts = [swap(gate_part, "blk", QUAD * k) for k in range(1, mates)]
    h_all, d_final_low, mine, rows_down = after((h_all, d_final_low, mine, rows_down), cosine)

    mine = dp_steps(mine, 1, None)
    d_final_pair = jnp.concatenate([d_final_low, swap(d_final_low, "blk", 2)], axis=0)
    down_rows = lax.all_gather(rows_down, "dp", axis=0, tiled=True)
    triple = dot(h_all, w_qkv)
    q, k, v, attended_heads, mixed_t, lse = attention_forward(triple, cosine, sine, begin)


    attended_heads = after(attended_heads, mine, gate_parts, d_final_pair)
    one, two, d_final_pair, gate_parts = after(
        (*mine, d_final_pair, gate_parts), attended_heads
    )
    over = swap(one, "blk", 1), swap(two, "blk", 1)
    up_part = after(gu_part[1], attended_heads)
    up_parts = [swap(up_part, "blk", QUAD * k) for k in range(1, mates)]
    gate_states = [dp_steps(dp_start(g)) for g in gate_parts]
    out_full = blank((groups, 2, MODEL_WIDTH // (2 * groups), MODEL_WIDTH), bf16)
    out_full = dp_lay((one, two), out_full, core)
    out_full = dp_lay(over, out_full, 1 - core).reshape(MODEL_WIDTH, MODEL_WIDTH)
    attended = lax.all_to_all(
        attended_heads.reshape(members, length, wide), "blk", 0, 0, tiled=True
    )
    a_low = flip(query_key_value_downmap).astype(bf16).reshape(3 * rank, MODEL_WIDTH)
    h_all_late = after(h_all, attended_heads)
    xa_qkv = dot(a_low, h_all_late, NT).astype(bf16)
    aw_qkv = dot(a_low, w_qkv)
    attended = after(
        attended, xa_qkv, aw_qkv, out_full, gate_states, up_parts, down_rows
    )

    attended = jnp.transpose(attended, (1, 0, 2)).reshape(length, MODEL_WIDTH)
    a_out_low = flip(output_adapter_downmap).astype(bf16)
    y_out = dot(jnp.concatenate([attended, a_out_low], axis=0), out_full)
    y_out, aw_out = y_out[:length], y_out[length:]
    residual = x_full + y_out
    normed_two, inverse_two = normalize(residual, feedforward_norm_gain)
    h_two = normed_two.astype(bf16)
    up_parts = after(up_parts, attended)
    up_states = [dp_steps(dp_start(g), 0, 1) for g in up_parts]
    h_two = after(h_two, up_states)

    attended_late = after(attended, h_two)
    xa_out = dot(a_out_low, attended_late, NT).astype(bf16)
    gate_states = after(gate_states, h_two)
    up_states = [dp_steps(after(state, h_two), 1, None) for state in up_states]
    d_final_pair = after(d_final_pair, h_two)
    d_final_all = jnp.concatenate([d_final_pair, swap(d_final_pair, "blk", 1)], axis=0)
    for k_ in range(1, mates):
        gu = dp_lay(gate_states[k_ - 1], gu, (k_, 0))
        gu = dp_lay(up_states[k_ - 1], gu, (k_, 1))
    gu = gu.reshape(mates * 2 * hidden, MODEL_WIDTH)
    a_gu_low = flip(gate_up_adapter_downmap).astype(bf16).reshape(2 * rank, MODEL_WIDTH)
    norms_out = norms[:, :wide].reshape(-1)
    norms_down = norms[:, wide + 2 * hidden : 2 * wide + 2 * hidden].reshape(-1)

    h_two_all = after(quad_gather(h_two), xa_out, gu, down_rows)
    acts, g_gu, gm_gu = feed_forward(gu, down_rows, h_two_all, d_final_all, mates)
    dh_parts = dot(g_gu, gu, TN).astype(bf16)
    dh_half = quad_halve(dh_parts)
    dh_two = quad_finish(dh_half)

    acts_late, down_late, h_two_late, gu_late = after(
        (acts, down_rows, h_two_all, gu), dh_half
    )
    y_parts = dot(acts_late, down_late, TN).astype(bf16)
    a_down_low = flip(down_adapter_downmap).astype(bf16)
    order = [me ^ (QUAD * k_) for k_ in range(mates)]
    low = jnp.concatenate([home(a_down_low, 1, hidden, who) for who in order], axis=1)
    xa_down = dot(low, acts_late).astype(bf16)
    aw_down = dot(low, down_late)
    xa_gu = dot(a_gu_low, h_two_late, NT).astype(bf16)
    aw_gu = dot(a_gu_low, gu_late, NT)
    dh_two = after(dh_two, y_parts, xa_down, aw_down, xa_gu, aw_gu)

    d_norm_two = normalize_back(residual, inverse_two, feedforward_norm_gain, dh_two)
    d_residual = d_final + d_norm_two
    g_out = d_residual.astype(bf16)
    d_attended = dot(g_out, out_full, NT).astype(bf16)
    d_parts = jnp.transpose(d_attended.reshape(length, members, wide), (1, 0, 2))
    d_heads = lax.all_to_all(d_parts, "blk", 0, 0, tiled=True).reshape(count, wide)

    y_down = quad_finish(quad_halve(after(y_parts, d_parts)))
    result = (residual + y_down).astype(bf16)
    g_late, h_two_late, gu_late, gm_gu = after((g_gu, h_two_all, gu, gm_gu), d_parts)

    def joined(pick):
        return jnp.concatenate([pick(who, i) for who in order for i in range(2)], axis=-1)

    m_gu = joined(lambda who, i: home(gate_up_column_norm[i], 0, hidden, who))
    n_gu_all = joined(
        lambda who, i: lax.dynamic_slice(norms, (who, wide + i * hidden), (1, hidden))[0]
    )
    b_gu = joined(lambda who, i: home(gate_up_adapter_upmap[i], 1, hidden, who))
    s_gu = m_gu / n_gu_all
    gm_gu = gm_gu.reshape(-1) / m_gu
    row = lax.broadcasted_iota(jnp.int32, (2 * rank, b_gu.shape[1]), 0) // rank
    column = (lax.broadcasted_iota(jnp.int32, (2 * rank, b_gu.shape[1]), 1) // hidden) % 2
    own_gu = row == column
    spread = jnp.where(own_gu, jnp.tile(b_gu, (2, 1)), 0.0)
    p_gu = dot((spread * s_gu).astype(bf16), g_late).astype(bf16)
    tilt = (spread * (gm_gu / n_gu_all)).astype(bf16)
    ga_gu = adapter_scale * (dot(p_gu, h_two_late) - dot(tilt, gu_late))
    gb_gu = adapter_scale * (dot(xa_gu, g_late, NT) * s_gu - aw_gu * (gm_gu / n_gu_all))
    gb_gu = jnp.sum(jnp.where(own_gu, gb_gu, 0.0).reshape(2, rank, -1), axis=0)
    d_heads = after(d_heads, ga_gu, gb_gu)

    g_three, gm_heads = attention_backward(
        q, k, v, triple, cosine, sine, begin, d_heads, mixed_t, lse
    )
    g_three = after(g_three, y_down)
    dh_parts = dot(g_three, w_qkv, NT).astype(bf16)
    total = core_scatter(dh_parts)
    acts_late, d_final_late, y_down, dh_late, unit_two, g_out, out_late = after(
        (acts, d_final_all, y_down, dh_two, residual * inverse_two, g_out, out_full), total
    )
    grad_g_ffn = jnp.sum(dh_late * unit_two, axis=0)
    gm_down = jnp.sum(d_final_low.astype(f32) * y_down, axis=0) / down_column_norm
    gm_quad = gm_down + swap(gm_down, "blk", 1)
    gm_quad = gm_quad + swap(gm_quad, "blk", 2)
    s_down = down_column_norm / norms_down
    p_down = dot((down_adapter_upmap * s_down).astype(bf16), d_final_late, NT).astype(bf16)
    tilt_down = (down_adapter_upmap * (gm_quad / norms_down)).astype(bf16)
    ga_down = adapter_scale * (dot(p_down, acts_late, NT) - dot(tilt_down, down_rows, NT))
    gb_down = adapter_scale * (
        dot(xa_down, d_final_late) * s_down - aw_down * (gm_quad / norms_down)
    )
    gm_out = jnp.sum(g_out.astype(f32) * y_out, axis=0) / output_column_norm
    s_out = output_column_norm / norms_out
    p_out = dot((output_adapter_upmap * s_out).astype(bf16), g_out, NT).astype(bf16)
    tilt_out = (output_adapter_upmap * (gm_out / norms_out)).astype(bf16)
    ga_out = adapter_scale * (dot(p_out, attended) - dot(tilt_out, out_late, NT))
    gb_out = adapter_scale * (dot(xa_out, g_out) * s_out - aw_out * (gm_out / norms_out))

    state = chips_step(total, 1, None)
    state = after(state, ga_down, gb_down, ga_out, gb_out, grad_g_ffn)
    g_three, gm_heads, h_all_late = after((g_three, gm_heads, h_all), state)
    chips = members // 2

    gm = gm_heads[0:1] / m_qkv
    s_qkv = m_qkv / n_qkv
    row = lax.broadcasted_iota(jnp.int32, (3 * rank, 3 * wide), 0) // rank
    column = (lax.broadcasted_iota(jnp.int32, (3 * rank, 3 * wide), 1) // HDIM) % 3
    own_block = row == column
    spread = jnp.where(own_block, jnp.tile(by_head(b_qkv), (3, 1)), 0.0)
    p = dot((spread * s_qkv).astype(bf16), g_three, NT).astype(bf16)
    tilt = (spread * (gm / n_qkv)).astype(bf16)
    grad_a = adapter_scale * (dot(p, h_all_late) - dot(tilt, w_qkv, NT))
    grad_b = adapter_scale * (dot(xa_qkv, g_three) * s_qkv - aw_qkv * (gm / n_qkv))
    grad_b = jnp.sum(jnp.where(own_block, grad_b, 0.0).reshape(3, rank, 3 * wide), axis=0)
    grad_b = by_three(grad_b)
    grad_m = by_three(gm)[:, 0]
    grad_g_attn = (
        jnp.sum(dh_parts.astype(f32) * h_all_late.astype(f32), axis=0) / attention_norm_gain
    )


    for t in range(2, chips - 1):
        state = chips_step(total, t, state)
        state = after(state, grad_a, grad_b, grad_g_attn)
    grad_a, grad_b, grad_m, ga_gu, gb_gu = after((grad_a, grad_b, grad_m, ga_gu, gb_gu), state)
    ends = {}

    def between(buffer, stage):
        if stage == 1:
            ends[0] = after(chips_step(total, chips - 1, state), buffer)
            buffer = after(buffer, ends[0])
        return buffer

    def placed(array, total, k_, i):
        part = array[..., (2 * k_ + i) * hidden : (2 * k_ + i + 1) * hidden]
        return lax.dynamic_update_slice_in_dim(total, part, order[k_] * hidden, array.ndim - 1)

    units = members * hidden
    all_b, all_m = [], []
    for i in range(2):
        tall, thin = jnp.zeros((rank, units), f32), jnp.zeros((units,), f32)
        for k_ in range(mates):
            tall, thin = placed(gb_gu, tall, k_, i), placed(gm_gu, thin, k_, i)
        all_b.append(tall)
        all_m.append(thin)
    all_a = jnp.zeros((rank, units), f32)
    for k_ in range(mates):
        all_a = lax.dynamic_update_slice_in_dim(
            all_a, ga_down[:, k_ * hidden : (k_ + 1) * hidden], order[k_] * hidden, 1
        )
    empty = jnp.zeros((rank, MODEL_WIDTH), f32)
    tables, vectors = sum_all(
        [grad_a[i * rank : (i + 1) * rank] for i in range(3)]
        + [lax.dynamic_update_slice_in_dim(empty, grad_b[i], me * wide, 1) for i in range(3)]
        + [ga_out, gb_out, ga_gu[:rank], ga_gu[rank:], gb_down]
        + [*all_b, all_a],
        [grad_g_attn, grad_g_ffn, gm_out, gm_down]
        + [lax.dynamic_update_slice_in_dim(empty[0], grad_m[i], me * wide, 0) for i in range(3)]
        + all_m,
        between,
    )
    d_norm_one = normalize_back(x_full, inverse_one, attention_norm_gain, chips_end(total, ends[0]))
    grad_input = d_residual + d_norm_one
    a_out, b_out, a_gate, a_up, b_down, b_gate, b_up, a_down = tables[6:]
    return (
        result,
        grad_input,
        vectors[0],
        vectors[1],
        flip(jnp.stack(tables[:3])),
        jnp.stack(tables[3:6]),
        jnp.stack(vectors[4:7]),
        flip(a_out),
        b_out,
        vectors[2],
        flip(jnp.stack([a_gate, a_up])),
        jnp.stack([b_gate, b_up]),
        jnp.stack(vectors[7:]),
        flip(a_down),
        b_down,
        vectors[3],
    )


def solution(mesh):
    rows, none = P(("dp", "blk"), None), P()
    in_specs = (
        rows,
        rows,
        P("dp", None),
        none,
        none,
        P(None, None, "blk"),
        none,
        none,
        none,
        P(None, "blk"),
        none,
        none,
        none,
        P(None, None, "blk"),
        none,
        none,
        none,
        P(None, "blk"),
        none,
        none,
        none,
    )
    out_specs = (rows, rows) + (none,) * 14
    return jax.shard_map(
        per_device, mesh=mesh, in_specs=in_specs, out_specs=out_specs, check_vma=False
    )
```

```python
import functools

import jax
import jax.numpy as jnp
from jax import lax
from jax.experimental import pallas as pl
from jax.experimental.pallas import tpu as pltpu
from jax.sharding import PartitionSpec as P

MODEL_WIDTH = 2048
HEADS = 16
ADAPTER_RANK = 16
ALPHA = 32
HDIM = 128
TILE = 256
QUAD = 4

norm_eps = 1e-05
column_eps = 1e-06
rope_base = 10000.0
far_negative = -1e30
log2_e = 1.4426950408889634
adapter_scale = ALPHA / ADAPTER_RANK
bf16 = jnp.bfloat16
f32 = jnp.float32
NT = (((1,), (1,)), ((), ()))
TN = (((0,), (0,)), ((), ()))
NN = (((1,), (0,)), ((), ()))


def dot(a, b, dims=NN):
    return lax.dot_general(a, b, dims, preferred_element_type=f32)


def after(array, *earlier):
    return lax.optimization_barrier((array, *earlier))[0]


def blank(shape, dtype):
    return pl.pallas_call(
        lambda out: None,
        out_shape=jax.ShapeDtypeStruct(shape, dtype),
        out_specs=pl.BlockSpec(memory_space=pl.ANY),
        name="blank",
    )()


def swap(array, axis, bit):
    return lax.ppermute(array, axis, [(i, i ^ bit) for i in range(lax.axis_size(axis))])


def axis_sum(array, axis):
    bit = 1
    while bit < lax.axis_size(axis):
        array = array + swap(array, axis, bit)
        bit *= 2
    return array


def begins_of(lens_row, count):
    places = jnp.arange(count, dtype=jnp.int32)
    ends = jnp.cumsum(lens_row, dtype=jnp.int32)
    after = (places[:, None] >= ends[None, :]).astype(jnp.int32)
    return places, jnp.sum(after * lens_row[None, :], axis=1, dtype=jnp.int32), ends[-1]


def split_three(a):
    one = lax.reduce_precision(a, 8, 7)
    rest = a - one
    two = lax.reduce_precision(rest, 8, 7)
    return one.astype(bf16), two.astype(bf16), (rest - two).astype(bf16)


def parts_of(a, b):
    a1, a2, a3 = split_three(a * adapter_scale)
    b1, b2, b3 = split_three(b)
    return (
        jnp.concatenate([a1, a1, a2, a1, a2, a3], axis=-2),
        jnp.concatenate([b1, b2, b1, b3, b2, b1], axis=-2),
    )


def merge_kernel(w_ref, a_ref, b_ref, m_ref, out_ref, n_ref, v_ref):
    rows = w_ref.shape[1]

    def add(i, acc):
        at = pl.ds(pl.multiple_of(i * TILE, TILE), TILE)
        v = w_ref[0, at, :].astype(f32) + dot(a_ref[0, :, at], b_ref[0], TN)
        v_ref[at, :] = v
        return acc + jnp.sum(v * v, axis=0, keepdims=True)

    total = lax.fori_loop(0, rows // TILE, add, jnp.zeros(m_ref.shape, f32), unroll=2)
    norms = jnp.sqrt(total + column_eps)
    n_ref[...] = norms
    s = m_ref[...] / norms

    def put(i, carry):
        at = pl.ds(pl.multiple_of(i * TILE, TILE), TILE)
        out_ref[at, :] = (v_ref[at, :] * s).astype(bf16)
        return carry

    lax.fori_loop(0, rows // TILE, put, 0, unroll=2)


def merge(w, a, b, m):
    k, rows, cols = w.shape
    a_cat, b_cat = parts_of(a, b)
    wide = a_cat.shape[1]
    place = lambda i, h: (0, h * k + i)
    return pl.pallas_call(
        merge_kernel,
        grid=(k, cols // HDIM),
        in_specs=[
            pl.BlockSpec((1, rows, HDIM), lambda i, h: (i, 0, h)),
            pl.BlockSpec((1, wide, rows), lambda i, h: (i, 0, 0)),
            pl.BlockSpec((1, wide, HDIM), lambda i, h: (i, 0, h)),
            pl.BlockSpec((1, HDIM), place),
        ],
        out_specs=[pl.BlockSpec((rows, HDIM), place), pl.BlockSpec((1, HDIM), place)],
        out_shape=[
            jax.ShapeDtypeStruct((rows, k * cols), bf16),
            jax.ShapeDtypeStruct((1, k * cols), f32),
        ],
        scratch_shapes=[pltpu.VMEM((rows, HDIM), f32)],
        compiler_params=pltpu.CompilerParams(vmem_limit_bytes=48 * 2**20),
        cost_estimate=pl.CostEstimate(
            flops=2 * k * rows * cols * wide, bytes_accessed=4 * k * rows * cols, transcendentals=0
        ),
        name="merge",
    )(w, a_cat, b_cat, m)


def merge_rows_kernel(w_ref, a_ref, b_ref, m_ref, out_ref, n_ref):
    out_ref = out_ref.at[0]
    v = w_ref[0].astype(f32) + dot(b_ref[0], a_ref[0], TN)
    norms = jnp.sqrt(jnp.sum(v * v, axis=1, keepdims=True) + column_eps)
    n_ref[0] = norms
    out_ref[0] = (v * (m_ref[0] / norms)).astype(bf16)


def merge_rows(w, a, b, m, mates):
    k, cols, rows = w.shape
    a_cat, b_cat = parts_of(a, b)
    wide = a_cat.shape[1]
    return pl.pallas_call(
        merge_rows_kernel,
        grid=(k,),
        in_specs=[
            pl.BlockSpec((1, cols, rows), lambda i: (i, 0, 0)),
            pl.BlockSpec((1, wide, rows), lambda i: (i, 0, 0)),
            pl.BlockSpec((1, wide, cols), lambda i: (i, 0, 0)),
            pl.BlockSpec((1, cols, 1), lambda i: (i, 0, 0)),
        ],
        out_specs=[
            pl.BlockSpec((1, 1, cols, rows), lambda i: (0, i, 0, 0)),
            pl.BlockSpec((1, cols, 1), lambda i: (i, 0, 0)),
        ],
        out_shape=[
            jax.ShapeDtypeStruct((mates, k, cols, rows), bf16),
            jax.ShapeDtypeStruct((k, cols, 1), f32),
        ],
        compiler_params=pltpu.CompilerParams(vmem_limit_bytes=56 * 2**20),
        cost_estimate=pl.CostEstimate(
            flops=2 * k * rows * cols * wide, bytes_accessed=4 * k * rows * cols, transcendentals=0
        ),
        name="merge_rows",
    )(w, a_cat, b_cat, m)


def turned(u, cosine, sine):
    return u * cosine + pltpu.roll(u, HDIM // 2, 1) * sine


def forward_kernel(
    pre, cosine, sine, begin, q_out, k_out, v_out, att_out, mixed_t, lse_out, v_t
):
    count = pre.shape[0]
    scale = HDIM**-0.5 * log2_e
    for i in range(count // TILE):
        at = pl.ds(i * TILE, TILE)
        cos, sin = cosine[at, :], sine[at, :]
        q_out[at, :] = turned(pre[at, :HDIM], cos, sin).astype(bf16)
        k_out[at, :] = turned(pre[at, HDIM : 2 * HDIM], cos, sin).astype(bf16)
        v = pre[at, 2 * HDIM :]
        v_out[at, :] = v.astype(bf16)
        v_t[:, at] = v.T.astype(bf16)
    for i in range(count // TILE):
        rows = pl.ds(i * TILE, TILE)
        q = q_out[rows, :]
        start = begin[:, rows]

        def visit(j, state, diagonal):
            top, total, mixed = state
            keys = pl.ds(pl.multiple_of(j * TILE, TILE), TILE)
            s = dot(k_out[keys, :], q, NT) * scale
            place = j * TILE + lax.broadcasted_iota(jnp.int32, (TILE, TILE), 0)
            allowed = place >= start
            if diagonal:
                mine = i * TILE + lax.broadcasted_iota(jnp.int32, (TILE, TILE), 1)
                allowed = allowed & (place <= mine)
            s = jnp.where(allowed, s, far_negative)
            high = jnp.maximum(top, jnp.max(s, axis=0, keepdims=True))
            keep = jnp.exp2(top - high)
            p = jnp.exp2(s - high)
            total = total * keep + jnp.sum(p, axis=0, keepdims=True)
            mixed = mixed * keep + dot(v_t[:, keys], p.astype(bf16))
            return high, total, mixed

        state = (
            jnp.full((1, TILE), far_negative, f32),
            jnp.zeros((1, TILE), f32),
            jnp.zeros((HDIM, TILE), f32),
        )
        state = visit(i, state, True)
        for j in range(i):
            state = visit(j, state, False)
        top, total, mixed = state
        mixed = mixed / total
        mixed_t[:, rows] = mixed
        att_out[rows, :] = mixed.T.astype(bf16)
        lse_out[0, :, rows] = top + jnp.log2(total)


def backward_kernel(
    q_ref, k_ref, v_ref, pre, cosine, sine, begin, grad_att, mixed_t, lse,
    g_out, gm_out, dk, dv, k_t,
):
    count = q_ref.shape[0]
    scale = HDIM**-0.5
    dk[...] = jnp.zeros_like(dk)
    dv[...] = jnp.zeros_like(dv)
    for i in range(count // TILE):
        at = pl.ds(i * TILE, TILE)
        k_t[:, at] = k_ref[at, :].astype(f32).T.astype(bf16)
    gm_q = jnp.zeros((1, HDIM), f32)
    for i in range(count // TILE):
        rows = pl.ds(i * TILE, TILE)
        q = q_ref[rows, :]
        d_mixed = grad_att[rows, :]
        delta = jnp.sum(d_mixed.astype(f32).T * mixed_t[:, rows], axis=0, keepdims=True)
        start = begin[:, rows]
        high = lse[0, :, rows]
        dq_t = jnp.zeros((HDIM, TILE), f32)
        for j in range(i + 1):
            keys = pl.ds(j * TILE, TILE)
            s = dot(k_ref[keys, :], q, NT) * (scale * log2_e)
            place = j * TILE + lax.broadcasted_iota(jnp.int32, (TILE, TILE), 0)
            allowed = place >= start
            if j == i:
                mine = i * TILE + lax.broadcasted_iota(jnp.int32, (TILE, TILE), 1)
                allowed = allowed & (place <= mine)
            p = jnp.where(allowed, jnp.exp2(s - high), 0.0)
            dp = dot(v_ref[keys, :], d_mixed, NT)
            ds = (p * (dp - delta)).astype(bf16)
            dv[keys, :] += dot(p.astype(bf16), d_mixed)
            dk[keys, :] += dot(ds, q)
            dq_t = dq_t + dot(k_t[:, keys], ds)
        gq = turned(dq_t.T * scale, cosine[rows, :], -sine[rows, :]).astype(bf16)
        g_out[rows, :HDIM] = gq
        gm_q = gm_q + jnp.sum(gq.astype(f32) * pre[rows, :HDIM], axis=0, keepdims=True)
    gm_k = jnp.zeros((1, HDIM), f32)
    gm_v = jnp.zeros((1, HDIM), f32)
    for i in range(count // TILE):
        at = pl.ds(i * TILE, TILE)
        gk = turned(dk[at, :] * scale, cosine[at, :], -sine[at, :]).astype(bf16)
        g_out[at, HDIM : 2 * HDIM] = gk
        gm_k = gm_k + jnp.sum(gk.astype(f32) * pre[at, HDIM : 2 * HDIM], axis=0, keepdims=True)
        gv = dv[at, :].astype(bf16)
        g_out[at, 2 * HDIM :] = gv
        gm_v = gm_v + jnp.sum(gv.astype(f32) * pre[at, 2 * HDIM :], axis=0, keepdims=True)
    gm_out[0:1, :HDIM] = gm_q
    gm_out[0:1, HDIM : 2 * HDIM] = gm_k
    gm_out[0:1, 2 * HDIM :] = gm_v


def attention_forward(triple, cosine, sine, begin):
    count, width = triple.shape[0], triple.shape[1] // 3
    heads = width // HDIM
    whole = lambda h: (0, 0)
    head = lambda h: (0, h)
    tall = lambda at: pl.BlockSpec((count, HDIM), at)
    return pl.pallas_call(
        forward_kernel,
        grid=(heads,),
        in_specs=[
            pl.BlockSpec((count, 3 * HDIM), head),
            tall(whole),
            tall(whole),
            pl.BlockSpec((1, count), whole),
        ],
        out_specs=[
            tall(head),
            tall(head),
            tall(head),
            tall(head),
            pl.BlockSpec((HDIM, count), lambda h: (h, 0)),
            pl.BlockSpec((1, 1, count), lambda h: (h, 0, 0)),
        ],
        out_shape=[jax.ShapeDtypeStruct((count, width), bf16)] * 4
        + [
            jax.ShapeDtypeStruct((width, count), f32),
            jax.ShapeDtypeStruct((heads, 1, count), f32),
        ],
        scratch_shapes=[pltpu.VMEM((HDIM, count), bf16)],
        compiler_params=pltpu.CompilerParams(vmem_limit_bytes=48 * 2**20),
        cost_estimate=pl.CostEstimate(
            flops=2 * count * count * width, bytes_accessed=30 * count * width, transcendentals=0
        ),
        name="attend",
    )(triple, cosine, sine, begin)


def attention_backward(q, k, v, triple, cosine, sine, begin, grad_att, mixed_t, lse):
    count, width = q.shape
    heads = width // HDIM
    whole = lambda h: (0, 0)
    head = lambda h: (0, h)
    tall = lambda at: pl.BlockSpec((count, HDIM), at)
    return pl.pallas_call(
        backward_kernel,
        grid=(heads,),
        in_specs=[
            tall(head),
            tall(head),
            tall(head),
            pl.BlockSpec((count, 3 * HDIM), head),
            tall(whole),
            tall(whole),
            pl.BlockSpec((1, count), whole),
            tall(head),
            pl.BlockSpec((HDIM, count), lambda h: (h, 0)),
            pl.BlockSpec((1, 1, count), lambda h: (h, 0, 0)),
        ],
        out_specs=[pl.BlockSpec((count, 3 * HDIM), head), pl.BlockSpec((8, 3 * HDIM), head)],
        out_shape=[
            jax.ShapeDtypeStruct((count, 3 * width), bf16),
            jax.ShapeDtypeStruct((8, 3 * width), f32),
        ],
        scratch_shapes=[
            pltpu.VMEM((count, HDIM), f32),
            pltpu.VMEM((count, HDIM), f32),
            pltpu.VMEM((HDIM, count), bf16),
        ],
        compiler_params=pltpu.CompilerParams(vmem_limit_bytes=48 * 2**20),
        cost_estimate=pl.CostEstimate(
            flops=5 * count * count * width, bytes_accessed=40 * count * width, transcendentals=0
        ),
        name="attend_back",
    )(q, k, v, triple, cosine, sine, begin, grad_att, mixed_t, lse)


def feed_kernel(gu_ref, down_ref, h_ref, d_ref, acts_out, g_out, gm_out):
    h = h_ref[...]
    gate = dot(gu_ref[0, 0], h, NT)
    upward = dot(gu_ref[0, 1], h, NT)
    d_act = dot(down_ref[...], d_ref[...], NT)
    sigmoid_gate = jax.nn.sigmoid(gate)
    silu = gate * sigmoid_gate
    acts_out[...] = (silu * upward).astype(bf16)
    d_gate = (d_act * upward * sigmoid_gate * (1.0 + gate * (1.0 - sigmoid_gate))).astype(bf16)
    d_upward = (d_act * silu).astype(bf16)
    g_out[0, 0] = d_gate
    g_out[0, 1] = d_upward
    gm_out[0, 0] = jnp.sum(d_gate.astype(f32) * gate, axis=1, keepdims=True)
    gm_out[0, 1] = jnp.sum(d_upward.astype(f32) * upward, axis=1, keepdims=True)


def feed_forward(gu, down, h, d, mates):
    rows, width = h.shape
    hidden = down.shape[0] // mates
    unit = hidden // max(1, hidden // 352)
    steps = hidden // unit
    flat = lambda k, j: (k * steps + j, 0)
    deep = lambda k, j: (k, 0, j, 0)
    whole = lambda k, j: (0, 0)
    acts, g, gm = pl.pallas_call(
        feed_kernel,
        grid=(mates, steps),
        in_specs=[
            pl.BlockSpec((1, 2, unit, width), deep),
            pl.BlockSpec((unit, width), flat),
            pl.BlockSpec((rows, width), whole),
            pl.BlockSpec((rows, width), whole),
        ],
        out_specs=[
            pl.BlockSpec((unit, rows), flat),
            pl.BlockSpec((1, 2, unit, rows), deep),
            pl.BlockSpec((1, 2, unit, 1), deep),
        ],
        out_shape=[
            jax.ShapeDtypeStruct((mates * hidden, rows), bf16),
            jax.ShapeDtypeStruct((mates, 2, hidden, rows), bf16),
            jax.ShapeDtypeStruct((mates, 2, hidden, 1), f32),
        ],
        compiler_params=pltpu.CompilerParams(vmem_limit_bytes=58 * 2**20),
        cost_estimate=pl.CostEstimate(
            flops=6 * mates * hidden * rows * width,
            bytes_accessed=6 * mates * hidden * width + 4 * rows * width,
            transcendentals=0,
        ),
        name="feed_forward",
    )(gu.reshape(mates, 2, hidden, width), down, h, d)
    return acts, g.reshape(2 * mates * hidden, rows), gm


def back_kernel(
    core, g_ref, h_ref, w_ref, spread, s_ref, over_n, sums, m_ref, xa_ref, aw_ref,
    own_out, other_out, ga_out, gb_out, gg_out, gm_out,
):
    step = pl.program_id(0)
    length = own_out.shape[1]
    g = g_ref[...]
    h = h_ref[...]
    s = s_ref[...]
    dh = dot(g, w_ref[...], NT)
    low = dh.astype(bf16)

    @pl.when(core[0] == 0)
    def _():
        own_out[0] = low[:length]
        other_out[0] = low[length:]

    @pl.when(core[0] != 0)
    def _():
        own_out[0] = low[length:]
        other_out[0] = low[:length]

    p = dot((spread[...] * s).astype(bf16), g, NT).astype(bf16)
    ga = dot(p, h)
    gb = dot(xa_ref[...], g)
    gg = jnp.sum(dh * h.astype(f32), axis=0, keepdims=True)

    @pl.when(step == 0)
    def _():
        gm = sums[0:1, :] / m_ref[...]
        gm_out[...] = gm
        tilt = (spread[...] * (gm * over_n[...])).astype(bf16)
        ga_out[...] = ga - dot(tilt, w_ref[...], NT)
        gb_out[...] = gb * s - aw_ref[...] * (gm * over_n[...])
        gg_out[...] = gg

    @pl.when(step > 0)
    def _():
        ga_out[...] += ga
        gb_out[...] += gb * s
        gg_out[...] += gg


def back_qkv(g, h, w, spread, m, n, sums, xa, aw):
    chips = lax.axis_size("blk") // 2
    core = (lax.axis_index("blk") % 2).astype(jnp.int32).reshape(1)
    count, cols = g.shape
    width = h.shape[1]
    pair = count // chips
    wide = spread.shape[0]
    rows = lambda i, core: (i, 0)
    whole = lambda i, core: (0, 0)
    deep = lambda i, core: (i, 0, 0)
    return pl.pallas_call(
        back_kernel,
        grid_spec=pltpu.PrefetchScalarGridSpec(
            num_scalar_prefetch=1,
            grid=(chips,),
            in_specs=[
                pl.BlockSpec((pair, cols), rows),
                pl.BlockSpec((pair, width), rows),
                pl.BlockSpec((width, cols), whole),
                pl.BlockSpec((wide, cols), whole),
                pl.BlockSpec((1, cols), whole),
                pl.BlockSpec((1, cols), whole),
                pl.BlockSpec((8, cols), whole),
                pl.BlockSpec((1, cols), whole),
                pl.BlockSpec((None, wide, pair), deep),
                pl.BlockSpec((wide, cols), whole),
            ],
            out_specs=[
                pl.BlockSpec((1, pair // 2, width), deep),
                pl.BlockSpec((1, pair // 2, width), deep),
                pl.BlockSpec((wide, width), whole),
                pl.BlockSpec((wide, cols), whole),
                pl.BlockSpec((1, width), whole),
                pl.BlockSpec((1, cols), whole),
            ],
        ),
        out_shape=[
            jax.ShapeDtypeStruct((chips, pair // 2, width), bf16),
            jax.ShapeDtypeStruct((chips, pair // 2, width), bf16),
            jax.ShapeDtypeStruct((wide, width), f32),
            jax.ShapeDtypeStruct((wide, cols), f32),
            jax.ShapeDtypeStruct((1, width), f32),
            jax.ShapeDtypeStruct((1, cols), f32),
        ],
        compiler_params=pltpu.CompilerParams(vmem_limit_bytes=56 * 2**20),
        cost_estimate=pl.CostEstimate(
            flops=3 * count * cols * width, bytes_accessed=8 * count * width, transcendentals=0
        ),
        name="back_qkv",
    )(core, g, h, w, spread, m / n, 1.0 / n, sums, m, xa, aw)


def normalize(values, gain):
    inverse = lax.rsqrt(jnp.mean(values * values, axis=-1, keepdims=True) + norm_eps)
    return (values * inverse * gain, inverse)


def normalize_back(values, inverse, gain, grad):
    unit = values * inverse
    scaled = grad * gain
    return inverse * (scaled - unit * jnp.mean(scaled * unit, axis=-1, keepdims=True))


def quad_gather(block):
    pair = jnp.concatenate([block, swap(block, "blk", 2)], axis=0)
    return jnp.concatenate([pair, swap(pair, "blk", 1)], axis=0)


def quad_halve(parts):
    half = parts.shape[0] // 2
    return parts[:half].astype(f32) + swap(parts[half:], "blk", 1).astype(f32)


def quad_finish(mine):
    half = mine.shape[0] // 2
    return mine[:half] + swap(mine[half:].astype(bf16), "blk", 2).astype(f32)


def step_chips(array, first, last, by):
    pairs = [(2 * i + c, 2 * (i + by) + c) for i in range(first, last + 1) for c in range(2)]
    return lax.ppermute(array, "blk", pairs)


def chips_step(total, t, state):
    chips = total.shape[0]
    chip = lax.axis_index("blk") // 2
    pick = lambda c: lax.dynamic_index_in_dim(
        total, jnp.clip(c, 0, chips - 1), 0, keepdims=False
    )
    up, down = pick(chips - t + chip), pick(t - chips + chip)
    if t > 1:
        up = (up.astype(f32) + state[0].astype(f32)).astype(bf16)
        down = (down.astype(f32) + state[1].astype(f32)).astype(bf16)
    up, down = after((up, down))
    return step_chips(up, 0, t - 1, 1), step_chips(down, chips - t, chips - 1, -1)


def chips_end(total, state):
    chip = lax.axis_index("blk") // 2
    own = lax.dynamic_index_in_dim(total, chip, 0, keepdims=False)
    return own.astype(f32) + state[0].astype(f32) + state[1].astype(f32)


def dp_start(piece):
    half = piece.shape[0] // 2
    return piece[None, :half], piece[None, half:]


def dp_steps(state, first=None, last=None):
    bits = [1 << i for i in range(lax.axis_size("dp").bit_length() - 1)]
    one, two = state
    for step in range(len(bits))[first:last]:
        one = jnp.concatenate([one, swap(one, "dp", bits[step])], axis=0)
        two = jnp.concatenate([two, swap(two, "dp", bits[::-1][step])], axis=0)
    return one, two


def dp_last(state):
    bits = [1 << i for i in range(lax.axis_size("dp").bit_length() - 1)]
    one, two = state
    return jnp.concatenate(
        [one, swap(one, "dp", bits[-1]), two, swap(two, "dp", bits[0])], axis=0
    )


def dp_places():
    groups = lax.axis_size("dp")
    bits = groups.bit_length() - 1
    who = jnp.arange(groups, dtype=jnp.int32) ^ lax.axis_index("dp")
    turned = sum(((who >> i) & 1) << (bits - 1 - i) for i in range(bits))
    return jnp.stack([who, turned + groups]).astype(jnp.int32)


def lay_kernel(places, one, two, into, out):
    place = out.at[0, 0] if len(out.shape) == 5 else out.at[0, 0, 0]
    place[0] = one[0]
    place[1] = two[0]


def dp_lay(state, into, at):
    groups, half, width = state.shape[0] // 2, state.shape[1], state.shape[2]
    shape = into.shape
    if isinstance(at, tuple):
        split = into.reshape(shape[0], shape[1], groups, 2, half, width)
        block = (1, 1, 1, 2, half, width)
        where = lambda c, places: (at[0], at[1], c, 0, 0, 0)
        second = jnp.zeros((1, groups), jnp.int32)
    else:
        split = into.reshape(groups, 2, 2, half, width)
        block = (1, 1, 2, half, width)
        where = lambda c, places: (c, places[2, c], 0, 0, 0)
        second = jnp.full((1, groups), at, jnp.int32)
    out = pl.pallas_call(
        lay_kernel,
        grid_spec=pltpu.PrefetchScalarGridSpec(
            num_scalar_prefetch=1,
            grid=(groups,),
            in_specs=[
                pl.BlockSpec((1, half, width), lambda c, places: (places[0, c], 0, 0)),
                pl.BlockSpec((1, half, width), lambda c, places: (places[1, c], 0, 0)),
                pl.BlockSpec(memory_space=pl.ANY),
            ],
            out_specs=pl.BlockSpec(block, where),
        ),
        out_shape=jax.ShapeDtypeStruct(split.shape, into.dtype),
        input_output_aliases={3: 0},
        name="lay",
    )(jnp.concatenate([dp_places(), second]), state, state, split)
    return out.reshape(shape)


def total_sum(buffer, between):
    stages = [("blk", 2, 1), ("dp", lax.axis_size("dp"), 1), ("blk", lax.axis_size("blk") // 2, 2)]
    for number, (axis, ways, unit) in enumerate(stages):
        part = buffer.shape[1] // ways
        mine = (lax.axis_index(axis) // unit) % ways
        cut = lambda d: lax.dynamic_slice_in_dim(buffer, (mine ^ d) * part, part, 1)
        arrived = [swap(cut(d), axis, d * unit) for d in range(1, ways)]
        buffer = between(functools.reduce(jnp.add, arrived, cut(0)), number)
    for number, (axis, ways, unit) in enumerate(stages[::-1]):
        part = buffer.shape[1]
        mine = (lax.axis_index(axis) // unit) % ways
        whole = blank((buffer.shape[0], ways * part), f32)
        for d in range(ways):
            piece = swap(buffer, axis, d * unit) if d else buffer
            whole = lax.dynamic_update_slice_in_dim(whole, piece, (mine ^ d) * part, 1)
        buffer = between(whole, 3 + number)
    return buffer


def packed_up(tables, vectors):
    devices = lax.axis_size("dp") * lax.axis_size("blk")
    joined = jnp.concatenate([*tables, *[v.reshape(16, -1) for v in vectors]], axis=1)
    return jnp.pad(joined, ((0, 0), (0, -joined.shape[1] % (128 * devices))))


def unpacked(joined, tables, vectors):
    out, at = [], 0
    for t in (*tables, *vectors):
        size = t.size // 16
        out.append(joined[:, at : at + size].reshape(t.shape))
        at += size
    return out[: len(tables)], out[len(tables) :]


def per_device(
    tokens,
    cotangent,
    document_length_list,
    attention_norm_gain,
    feedforward_norm_gain,
    frozen_query_key_value,
    query_key_value_downmap,
    query_key_value_upmap,
    query_key_value_norm,
    frozen_output_weight,
    output_adapter_downmap,
    output_adapter_upmap,
    output_column_norm,
    frozen_gate_up_weight,
    gate_up_adapter_downmap,
    gate_up_adapter_upmap,
    gate_up_column_norm,
    frozen_down_weight,
    down_adapter_downmap,
    down_adapter_upmap,
    down_column_norm,
):
    length = tokens.shape[0]
    members, groups = lax.axis_size("blk"), lax.axis_size("dp")
    me, line = lax.axis_index("blk"), lax.axis_index("dp")
    count = length * members
    mates = members // QUAD
    wide = frozen_output_weight.shape[1]
    heads = wide // HDIM
    hidden = frozen_gate_up_weight.shape[2]
    lens_row = document_length_list[0]
    rank = ADAPTER_RANK
    flip = lambda a: jnp.swapaxes(a, -1, -2)

    def home(array, axis, width, who=None):
        return lax.dynamic_slice_in_dim(array, (me if who is None else who) * width, width, axis)

    def by_head(array):
        split = array.reshape(3, array.shape[1], heads, HDIM)
        return jnp.transpose(split, (1, 2, 0, 3)).reshape(array.shape[1], 3 * wide)

    def by_three(array):
        split = array.reshape(array.shape[0], heads, 3, HDIM)
        return jnp.transpose(split, (2, 0, 1, 3)).reshape(3, array.shape[0], wide)

    x_full = tokens.astype(f32)
    normed_one, inverse_one = normalize(x_full, attention_norm_gain)
    h_one = normed_one.astype(bf16)
    h_all = lax.all_gather(h_one, "blk", axis=0, tiled=True)

    w_out, n_out = merge(
        after(frozen_output_weight, h_one)[None],
        flip(output_adapter_downmap)[None],
        home(output_adapter_upmap, 1, wide)[None],
        home(output_column_norm, 0, wide)[None],
    )
    gu, n_gu = merge_rows(
        flip(frozen_gate_up_weight),
        flip(gate_up_adapter_downmap),
        home(gate_up_adapter_upmap, 2, hidden),
        home(gate_up_column_norm, 1, hidden)[:, :, None],
        mates,
    )
    b_qkv = home(query_key_value_upmap, 2, wide)
    m_qkv = by_head(home(query_key_value_norm, 1, wide)[:, None, :])
    w_qkv, n_qkv = merge(frozen_query_key_value, flip(query_key_value_downmap), b_qkv, m_qkv)
    w_down, n_down = merge(
        frozen_down_weight[None],
        flip(down_adapter_downmap)[None],
        home(down_adapter_upmap, 1, wide)[None],
        home(down_column_norm, 0, wide)[None],
    )
    places, begins, end = begins_of(lens_row, count)
    half = HDIM // 2
    freq = rope_base ** (-(jnp.arange(half, dtype=f32) * 2.0 / HDIM))
    angle = (places - begins).astype(f32)[:, None] * freq[None, :]
    cosine, sine = jnp.cos(angle), jnp.sin(angle)
    cosine = jnp.concatenate([cosine, cosine], axis=1)
    sine = jnp.concatenate([-sine, sine], axis=1)
    begin = begins[None, :]
    valid = (me * length + jnp.arange(length, dtype=jnp.int32)) < end
    d_final = cotangent.astype(f32) * valid.astype(f32)[:, None]
    d_final_low = d_final.astype(bf16)

    def spread_rows(chunks):
        got = lax.all_to_all(chunks, "blk", 0, 0, tiled=True)
        return jnp.transpose(got, (1, 0, 2)).reshape(chunks.shape[1], members * wide)

    def spread_rows(chunks):
        got = lax.all_to_all(chunks, "blk", 0, 0, tiled=True)
        return jnp.transpose(got, (1, 0, 2)).reshape(chunks.shape[1], members * wide)

    w_out, gu = after((w_out, gu), w_qkv, w_down, cosine, sine)
    piece = MODEL_WIDTH // (2 * groups)
    core = me % 2
    pair = lax.dynamic_slice_in_dim(w_out, 2 * line * piece, 2 * piece, 0)
    pair = pair.reshape(1, 2, piece, wide)
    mine = spread_rows(jnp.tile(pair, (members // 2, 1, 1, 1)).reshape(members, piece, wide))
    mine = dp_steps(dp_start(mine), 0, 1)
    piece = mates * hidden // groups
    per_shard = groups // mates
    turn = line // per_shard
    shards = lax.dynamic_slice_in_dim(
        after(w_down, w_out).reshape(mates, QUAD, hidden, wide),
        (line % per_shard) * piece,
        piece,
        2,
    )
    chosen = jnp.stack(
        [
            functools.reduce(
                lambda rest, k: jnp.where(turn == k, shards[q ^ k], rest),
                range(1, mates),
                shards[q],
            )
            for q in range(mates)
        ]
    ).reshape(members, piece, wide)
    own = jnp.concatenate([n_out[0], n_gu[0, :, 0], n_gu[1, :, 0], n_down[0]])
    own = jnp.pad(own, (0, -own.shape[0] % wide)).reshape(-1, wide)
    own_high = lax.reduce_precision(own, 8, 7)
    riders = jnp.concatenate([own_high, own - own_high], axis=0).astype(bf16)
    extra = -riders.shape[0] % 16
    riders = jnp.pad(riders, ((0, extra), (0, 0)))
    riders = jnp.broadcast_to(riders[None], (members, *riders.shape))
    rows_down = spread_rows(jnp.concatenate([chosen, riders], axis=1))
    norm_rows = rows_down[piece:].astype(f32)
    norms = norm_rows[: own.shape[0]] + norm_rows[own.shape[0] : 2 * own.shape[0]]
    norms = jnp.transpose(norms.reshape(own.shape[0], members, wide), (1, 0, 2))
    norms = norms.reshape(members, own.shape[0] * wide)
    rows_down = rows_down[:piece]
    piece_gu = hidden // groups
    gu_part = lax.dynamic_slice(
        gu, (0, 0, line * piece_gu, 0), (1, 2, piece_gu, MODEL_WIDTH)
    ).reshape(2, piece_gu, MODEL_WIDTH)
    gate_part = after(gu_part[0], rows_down)
    gate_parts = [swap(gate_part, "blk", QUAD * k) for k in range(1, mates)]
    h_all, d_final_low, mine, rows_down = after((h_all, d_final_low, mine, rows_down), cosine)

    mine = dp_last(dp_steps(mine, 1, -1))
    down_rows = lax.all_gather(rows_down, "dp", axis=0, tiled=True)
    triple = dot(h_all, w_qkv)
    q, k, v, attended_heads, mixed_t, lse = attention_forward(triple, cosine, sine, begin)


    attended_heads = after(attended_heads, mine, gate_parts)
    mine, d_final_low, gate_parts = after((mine, d_final_low, gate_parts), attended_heads)
    over = swap(mine, "blk", 1)
    up_part = after(gu_part[1], attended_heads)
    up_parts = [swap(up_part, "blk", QUAD * k) for k in range(1, mates)]
    gate_states = [dp_steps(dp_start(g), 0, 1) for g in gate_parts]
    out_full = blank((groups, 2, MODEL_WIDTH // (2 * groups), MODEL_WIDTH), bf16)
    out_full = dp_lay(mine, out_full, core)
    out_full = dp_lay(over, out_full, 1 - core).reshape(MODEL_WIDTH, MODEL_WIDTH)
    attended = lax.all_to_all(
        attended_heads.reshape(members, length, wide), "blk", 0, 0, tiled=True
    )
    a_low = flip(query_key_value_downmap).astype(bf16).reshape(3 * rank, MODEL_WIDTH)
    h_all_late = after(h_all, attended_heads)
    xa_qkv = dot(a_low, h_all_late, NT).astype(bf16)
    chips = members // 2
    xa_qkv = jnp.transpose(xa_qkv.reshape(3 * rank, chips, 2 * length), (1, 0, 2))
    aw_qkv = dot(a_low, w_qkv)
    row = lax.broadcasted_iota(jnp.int32, (3 * rank, 3 * wide), 0) // rank
    column = (lax.broadcasted_iota(jnp.int32, (3 * rank, 3 * wide), 1) // HDIM) % 3
    own_block = row == column
    spread_qkv = jnp.where(own_block, jnp.tile(by_head(b_qkv), (3, 1)), 0.0)
    attended = after(
        attended, xa_qkv, aw_qkv, spread_qkv, out_full, gate_states, up_parts
    )

    attended = jnp.transpose(attended, (1, 0, 2)).reshape(length, MODEL_WIDTH)
    a_out_low = flip(output_adapter_downmap).astype(bf16)
    y_out = dot(jnp.concatenate([attended, a_out_low], axis=0), out_full)
    y_out, aw_out = y_out[:length], y_out[length:]
    residual = x_full + y_out
    normed_two, inverse_two = normalize(residual, feedforward_norm_gain)
    h_two = normed_two.astype(bf16)
    up_parts, d_final_low, gate_states = after((up_parts, d_final_low, gate_states), attended)
    gate_states = [dp_last(dp_steps(state, 1, -1)) for state in gate_states]
    d_final_pair = jnp.concatenate([d_final_low, swap(d_final_low, "blk", 2)], axis=0)
    up_states = [dp_steps(dp_start(g), 0, 1) for g in up_parts]
    h_two = after(h_two, up_states, d_final_pair)

    attended_late = after(attended, h_two)
    xa_out = dot(a_out_low, attended_late, NT).astype(bf16)
    up_states = [dp_last(dp_steps(after(state, h_two), 1, -1)) for state in up_states]
    d_final_pair = after(d_final_pair, h_two)
    d_final_all = jnp.concatenate([d_final_pair, swap(d_final_pair, "blk", 1)], axis=0)
    for k_ in range(1, mates):
        gu = dp_lay(gate_states[k_ - 1], gu, (k_, 0))
        gu = dp_lay(up_states[k_ - 1], gu, (k_, 1))
    gu = gu.reshape(mates * 2 * hidden, MODEL_WIDTH)
    a_gu_low = flip(gate_up_adapter_downmap).astype(bf16).reshape(2 * rank, MODEL_WIDTH)
    norms_out = norms[:, :wide].reshape(-1)
    norms_down = norms[:, wide + 2 * hidden : 2 * wide + 2 * hidden].reshape(-1)

    h_two_all = after(quad_gather(h_two), xa_out, gu, down_rows)
    acts, g_gu, gm_gu = feed_forward(gu, down_rows, h_two_all, d_final_all, mates)
    dh_parts = dot(g_gu, gu, TN).astype(bf16)
    dh_half = quad_halve(dh_parts)
    dh_two = quad_finish(dh_half)

    acts_late, down_late, h_two_late, gu_late = after(
        (acts, down_rows, h_two_all, gu), dh_half
    )
    y_parts = dot(acts_late, down_late, TN).astype(bf16)
    a_down_low = flip(down_adapter_downmap).astype(bf16)
    order = [me ^ (QUAD * k_) for k_ in range(mates)]
    low = jnp.concatenate([home(a_down_low, 1, hidden, who) for who in order], axis=1)
    xa_down = dot(low, acts_late).astype(bf16)
    aw_down = dot(low, down_late)
    xa_gu = dot(a_gu_low, h_two_late, NT).astype(bf16)
    aw_gu = dot(a_gu_low, gu_late, NT)
    dh_two = after(dh_two, y_parts, xa_down, aw_down, xa_gu, aw_gu)

    d_norm_two = normalize_back(residual, inverse_two, feedforward_norm_gain, dh_two)
    d_residual = d_final + d_norm_two
    g_out = d_residual.astype(bf16)
    d_attended = dot(g_out, out_full, NT).astype(bf16)
    d_parts = jnp.transpose(d_attended.reshape(length, members, wide), (1, 0, 2))
    d_heads = lax.all_to_all(d_parts, "blk", 0, 0, tiled=True).reshape(count, wide)

    y_down = quad_finish(quad_halve(after(y_parts, d_parts)))
    result = (residual + y_down).astype(bf16)
    g_late, h_two_late, gu_late, gm_gu = after((g_gu, h_two_all, gu, gm_gu), d_parts)

    def joined(pick):
        return jnp.concatenate([pick(who, i) for who in order for i in range(2)], axis=-1)

    m_gu = joined(lambda who, i: home(gate_up_column_norm[i], 0, hidden, who))
    n_gu_all = joined(
        lambda who, i: lax.dynamic_slice(norms, (who, wide + i * hidden), (1, hidden))[0]
    )
    b_gu = joined(lambda who, i: home(gate_up_adapter_upmap[i], 1, hidden, who))
    s_gu = m_gu / n_gu_all
    gm_gu = gm_gu.reshape(-1) / m_gu
    row = lax.broadcasted_iota(jnp.int32, (2 * rank, b_gu.shape[1]), 0) // rank
    column = (lax.broadcasted_iota(jnp.int32, (2 * rank, b_gu.shape[1]), 1) // hidden) % 2
    own_gu = row == column
    spread = jnp.where(own_gu, jnp.tile(b_gu, (2, 1)), 0.0)
    p_gu = dot((spread * s_gu).astype(bf16), g_late).astype(bf16)
    tilt = (spread * (gm_gu / n_gu_all)).astype(bf16)
    gb_gu = adapter_scale * (dot(xa_gu, g_late, NT) * s_gu - aw_gu * (gm_gu / n_gu_all))
    gb_gu = jnp.sum(jnp.where(own_gu, gb_gu, 0.0).reshape(2, rank, -1), axis=0)
    d_heads = after(d_heads, p_gu, tilt, gb_gu)

    g_three, gm_heads = attention_backward(
        q, k, v, triple, cosine, sine, begin, d_heads, mixed_t, lse
    )
    gm_down = jnp.sum(d_final_low.astype(f32) * y_down, axis=0) / down_column_norm
    g_three = after(g_three, gm_down)
    own_rows, other_rows, grad_a, grad_b, grad_g_attn, gm = back_qkv(
        g_three, h_all, w_qkv, spread_qkv, m_qkv, n_qkv, gm_heads, xa_qkv, aw_qkv
    )
    gm_quad = gm_down + swap(gm_down, "blk", 1)
    total = (own_rows.astype(f32) + swap(other_rows, "blk", 1).astype(f32)).astype(bf16)
    total, gm_quad = after((total, gm_quad))
    state = chips_step(total, 1, None)
    gm_quad = gm_quad + swap(gm_quad, "blk", 2)
    acts_late, d_final_late, dh_late, unit_two, g_out, out_late = after(
        (acts, d_final_all, dh_two, residual * inverse_two, g_out, out_full), gm_quad
    )
    grad_g_ffn = jnp.sum(dh_late * unit_two, axis=0)
    gm_out = jnp.sum(g_out.astype(f32) * y_out, axis=0) / output_column_norm
    s_out = output_column_norm / norms_out
    p_out = dot((output_adapter_upmap * s_out).astype(bf16), g_out, NT).astype(bf16)
    tilt_out = (output_adapter_upmap * (gm_out / norms_out)).astype(bf16)
    ga_out = adapter_scale * (dot(p_out, attended) - dot(tilt_out, out_late, NT))
    gb_out = adapter_scale * (dot(xa_out, g_out) * s_out - aw_out * (gm_out / norms_out))
    s_down = down_column_norm / norms_down
    p_down = dot((down_adapter_upmap * s_down).astype(bf16), d_final_late, NT).astype(bf16)
    state = after(state, ga_out, gb_out, grad_g_ffn, p_down, gm_quad)

    gm_quad, p_down, p_gu, tilt = after((gm_quad, p_down, p_gu, tilt), state)
    ga_gu = adapter_scale * (dot(p_gu, h_two_late) - dot(tilt, gu_late))
    tilt_down = (down_adapter_upmap * (gm_quad / norms_down)).astype(bf16)
    ga_down = adapter_scale * (dot(p_down, acts_late, NT) - dot(tilt_down, down_rows, NT))
    gb_down = adapter_scale * (
        dot(xa_down, d_final_late) * s_down - aw_down * (gm_quad / norms_down)
    )
    room = -hidden % 128
    place = jnp.stack(order)[:, None] == jnp.arange(members)[None, :]

    def spread_shards(array):
        array = jnp.pad(array, [(0, 0)] * (array.ndim - 1) + [(0, room)])
        return sum(
            jnp.where(place[k_][:, None], array[..., k_, None, :], 0.0) for k_ in range(mates)
        )

    gb_both = jnp.swapaxes(gb_gu.reshape(rank, mates, 2, hidden), 1, 2)
    tall = jnp.stack([gb_both[:, 0], gb_both[:, 1], ga_down.reshape(rank, mates, hidden)])
    tall = spread_shards(tall).reshape(3, rank, -1)
    thin = spread_shards(jnp.swapaxes(gm_gu.reshape(mates, 2, hidden), 0, 1)).reshape(2, -1)
    grad_b = jnp.sum(jnp.where(own_block, grad_b, 0.0).reshape(3, rank, 3 * wide), axis=0)
    mine_only = jnp.arange(members)[:, None] == me
    b_all = jnp.where(mine_only, by_three(adapter_scale * grad_b)[:, :, None, :], 0.0)
    b_all = b_all.reshape(3, rank, MODEL_WIDTH)
    m_all = jnp.where(mine_only, by_three(gm)[:, 0][:, None, :], 0.0).reshape(3, MODEL_WIDTH)
    grad_g_attn = grad_g_attn[0] / attention_norm_gain
    grad_a = adapter_scale * grad_a
    tables = (
        [grad_a[i * rank : (i + 1) * rank] for i in range(3)]
        + [b_all[i] for i in range(3)]
        + [ga_out, gb_out, ga_gu[:rank], ga_gu[rank:], gb_down]
        + [tall[0], tall[1], tall[2]]
    )
    vectors = [grad_g_attn, grad_g_ffn, gm_out, gm_down, m_all[0], m_all[1], m_all[2]]
    vectors += [thin[0], thin[1]]
    packed = packed_up(tables, vectors)
    for t in range(2, chips - 1):
        state = chips_step(total, t, state)
        state = after(state, packed)
    packed = after(packed, state)
    ends = {}

    def between(buffer, stage):
        if stage == 2:
            ends[0] = after(chips_step(total, chips - 1, state), buffer)
            buffer = after(buffer, ends[0])
        return buffer

    tables, vectors = unpacked(total_sum(packed, between), tables, vectors)
    d_norm_one = normalize_back(
        x_full, inverse_one, attention_norm_gain, chips_end(total, ends[0])
    )
    grad_input = d_residual + d_norm_one
    dense = lambda array: array.reshape(-1, members, hidden + room)[:, :, :hidden].reshape(
        array.shape[:-1] + (members * hidden,)
    )
    a_out, b_out, a_gate, a_up, b_down = tables[6:11]
    b_gate, b_up, a_down = [dense(t) for t in tables[11:]]
    return (
        result,
        grad_input,
        vectors[0],
        vectors[1],
        flip(jnp.stack(tables[:3])),
        jnp.stack(tables[3:6]),
        jnp.stack(vectors[4:7]),
        flip(a_out),
        b_out,
        vectors[2],
        flip(jnp.stack([a_gate, a_up])),
        jnp.stack([b_gate, b_up]),
        jnp.stack([dense(v) for v in vectors[7:]]),
        flip(a_down),
        b_down,
        vectors[3],
    )


def solution(mesh):
    rows, none = P(("dp", "blk"), None), P()
    in_specs = (
        rows,
        rows,
        P("dp", None),
        none,
        none,
        P(None, None, "blk"),
        none,
        none,
        none,
        P(None, "blk"),
        none,
        none,
        none,
        P(None, None, "blk"),
        none,
        none,
        none,
        P(None, "blk"),
        none,
        none,
        none,
    )
    out_specs = (rows, rows) + (none,) * 14
    return jax.shard_map(
        per_device, mesh=mesh, in_specs=in_specs, out_specs=out_specs, check_vma=False
    )
```

```python
import functools

import jax
import jax.numpy as jnp
from jax import lax
from jax.experimental import pallas as pl
from jax.experimental.pallas import tpu as pltpu
from jax.sharding import PartitionSpec as P

MODEL_WIDTH = 2048
HEADS = 16
ADAPTER_RANK = 16
ALPHA = 32
HDIM = 128
TILE = 256
QUAD = 4

norm_eps = 1e-05
column_eps = 1e-06
rope_base = 10000.0
far_negative = -1e30
log2_e = 1.4426950408889634
adapter_scale = ALPHA / ADAPTER_RANK
bf16 = jnp.bfloat16
f32 = jnp.float32
NT = (((1,), (1,)), ((), ()))
TN = (((0,), (0,)), ((), ()))
NN = (((1,), (0,)), ((), ()))


def dot(a, b, dims=NN):
    return lax.dot_general(a, b, dims, preferred_element_type=f32)


def after(array, *earlier):
    return lax.optimization_barrier((array, *earlier))[0]


def blank(shape, dtype):
    return pl.pallas_call(
        lambda out: None,
        out_shape=jax.ShapeDtypeStruct(shape, dtype),
        out_specs=pl.BlockSpec(memory_space=pl.ANY),
        name="blank",
    )()


def swap(array, axis, bit):
    return lax.ppermute(array, axis, [(i, i ^ bit) for i in range(lax.axis_size(axis))])


def axis_sum(array, axis):
    bit = 1
    while bit < lax.axis_size(axis):
        array = array + swap(array, axis, bit)
        bit *= 2
    return array


def begins_of(lens_row, count):
    places = jnp.arange(count, dtype=jnp.int32)
    ends = jnp.cumsum(lens_row, dtype=jnp.int32)
    after = (places[:, None] >= ends[None, :]).astype(jnp.int32)
    return places, jnp.sum(after * lens_row[None, :], axis=1, dtype=jnp.int32), ends[-1]


def split_three(a):
    one = lax.reduce_precision(a, 8, 7)
    rest = a - one
    two = lax.reduce_precision(rest, 8, 7)
    return one.astype(bf16), two.astype(bf16), (rest - two).astype(bf16)


def parts_of(a, b):
    a1, a2, a3 = split_three(a * adapter_scale)
    b1, b2, b3 = split_three(b)
    return (
        jnp.concatenate([a1, a1, a2, a1, a2, a3], axis=-2),
        jnp.concatenate([b1, b2, b1, b3, b2, b1], axis=-2),
    )


def merge_kernel(w_ref, a_ref, b_ref, m_ref, out_ref, n_ref, v_ref):
    rows = w_ref.shape[1]

    def add(i, acc):
        at = pl.ds(pl.multiple_of(i * TILE, TILE), TILE)
        v = w_ref[0, at, :].astype(f32) + dot(a_ref[0, :, at], b_ref[0], TN)
        v_ref[at, :] = v
        return acc + jnp.sum(v * v, axis=0, keepdims=True)

    total = lax.fori_loop(0, rows // TILE, add, jnp.zeros(m_ref.shape, f32), unroll=2)
    norms = jnp.sqrt(total + column_eps)
    n_ref[...] = norms
    s = m_ref[...] / norms

    def put(i, carry):
        at = pl.ds(pl.multiple_of(i * TILE, TILE), TILE)
        out_ref[at, :] = (v_ref[at, :] * s).astype(bf16)
        return carry

    lax.fori_loop(0, rows // TILE, put, 0, unroll=2)


def merge(w, a, b, m):
    k, rows, cols = w.shape
    a_cat, b_cat = parts_of(a, b)
    wide = a_cat.shape[1]
    place = lambda i, h: (0, h * k + i)
    return pl.pallas_call(
        merge_kernel,
        grid=(k, cols // HDIM),
        in_specs=[
            pl.BlockSpec((1, rows, HDIM), lambda i, h: (i, 0, h)),
            pl.BlockSpec((1, wide, rows), lambda i, h: (i, 0, 0)),
            pl.BlockSpec((1, wide, HDIM), lambda i, h: (i, 0, h)),
            pl.BlockSpec((1, HDIM), place),
        ],
        out_specs=[pl.BlockSpec((rows, HDIM), place), pl.BlockSpec((1, HDIM), place)],
        out_shape=[
            jax.ShapeDtypeStruct((rows, k * cols), bf16),
            jax.ShapeDtypeStruct((1, k * cols), f32),
        ],
        scratch_shapes=[pltpu.VMEM((rows, HDIM), f32)],
        compiler_params=pltpu.CompilerParams(vmem_limit_bytes=48 * 2**20),
        cost_estimate=pl.CostEstimate(
            flops=2 * k * rows * cols * wide, bytes_accessed=4 * k * rows * cols, transcendentals=0
        ),
        name="merge",
    )(w, a_cat, b_cat, m)


def merge_rows_kernel(w_ref, a_ref, b_ref, m_ref, out_ref, n_ref):
    out_ref = out_ref.at[0]
    v = w_ref[0].astype(f32) + dot(b_ref[0], a_ref[0], TN)
    norms = jnp.sqrt(jnp.sum(v * v, axis=1, keepdims=True) + column_eps)
    n_ref[0] = norms
    out_ref[0] = (v * (m_ref[0] / norms)).astype(bf16)


def merge_rows(w, a, b, m, mates):
    k, cols, rows = w.shape
    a_cat, b_cat = parts_of(a, b)
    wide = a_cat.shape[1]
    return pl.pallas_call(
        merge_rows_kernel,
        grid=(k,),
        in_specs=[
            pl.BlockSpec((1, cols, rows), lambda i: (i, 0, 0)),
            pl.BlockSpec((1, wide, rows), lambda i: (i, 0, 0)),
            pl.BlockSpec((1, wide, cols), lambda i: (i, 0, 0)),
            pl.BlockSpec((1, cols, 1), lambda i: (i, 0, 0)),
        ],
        out_specs=[
            pl.BlockSpec((1, 1, cols, rows), lambda i: (0, i, 0, 0)),
            pl.BlockSpec((1, cols, 1), lambda i: (i, 0, 0)),
        ],
        out_shape=[
            jax.ShapeDtypeStruct((mates, k, cols, rows), bf16),
            jax.ShapeDtypeStruct((k, cols, 1), f32),
        ],
        compiler_params=pltpu.CompilerParams(vmem_limit_bytes=56 * 2**20),
        cost_estimate=pl.CostEstimate(
            flops=2 * k * rows * cols * wide, bytes_accessed=4 * k * rows * cols, transcendentals=0
        ),
        name="merge_rows",
    )(w, a_cat, b_cat, m)


def turned(u, cosine, sine):
    return u * cosine + pltpu.roll(u, HDIM // 2, 1) * sine


def forward_kernel(
    pre, cosine, sine, begin, q_out, k_out, v_out, att_out, mixed_t, lse_out, v_t
):
    count = pre.shape[0]
    scale = HDIM**-0.5 * log2_e
    for i in range(count // TILE):
        at = pl.ds(i * TILE, TILE)
        cos, sin = cosine[at, :], sine[at, :]
        q_out[at, :] = turned(pre[at, :HDIM], cos, sin).astype(bf16)
        k_out[at, :] = turned(pre[at, HDIM : 2 * HDIM], cos, sin).astype(bf16)
        v = pre[at, 2 * HDIM :]
        v_out[at, :] = v.astype(bf16)
        v_t[:, at] = v.T.astype(bf16)
    for i in range(count // TILE):
        rows = pl.ds(i * TILE, TILE)
        q = q_out[rows, :]
        start = begin[:, rows]

        def visit(j, state, diagonal):
            top, total, mixed = state
            keys = pl.ds(pl.multiple_of(j * TILE, TILE), TILE)
            s = dot(k_out[keys, :], q, NT) * scale
            place = j * TILE + lax.broadcasted_iota(jnp.int32, (TILE, TILE), 0)
            allowed = place >= start
            if diagonal:
                mine = i * TILE + lax.broadcasted_iota(jnp.int32, (TILE, TILE), 1)
                allowed = allowed & (place <= mine)
            s = jnp.where(allowed, s, far_negative)
            high = jnp.maximum(top, jnp.max(s, axis=0, keepdims=True))
            keep = jnp.exp2(top - high)
            p = jnp.exp2(s - high)
            total = total * keep + jnp.sum(p, axis=0, keepdims=True)
            mixed = mixed * keep + dot(v_t[:, keys], p.astype(bf16))
            return high, total, mixed

        state = (
            jnp.full((1, TILE), far_negative, f32),
            jnp.zeros((1, TILE), f32),
            jnp.zeros((HDIM, TILE), f32),
        )
        state = visit(i, state, True)
        for j in range(i):
            state = visit(j, state, False)
        top, total, mixed = state
        mixed = mixed / total
        mixed_t[:, rows] = mixed
        att_out[rows, :] = mixed.T.astype(bf16)
        lse_out[0, :, rows] = top + jnp.log2(total)


def backward_kernel(
    q_ref, k_ref, v_ref, pre, cosine, sine, begin, grad_att, mixed_t, lse,
    g_out, gm_out, dk, dv, k_t,
):
    count = q_ref.shape[0]
    scale = HDIM**-0.5
    dk[...] = jnp.zeros_like(dk)
    dv[...] = jnp.zeros_like(dv)
    for i in range(count // TILE):
        at = pl.ds(i * TILE, TILE)
        k_t[:, at] = k_ref[at, :].astype(f32).T.astype(bf16)
    gm_q = jnp.zeros((1, HDIM), f32)
    for i in range(count // TILE):
        rows = pl.ds(i * TILE, TILE)
        q = q_ref[rows, :]
        d_mixed = grad_att[rows, :]
        delta = jnp.sum(d_mixed.astype(f32).T * mixed_t[:, rows], axis=0, keepdims=True)
        start = begin[:, rows]
        high = lse[0, :, rows]
        dq_t = jnp.zeros((HDIM, TILE), f32)
        for j in range(i + 1):
            keys = pl.ds(j * TILE, TILE)
            s = dot(k_ref[keys, :], q, NT) * (scale * log2_e)
            place = j * TILE + lax.broadcasted_iota(jnp.int32, (TILE, TILE), 0)
            allowed = place >= start
            if j == i:
                mine = i * TILE + lax.broadcasted_iota(jnp.int32, (TILE, TILE), 1)
                allowed = allowed & (place <= mine)
            p = jnp.where(allowed, jnp.exp2(s - high), 0.0)
            dp = dot(v_ref[keys, :], d_mixed, NT)
            ds = (p * (dp - delta)).astype(bf16)
            dv[keys, :] += dot(p.astype(bf16), d_mixed)
            dk[keys, :] += dot(ds, q)
            dq_t = dq_t + dot(k_t[:, keys], ds)
        gq = turned(dq_t.T * scale, cosine[rows, :], -sine[rows, :]).astype(bf16)
        g_out[rows, :HDIM] = gq
        gm_q = gm_q + jnp.sum(gq.astype(f32) * pre[rows, :HDIM], axis=0, keepdims=True)
    gm_k = jnp.zeros((1, HDIM), f32)
    gm_v = jnp.zeros((1, HDIM), f32)
    for i in range(count // TILE):
        at = pl.ds(i * TILE, TILE)
        gk = turned(dk[at, :] * scale, cosine[at, :], -sine[at, :]).astype(bf16)
        g_out[at, HDIM : 2 * HDIM] = gk
        gm_k = gm_k + jnp.sum(gk.astype(f32) * pre[at, HDIM : 2 * HDIM], axis=0, keepdims=True)
        gv = dv[at, :].astype(bf16)
        g_out[at, 2 * HDIM :] = gv
        gm_v = gm_v + jnp.sum(gv.astype(f32) * pre[at, 2 * HDIM :], axis=0, keepdims=True)
    gm_out[0:1, :HDIM] = gm_q
    gm_out[0:1, HDIM : 2 * HDIM] = gm_k
    gm_out[0:1, 2 * HDIM :] = gm_v


def attention_forward(triple, cosine, sine, begin):
    count, width = triple.shape[0], triple.shape[1] // 3
    heads = width // HDIM
    whole = lambda h: (0, 0)
    head = lambda h: (0, h)
    tall = lambda at: pl.BlockSpec((count, HDIM), at)
    return pl.pallas_call(
        forward_kernel,
        grid=(heads,),
        in_specs=[
            pl.BlockSpec((count, 3 * HDIM), head),
            tall(whole),
            tall(whole),
            pl.BlockSpec((1, count), whole),
        ],
        out_specs=[
            tall(head),
            tall(head),
            tall(head),
            tall(head),
            pl.BlockSpec((HDIM, count), lambda h: (h, 0)),
            pl.BlockSpec((1, 1, count), lambda h: (h, 0, 0)),
        ],
        out_shape=[jax.ShapeDtypeStruct((count, width), bf16)] * 4
        + [
            jax.ShapeDtypeStruct((width, count), f32),
            jax.ShapeDtypeStruct((heads, 1, count), f32),
        ],
        scratch_shapes=[pltpu.VMEM((HDIM, count), bf16)],
        compiler_params=pltpu.CompilerParams(vmem_limit_bytes=48 * 2**20),
        cost_estimate=pl.CostEstimate(
            flops=2 * count * count * width, bytes_accessed=30 * count * width, transcendentals=0
        ),
        name="attend",
    )(triple, cosine, sine, begin)


def attention_backward(q, k, v, triple, cosine, sine, begin, grad_att, mixed_t, lse):
    count, width = q.shape
    heads = width // HDIM
    whole = lambda h: (0, 0)
    head = lambda h: (0, h)
    tall = lambda at: pl.BlockSpec((count, HDIM), at)
    return pl.pallas_call(
        backward_kernel,
        grid=(heads,),
        in_specs=[
            tall(head),
            tall(head),
            tall(head),
            pl.BlockSpec((count, 3 * HDIM), head),
            tall(whole),
            tall(whole),
            pl.BlockSpec((1, count), whole),
            tall(head),
            pl.BlockSpec((HDIM, count), lambda h: (h, 0)),
            pl.BlockSpec((1, 1, count), lambda h: (h, 0, 0)),
        ],
        out_specs=[pl.BlockSpec((count, 3 * HDIM), head), pl.BlockSpec((8, 3 * HDIM), head)],
        out_shape=[
            jax.ShapeDtypeStruct((count, 3 * width), bf16),
            jax.ShapeDtypeStruct((8, 3 * width), f32),
        ],
        scratch_shapes=[
            pltpu.VMEM((count, HDIM), f32),
            pltpu.VMEM((count, HDIM), f32),
            pltpu.VMEM((HDIM, count), bf16),
        ],
        compiler_params=pltpu.CompilerParams(vmem_limit_bytes=48 * 2**20),
        cost_estimate=pl.CostEstimate(
            flops=5 * count * count * width, bytes_accessed=40 * count * width, transcendentals=0
        ),
        name="attend_back",
    )(q, k, v, triple, cosine, sine, begin, grad_att, mixed_t, lse)


def feed_kernel(gu_ref, down_ref, h_ref, d_ref, acts_out, g_out, gm_out):
    h = h_ref[...]
    gate = dot(gu_ref[0, 0], h, NT)
    upward = dot(gu_ref[0, 1], h, NT)
    d_act = dot(down_ref[...], d_ref[...], NT)
    sigmoid_gate = jax.nn.sigmoid(gate)
    silu = gate * sigmoid_gate
    acts_out[...] = (silu * upward).astype(bf16)
    d_gate = (d_act * upward * sigmoid_gate * (1.0 + gate * (1.0 - sigmoid_gate))).astype(bf16)
    d_upward = (d_act * silu).astype(bf16)
    g_out[0, 0] = d_gate
    g_out[0, 1] = d_upward
    gm_out[0, 0] = jnp.sum(d_gate.astype(f32) * gate, axis=1, keepdims=True)
    gm_out[0, 1] = jnp.sum(d_upward.astype(f32) * upward, axis=1, keepdims=True)


def feed_forward(gu, down, h, d, mates):
    rows, width = h.shape
    hidden = down.shape[0] // mates
    unit = hidden // max(1, hidden // 352)
    steps = hidden // unit
    flat = lambda k, j: (k * steps + j, 0)
    deep = lambda k, j: (k, 0, j, 0)
    whole = lambda k, j: (0, 0)
    acts, g, gm = pl.pallas_call(
        feed_kernel,
        grid=(mates, steps),
        in_specs=[
            pl.BlockSpec((1, 2, unit, width), deep),
            pl.BlockSpec((unit, width), flat),
            pl.BlockSpec((rows, width), whole),
            pl.BlockSpec((rows, width), whole),
        ],
        out_specs=[
            pl.BlockSpec((unit, rows), flat),
            pl.BlockSpec((1, 2, unit, rows), deep),
            pl.BlockSpec((1, 2, unit, 1), deep),
        ],
        out_shape=[
            jax.ShapeDtypeStruct((mates * hidden, rows), bf16),
            jax.ShapeDtypeStruct((mates, 2, hidden, rows), bf16),
            jax.ShapeDtypeStruct((mates, 2, hidden, 1), f32),
        ],
        compiler_params=pltpu.CompilerParams(vmem_limit_bytes=58 * 2**20),
        cost_estimate=pl.CostEstimate(
            flops=6 * mates * hidden * rows * width,
            bytes_accessed=6 * mates * hidden * width + 4 * rows * width,
            transcendentals=0,
        ),
        name="feed_forward",
    )(gu.reshape(mates, 2, hidden, width), down, h, d)
    return acts, g.reshape(2 * mates * hidden, rows), gm


def back_kernel(
    core, g_ref, h_ref, w_ref, spread, s_ref, over_n, sums, m_ref, xa_ref, aw_ref,
    own_out, other_out, ga_out, gb_out, gg_out, gm_out,
):
    step = pl.program_id(0)
    length = own_out.shape[1]
    g = g_ref[...]
    h = h_ref[...]
    s = s_ref[...]
    dh = dot(g, w_ref[...], NT)
    low = dh.astype(bf16)

    @pl.when(core[0] == 0)
    def _():
        own_out[0] = low[:length]
        other_out[0] = low[length:]

    @pl.when(core[0] != 0)
    def _():
        own_out[0] = low[length:]
        other_out[0] = low[:length]

    p = dot((spread[...] * s).astype(bf16), g, NT).astype(bf16)
    ga = dot(p, h)
    gb = dot(xa_ref[...], g)
    gg = jnp.sum(dh * h.astype(f32), axis=0, keepdims=True)

    @pl.when(step == 0)
    def _():
        gm = sums[0:1, :] / m_ref[...]
        gm_out[...] = gm
        tilt = (spread[...] * (gm * over_n[...])).astype(bf16)
        ga_out[...] = ga - dot(tilt, w_ref[...], NT)
        gb_out[...] = gb * s - aw_ref[...] * (gm * over_n[...])
        gg_out[...] = gg

    @pl.when(step > 0)
    def _():
        ga_out[...] += ga
        gb_out[...] += gb * s
        gg_out[...] += gg


def back_qkv(g, h, w, spread, m, n, sums, xa, aw):
    chips = lax.axis_size("blk") // 2
    core = (lax.axis_index("blk") % 2).astype(jnp.int32).reshape(1)
    count, cols = g.shape
    width = h.shape[1]
    pair = count // chips
    wide = spread.shape[0]
    rows = lambda i, core: (i, 0)
    whole = lambda i, core: (0, 0)
    deep = lambda i, core: (i, 0, 0)
    return pl.pallas_call(
        back_kernel,
        grid_spec=pltpu.PrefetchScalarGridSpec(
            num_scalar_prefetch=1,
            grid=(chips,),
            in_specs=[
                pl.BlockSpec((pair, cols), rows),
                pl.BlockSpec((pair, width), rows),
                pl.BlockSpec((width, cols), whole),
                pl.BlockSpec((wide, cols), whole),
                pl.BlockSpec((1, cols), whole),
                pl.BlockSpec((1, cols), whole),
                pl.BlockSpec((8, cols), whole),
                pl.BlockSpec((1, cols), whole),
                pl.BlockSpec((None, wide, pair), deep),
                pl.BlockSpec((wide, cols), whole),
            ],
            out_specs=[
                pl.BlockSpec((1, pair // 2, width), deep),
                pl.BlockSpec((1, pair // 2, width), deep),
                pl.BlockSpec((wide, width), whole),
                pl.BlockSpec((wide, cols), whole),
                pl.BlockSpec((1, width), whole),
                pl.BlockSpec((1, cols), whole),
            ],
        ),
        out_shape=[
            jax.ShapeDtypeStruct((chips, pair // 2, width), bf16),
            jax.ShapeDtypeStruct((chips, pair // 2, width), bf16),
            jax.ShapeDtypeStruct((wide, width), f32),
            jax.ShapeDtypeStruct((wide, cols), f32),
            jax.ShapeDtypeStruct((1, width), f32),
            jax.ShapeDtypeStruct((1, cols), f32),
        ],
        compiler_params=pltpu.CompilerParams(vmem_limit_bytes=56 * 2**20),
        cost_estimate=pl.CostEstimate(
            flops=3 * count * cols * width, bytes_accessed=8 * count * width, transcendentals=0
        ),
        name="back_qkv",
    )(core, g, h, w, spread, m / n, 1.0 / n, sums, m, xa, aw)


def normalize(values, gain):
    inverse = lax.rsqrt(jnp.mean(values * values, axis=-1, keepdims=True) + norm_eps)
    return (values * inverse * gain, inverse)


def normalize_back(values, inverse, gain, grad):
    unit = values * inverse
    scaled = grad * gain
    return inverse * (scaled - unit * jnp.mean(scaled * unit, axis=-1, keepdims=True))


def quad_gather(block):
    pair = jnp.concatenate([block, swap(block, "blk", 2)], axis=0)
    return jnp.concatenate([pair, swap(pair, "blk", 1)], axis=0)


def quad_halve(parts):
    half = parts.shape[0] // 2
    return parts[:half].astype(f32) + swap(parts[half:], "blk", 1).astype(f32)


def quad_finish(mine):
    half = mine.shape[0] // 2
    return mine[:half] + swap(mine[half:].astype(bf16), "blk", 2).astype(f32)


def step_chips(array, first, last, by):
    pairs = [(2 * i + c, 2 * (i + by) + c) for i in range(first, last + 1) for c in range(2)]
    return lax.ppermute(array, "blk", pairs)


def chips_step(total, t, state):
    chips = total.shape[0]
    chip = lax.axis_index("blk") // 2
    pick = lambda c: lax.dynamic_index_in_dim(
        total, jnp.clip(c, 0, chips - 1), 0, keepdims=False
    )
    up, down = pick(chips - t + chip), pick(t - chips + chip)
    if t > 1:
        up = (up.astype(f32) + state[0].astype(f32)).astype(bf16)
        down = (down.astype(f32) + state[1].astype(f32)).astype(bf16)
    up, down = after((up, down))
    return step_chips(up, 0, t - 1, 1), step_chips(down, chips - t, chips - 1, -1)


def chips_end(total, state):
    chip = lax.axis_index("blk") // 2
    own = lax.dynamic_index_in_dim(total, chip, 0, keepdims=False)
    return own.astype(f32) + state[0].astype(f32) + state[1].astype(f32)


def dp_start(piece):
    half = piece.shape[0] // 2
    return piece[None, :half], piece[None, half:]


def dp_steps(state, first=None, last=None):
    bits = [1 << i for i in range(lax.axis_size("dp").bit_length() - 1)]
    one, two = state
    for step in range(len(bits))[first:last]:
        one = jnp.concatenate([one, swap(one, "dp", bits[step])], axis=0)
        two = jnp.concatenate([two, swap(two, "dp", bits[::-1][step])], axis=0)
    return one, two


def dp_last(state):
    bits = [1 << i for i in range(lax.axis_size("dp").bit_length() - 1)]
    one, two = state
    return jnp.concatenate(
        [one, swap(one, "dp", bits[-1]), two, swap(two, "dp", bits[0])], axis=0
    )


def dp_places():
    groups = lax.axis_size("dp")
    bits = groups.bit_length() - 1
    who = jnp.arange(groups, dtype=jnp.int32) ^ lax.axis_index("dp")
    turned = sum(((who >> i) & 1) << (bits - 1 - i) for i in range(bits))
    return jnp.stack([who, turned + groups]).astype(jnp.int32)


def lay_kernel(places, one, two, into, out):
    place = out.at[0, 0] if len(out.shape) == 5 else out.at[0, 0, 0]
    place[0] = one[0]
    place[1] = two[0]


def dp_lay(state, into, at):
    groups, half, width = state.shape[0] // 2, state.shape[1], state.shape[2]
    shape = into.shape
    if isinstance(at, tuple):
        split = into.reshape(shape[0], shape[1], groups, 2, half, width)
        block = (1, 1, 1, 2, half, width)
        where = lambda c, places: (at[0], at[1], c, 0, 0, 0)
        second = jnp.zeros((1, groups), jnp.int32)
    else:
        split = into.reshape(groups, 2, 2, half, width)
        block = (1, 1, 2, half, width)
        where = lambda c, places: (c, places[2, c], 0, 0, 0)
        second = jnp.full((1, groups), at, jnp.int32)
    out = pl.pallas_call(
        lay_kernel,
        grid_spec=pltpu.PrefetchScalarGridSpec(
            num_scalar_prefetch=1,
            grid=(groups,),
            in_specs=[
                pl.BlockSpec((1, half, width), lambda c, places: (places[0, c], 0, 0)),
                pl.BlockSpec((1, half, width), lambda c, places: (places[1, c], 0, 0)),
                pl.BlockSpec(memory_space=pl.ANY),
            ],
            out_specs=pl.BlockSpec(block, where),
        ),
        out_shape=jax.ShapeDtypeStruct(split.shape, into.dtype),
        input_output_aliases={3: 0},
        name="lay",
    )(jnp.concatenate([dp_places(), second]), state, state, split)
    return out.reshape(shape)


def total_sum(buffer, between):
    stages = [("blk", 2, 1), ("dp", lax.axis_size("dp"), 1), ("blk", lax.axis_size("blk") // 2, 2)]
    for number, (axis, ways, unit) in enumerate(stages):
        part = buffer.shape[1] // ways
        mine = (lax.axis_index(axis) // unit) % ways
        cut = lambda d: lax.dynamic_slice_in_dim(buffer, (mine ^ d) * part, part, 1)
        arrived = [swap(cut(d), axis, d * unit) for d in range(1, ways)]
        buffer = between(functools.reduce(jnp.add, arrived, cut(0)), number)
    for number, (axis, ways, unit) in enumerate(stages[::-1]):
        part = buffer.shape[1]
        mine = (lax.axis_index(axis) // unit) % ways
        whole = blank((buffer.shape[0], ways * part), f32)
        for d in range(ways):
            piece = swap(buffer, axis, d * unit) if d else buffer
            whole = lax.dynamic_update_slice_in_dim(whole, piece, (mine ^ d) * part, 1)
        buffer = between(whole, 3 + number)
    return buffer


def packed_up(tables, vectors):
    devices = lax.axis_size("dp") * lax.axis_size("blk")
    joined = jnp.concatenate([*tables, *[v.reshape(16, -1) for v in vectors]], axis=1)
    return jnp.pad(joined, ((0, 0), (0, -joined.shape[1] % (128 * devices))))


def unpacked(joined, tables, vectors):
    out, at = [], 0
    for t in (*tables, *vectors):
        size = t.size // 16
        out.append(joined[:, at : at + size].reshape(t.shape))
        at += size
    return out[: len(tables)], out[len(tables) :]


def per_device(
    tokens,
    cotangent,
    document_length_list,
    attention_norm_gain,
    feedforward_norm_gain,
    frozen_query_key_value,
    query_key_value_downmap,
    query_key_value_upmap,
    query_key_value_norm,
    frozen_output_weight,
    output_adapter_downmap,
    output_adapter_upmap,
    output_column_norm,
    frozen_gate_up_weight,
    gate_up_adapter_downmap,
    gate_up_adapter_upmap,
    gate_up_column_norm,
    frozen_down_weight,
    down_adapter_downmap,
    down_adapter_upmap,
    down_column_norm,
):
    length = tokens.shape[0]
    members, groups = lax.axis_size("blk"), lax.axis_size("dp")
    me, line = lax.axis_index("blk"), lax.axis_index("dp")
    count = length * members
    mates = members // QUAD
    wide = frozen_output_weight.shape[1]
    heads = wide // HDIM
    hidden = frozen_gate_up_weight.shape[2]
    lens_row = document_length_list[0]
    rank = ADAPTER_RANK
    flip = lambda a: jnp.swapaxes(a, -1, -2)

    def home(array, axis, width, who=None):
        return lax.dynamic_slice_in_dim(array, (me if who is None else who) * width, width, axis)

    def by_head(array):
        split = array.reshape(3, array.shape[1], heads, HDIM)
        return jnp.transpose(split, (1, 2, 0, 3)).reshape(array.shape[1], 3 * wide)

    def by_three(array):
        split = array.reshape(array.shape[0], heads, 3, HDIM)
        return jnp.transpose(split, (2, 0, 1, 3)).reshape(3, array.shape[0], wide)

    x_full = tokens.astype(f32)
    normed_one, inverse_one = normalize(x_full, attention_norm_gain)
    h_one = normed_one.astype(bf16)
    h_all = lax.all_gather(h_one, "blk", axis=0, tiled=True)

    w_out, n_out = merge(
        after(frozen_output_weight, h_one)[None],
        flip(output_adapter_downmap)[None],
        home(output_adapter_upmap, 1, wide)[None],
        home(output_column_norm, 0, wide)[None],
    )
    gu, n_gu = merge_rows(
        flip(frozen_gate_up_weight),
        flip(gate_up_adapter_downmap),
        home(gate_up_adapter_upmap, 2, hidden),
        home(gate_up_column_norm, 1, hidden)[:, :, None],
        mates,
    )
    b_qkv = home(query_key_value_upmap, 2, wide)
    m_qkv = by_head(home(query_key_value_norm, 1, wide)[:, None, :])
    w_qkv, n_qkv = merge(frozen_query_key_value, flip(query_key_value_downmap), b_qkv, m_qkv)
    w_down, n_down = merge(
        frozen_down_weight[None],
        flip(down_adapter_downmap)[None],
        home(down_adapter_upmap, 1, wide)[None],
        home(down_column_norm, 0, wide)[None],
    )
    places, begins, end = begins_of(lens_row, count)
    half = HDIM // 2
    freq = rope_base ** (-(jnp.arange(half, dtype=f32) * 2.0 / HDIM))
    angle = (places - begins).astype(f32)[:, None] * freq[None, :]
    cosine, sine = jnp.cos(angle), jnp.sin(angle)
    cosine = jnp.concatenate([cosine, cosine], axis=1)
    sine = jnp.concatenate([-sine, sine], axis=1)
    begin = begins[None, :]
    valid = (me * length + jnp.arange(length, dtype=jnp.int32)) < end
    d_final = cotangent.astype(f32) * valid.astype(f32)[:, None]
    d_final_low = d_final.astype(bf16)

    def spread_rows(chunks):
        got = lax.all_to_all(chunks, "blk", 0, 0, tiled=True)
        return jnp.transpose(got, (1, 0, 2)).reshape(chunks.shape[1], members * wide)

    def spread_rows(chunks):
        got = lax.all_to_all(chunks, "blk", 0, 0, tiled=True)
        return jnp.transpose(got, (1, 0, 2)).reshape(chunks.shape[1], members * wide)

    w_out, gu = after((w_out, gu), w_qkv, w_down, cosine, sine)
    piece = MODEL_WIDTH // (2 * groups)
    core = me % 2
    pair = lax.dynamic_slice_in_dim(w_out, 2 * line * piece, 2 * piece, 0)
    pair = pair.reshape(1, 2, piece, wide)
    mine = spread_rows(jnp.tile(pair, (members // 2, 1, 1, 1)).reshape(members, piece, wide))
    mine = dp_steps(dp_start(mine), 0, 1)
    piece = mates * hidden // groups
    per_shard = groups // mates
    turn = line // per_shard
    shards = lax.dynamic_slice_in_dim(
        after(w_down, w_out).reshape(mates, QUAD, hidden, wide),
        (line % per_shard) * piece,
        piece,
        2,
    )
    chosen = jnp.stack(
        [
            functools.reduce(
                lambda rest, k: jnp.where(turn == k, shards[q ^ k], rest),
                range(1, mates),
                shards[q],
            )
            for q in range(mates)
        ]
    ).reshape(members, piece, wide)
    own = jnp.concatenate([n_out[0], n_gu[0, :, 0], n_gu[1, :, 0], n_down[0]])
    own = jnp.pad(own, (0, -own.shape[0] % wide)).reshape(-1, wide)
    own_high = lax.reduce_precision(own, 8, 7)
    riders = jnp.concatenate([own_high, own - own_high], axis=0).astype(bf16)
    extra = -riders.shape[0] % 16
    riders = jnp.pad(riders, ((0, extra), (0, 0)))
    riders = jnp.broadcast_to(riders[None], (members, *riders.shape))
    rows_down = spread_rows(jnp.concatenate([chosen, riders], axis=1))
    norm_rows = rows_down[piece:].astype(f32)
    norms = norm_rows[: own.shape[0]] + norm_rows[own.shape[0] : 2 * own.shape[0]]
    norms = jnp.transpose(norms.reshape(own.shape[0], members, wide), (1, 0, 2))
    norms = norms.reshape(members, own.shape[0] * wide)
    rows_down = rows_down[:piece]
    piece_gu = hidden // groups
    gu_part = lax.dynamic_slice(
        gu, (0, 0, line * piece_gu, 0), (1, 2, piece_gu, MODEL_WIDTH)
    ).reshape(2, piece_gu, MODEL_WIDTH)
    gate_part = after(gu_part[0], rows_down)
    gate_parts = [swap(gate_part, "blk", QUAD * k) for k in range(1, mates)]
    h_all, d_final_low, mine, rows_down = after((h_all, d_final_low, mine, rows_down), cosine)

    mine = dp_last(dp_steps(mine, 1, -1))
    down_rows = lax.all_gather(rows_down, "dp", axis=0, tiled=True)
    triple = dot(h_all, w_qkv)
    q, k, v, attended_heads, mixed_t, lse = attention_forward(triple, cosine, sine, begin)


    attended_heads = after(attended_heads, mine, gate_parts)
    mine, d_final_low, gate_parts = after((mine, d_final_low, gate_parts), attended_heads)
    over = swap(mine, "blk", 1)
    up_part = after(gu_part[1], attended_heads)
    up_parts = [swap(up_part, "blk", QUAD * k) for k in range(1, mates)]
    gate_states = [dp_steps(dp_start(g), 0, 1) for g in gate_parts]
    out_full = blank((groups, 2, MODEL_WIDTH // (2 * groups), MODEL_WIDTH), bf16)
    out_full = dp_lay(mine, out_full, core)
    out_full = dp_lay(over, out_full, 1 - core).reshape(MODEL_WIDTH, MODEL_WIDTH)
    attended = lax.all_to_all(
        attended_heads.reshape(members, length, wide), "blk", 0, 0, tiled=True
    )
    a_low = flip(query_key_value_downmap).astype(bf16).reshape(3 * rank, MODEL_WIDTH)
    h_all_late = after(h_all, attended_heads)
    xa_qkv = dot(a_low, h_all_late, NT).astype(bf16)
    chips = members // 2
    xa_qkv = jnp.transpose(xa_qkv.reshape(3 * rank, chips, 2 * length), (1, 0, 2))
    aw_qkv = dot(a_low, w_qkv)
    row = lax.broadcasted_iota(jnp.int32, (3 * rank, 3 * wide), 0) // rank
    column = (lax.broadcasted_iota(jnp.int32, (3 * rank, 3 * wide), 1) // HDIM) % 3
    own_block = row == column
    spread_qkv = jnp.where(own_block, jnp.tile(by_head(b_qkv), (3, 1)), 0.0)
    attended = after(
        attended, xa_qkv, aw_qkv, spread_qkv, out_full, gate_states, up_parts
    )

    attended = jnp.transpose(attended, (1, 0, 2)).reshape(length, MODEL_WIDTH)
    a_out_low = flip(output_adapter_downmap).astype(bf16)
    y_out = dot(jnp.concatenate([attended, a_out_low], axis=0), out_full)
    y_out, aw_out = y_out[:length], y_out[length:]
    residual = x_full + y_out
    normed_two, inverse_two = normalize(residual, feedforward_norm_gain)
    h_two = normed_two.astype(bf16)
    up_parts, d_final_low, gate_states = after((up_parts, d_final_low, gate_states), attended)
    gate_states = [dp_last(dp_steps(state, 1, -1)) for state in gate_states]
    d_final_pair = jnp.concatenate([d_final_low, swap(d_final_low, "blk", 2)], axis=0)
    up_states = [dp_steps(dp_start(g), 0, 1) for g in up_parts]
    h_two = after(h_two, up_states, d_final_pair)

    attended_late = after(attended, h_two)
    xa_out = dot(a_out_low, attended_late, NT).astype(bf16)
    up_states = [dp_last(dp_steps(after(state, h_two), 1, -1)) for state in up_states]
    d_final_pair = after(d_final_pair, h_two)
    d_final_all = jnp.concatenate([d_final_pair, swap(d_final_pair, "blk", 1)], axis=0)
    for k_ in range(1, mates):
        gu = dp_lay(gate_states[k_ - 1], gu, (k_, 0))
        gu = dp_lay(up_states[k_ - 1], gu, (k_, 1))
    gu = gu.reshape(mates * 2 * hidden, MODEL_WIDTH)
    a_gu_low = flip(gate_up_adapter_downmap).astype(bf16).reshape(2 * rank, MODEL_WIDTH)
    norms_out = norms[:, :wide].reshape(-1)
    norms_down = norms[:, wide + 2 * hidden : 2 * wide + 2 * hidden].reshape(-1)

    h_two_all = after(quad_gather(h_two), xa_out, gu, down_rows)
    acts, g_gu, gm_gu = feed_forward(gu, down_rows, h_two_all, d_final_all, mates)
    dh_parts = dot(g_gu, gu, TN).astype(bf16)
    dh_half = quad_halve(dh_parts)
    dh_two = quad_finish(dh_half)

    acts_late, down_late, h_two_late, gu_late = after(
        (acts, down_rows, h_two_all, gu), dh_half
    )
    y_parts = dot(acts_late, down_late, TN).astype(bf16)
    a_down_low = flip(down_adapter_downmap).astype(bf16)
    order = [me ^ (QUAD * k_) for k_ in range(mates)]
    low = jnp.concatenate([home(a_down_low, 1, hidden, who) for who in order], axis=1)
    xa_down = dot(low, acts_late).astype(bf16)
    aw_down = dot(low, down_late)
    xa_gu = dot(a_gu_low, h_two_late, NT).astype(bf16)
    aw_gu = dot(a_gu_low, gu_late, NT)
    dh_two = after(dh_two, y_parts, xa_down, aw_down, xa_gu, aw_gu)

    d_norm_two = normalize_back(residual, inverse_two, feedforward_norm_gain, dh_two)
    d_residual = d_final + d_norm_two
    g_out = d_residual.astype(bf16)
    d_attended = dot(g_out, out_full, NT).astype(bf16)
    d_parts = jnp.transpose(d_attended.reshape(length, members, wide), (1, 0, 2))
    d_heads = lax.all_to_all(d_parts, "blk", 0, 0, tiled=True).reshape(count, wide)

    y_down = quad_finish(quad_halve(after(y_parts, d_parts)))
    result = (residual + y_down).astype(bf16)
    g_late, h_two_late, gu_late, gm_gu = after((g_gu, h_two_all, gu, gm_gu), d_parts)

    def joined(pick):
        return jnp.concatenate([pick(who, i) for who in order for i in range(2)], axis=-1)

    m_gu = joined(lambda who, i: home(gate_up_column_norm[i], 0, hidden, who))
    n_gu_all = joined(
        lambda who, i: lax.dynamic_slice(norms, (who, wide + i * hidden), (1, hidden))[0]
    )
    b_gu = joined(lambda who, i: home(gate_up_adapter_upmap[i], 1, hidden, who))
    s_gu = m_gu / n_gu_all
    gm_gu = gm_gu.reshape(-1) / m_gu
    row = lax.broadcasted_iota(jnp.int32, (2 * rank, b_gu.shape[1]), 0) // rank
    column = (lax.broadcasted_iota(jnp.int32, (2 * rank, b_gu.shape[1]), 1) // hidden) % 2
    own_gu = row == column
    spread = jnp.where(own_gu, jnp.tile(b_gu, (2, 1)), 0.0)
    p_gu = dot((spread * s_gu).astype(bf16), g_late).astype(bf16)
    tilt = (spread * (gm_gu / n_gu_all)).astype(bf16)
    gb_gu = adapter_scale * (dot(xa_gu, g_late, NT) * s_gu - aw_gu * (gm_gu / n_gu_all))
    gb_gu = jnp.sum(jnp.where(own_gu, gb_gu, 0.0).reshape(2, rank, -1), axis=0)
    d_heads = after(d_heads, p_gu, tilt, gb_gu)

    g_three, gm_heads = attention_backward(
        q, k, v, triple, cosine, sine, begin, d_heads, mixed_t, lse
    )
    gm_down = jnp.sum(d_final_low.astype(f32) * y_down, axis=0) / down_column_norm
    g_three = after(g_three, gm_down)
    own_rows, other_rows, grad_a, grad_b, grad_g_attn, gm = back_qkv(
        g_three, h_all, w_qkv, spread_qkv, m_qkv, n_qkv, gm_heads, xa_qkv, aw_qkv
    )
    gm_quad = gm_down + swap(gm_down, "blk", 1)
    total = (own_rows.astype(f32) + swap(other_rows, "blk", 1).astype(f32)).astype(bf16)
    total, gm_quad = after((total, gm_quad))
    state = chips_step(total, 1, None)
    gm_quad = gm_quad + swap(gm_quad, "blk", 2)
    acts_late, d_final_late, dh_late, unit_two, g_out, out_late = after(
        (acts, d_final_all, dh_two, residual * inverse_two, g_out, out_full), gm_quad
    )
    grad_g_ffn = jnp.sum(dh_late * unit_two, axis=0)
    gm_out = jnp.sum(g_out.astype(f32) * y_out, axis=0) / output_column_norm
    s_out = output_column_norm / norms_out
    p_out = dot((output_adapter_upmap * s_out).astype(bf16), g_out, NT).astype(bf16)
    tilt_out = (output_adapter_upmap * (gm_out / norms_out)).astype(bf16)
    ga_out = adapter_scale * (dot(p_out, attended) - dot(tilt_out, out_late, NT))
    gb_out = adapter_scale * (dot(xa_out, g_out) * s_out - aw_out * (gm_out / norms_out))
    s_down = down_column_norm / norms_down
    p_down = dot((down_adapter_upmap * s_down).astype(bf16), d_final_late, NT).astype(bf16)
    state = after(state, ga_out, gb_out, grad_g_ffn, p_down, gm_quad)

    gm_quad, p_down, p_gu, tilt = after((gm_quad, p_down, p_gu, tilt), state)
    ga_gu = adapter_scale * (dot(p_gu, h_two_late) - dot(tilt, gu_late))
    tilt_down = (down_adapter_upmap * (gm_quad / norms_down)).astype(bf16)
    ga_down = adapter_scale * (dot(p_down, acts_late, NT) - dot(tilt_down, down_rows, NT))
    gb_down = adapter_scale * (
        dot(xa_down, d_final_late) * s_down - aw_down * (gm_quad / norms_down)
    )
    room = -hidden % 128
    place = jnp.stack(order)[:, None] == jnp.arange(members)[None, :]

    def spread_shards(array):
        array = jnp.pad(array, [(0, 0)] * (array.ndim - 1) + [(0, room)])
        return sum(
            jnp.where(place[k_][:, None], array[..., k_, None, :], 0.0) for k_ in range(mates)
        )

    gb_both = jnp.swapaxes(gb_gu.reshape(rank, mates, 2, hidden), 1, 2)
    tall = jnp.stack([gb_both[:, 0], gb_both[:, 1], ga_down.reshape(rank, mates, hidden)])
    tall = spread_shards(tall).reshape(3, rank, -1)
    thin = spread_shards(jnp.swapaxes(gm_gu.reshape(mates, 2, hidden), 0, 1)).reshape(2, -1)
    grad_b = jnp.sum(jnp.where(own_block, grad_b, 0.0).reshape(3, rank, 3 * wide), axis=0)
    mine_only = jnp.arange(members)[:, None] == me
    b_all = jnp.where(mine_only, by_three(adapter_scale * grad_b)[:, :, None, :], 0.0)
    b_all = b_all.reshape(3, rank, MODEL_WIDTH)
    m_all = jnp.where(mine_only, by_three(gm)[:, 0][:, None, :], 0.0).reshape(3, MODEL_WIDTH)
    grad_g_attn = grad_g_attn[0] / attention_norm_gain
    grad_a = adapter_scale * grad_a
    tables = (
        [grad_a[i * rank : (i + 1) * rank] for i in range(3)]
        + [b_all[i] for i in range(3)]
        + [ga_out, gb_out, ga_gu[:rank], ga_gu[rank:], gb_down]
        + [tall[0], tall[1], tall[2]]
    )
    vectors = [grad_g_attn, grad_g_ffn, gm_out, gm_down, m_all[0], m_all[1], m_all[2]]
    vectors += [thin[0], thin[1]]
    packed = packed_up(tables, vectors)
    for t in range(2, chips - 1):
        state = chips_step(total, t, state)
    ends = {}

    def between(buffer, stage):
        if stage == 0:
            ends[1] = after(state, buffer)
        if stage == 1:
            buffer = after(buffer, ends[1])
        if stage == 3:
            ends[0] = chips_step(total, chips - 1, after(ends[1], buffer))
        return buffer

    tables, vectors = unpacked(total_sum(packed, between), tables, vectors)
    d_norm_one = normalize_back(
        x_full, inverse_one, attention_norm_gain, chips_end(total, ends[0])
    )
    grad_input = d_residual + d_norm_one
    dense = lambda array: array.reshape(-1, members, hidden + room)[:, :, :hidden].reshape(
        array.shape[:-1] + (members * hidden,)
    )
    a_out, b_out, a_gate, a_up, b_down = tables[6:11]
    b_gate, b_up, a_down = [dense(t) for t in tables[11:]]
    return (
        result,
        grad_input,
        vectors[0],
        vectors[1],
        flip(jnp.stack(tables[:3])),
        jnp.stack(tables[3:6]),
        jnp.stack(vectors[4:7]),
        flip(a_out),
        b_out,
        vectors[2],
        flip(jnp.stack([a_gate, a_up])),
        jnp.stack([b_gate, b_up]),
        jnp.stack([dense(v) for v in vectors[7:]]),
        flip(a_down),
        b_down,
        vectors[3],
    )


def solution(mesh):
    rows, none = P(("dp", "blk"), None), P()
    in_specs = (
        rows,
        rows,
        P("dp", None),
        none,
        none,
        P(None, None, "blk"),
        none,
        none,
        none,
        P(None, "blk"),
        none,
        none,
        none,
        P(None, None, "blk"),
        none,
        none,
        none,
        P(None, "blk"),
        none,
        none,
        none,
    )
    out_specs = (rows, rows) + (none,) * 14
    return jax.shard_map(
        per_device, mesh=mesh, in_specs=in_specs, out_specs=out_specs, check_vma=False
    )
```

```python
import functools

import jax
import jax.numpy as jnp
from jax import lax
from jax.experimental import pallas as pl
from jax.experimental.pallas import tpu as pltpu
from jax.sharding import PartitionSpec as P

MODEL_WIDTH = 2048
HEADS = 16
ADAPTER_RANK = 16
ALPHA = 32
HDIM = 128
TILE = 256
QUAD = 4

norm_eps = 1e-05
column_eps = 1e-06
rope_base = 10000.0
far_negative = -1e30
log2_e = 1.4426950408889634
adapter_scale = ALPHA / ADAPTER_RANK
bf16 = jnp.bfloat16
f32 = jnp.float32
NT = (((1,), (1,)), ((), ()))
TN = (((0,), (0,)), ((), ()))
NN = (((1,), (0,)), ((), ()))


def dot(a, b, dims=NN):
    return lax.dot_general(a, b, dims, preferred_element_type=f32)


def after(array, *earlier):
    return lax.optimization_barrier((array, *earlier))[0]


def blank(shape, dtype):
    return pl.pallas_call(
        lambda out: None,
        out_shape=jax.ShapeDtypeStruct(shape, dtype),
        out_specs=pl.BlockSpec(memory_space=pl.ANY),
        name="blank",
    )()


def swap(array, axis, bit):
    return lax.ppermute(array, axis, [(i, i ^ bit) for i in range(lax.axis_size(axis))])


def axis_sum(array, axis):
    bit = 1
    while bit < lax.axis_size(axis):
        array = array + swap(array, axis, bit)
        bit *= 2
    return array


def begins_of(lens_row, count):
    places = jnp.arange(count, dtype=jnp.int32)
    ends = jnp.cumsum(lens_row, dtype=jnp.int32)
    after = (places[:, None] >= ends[None, :]).astype(jnp.int32)
    return places, jnp.sum(after * lens_row[None, :], axis=1, dtype=jnp.int32), ends[-1]


def split_three(a):
    one = lax.reduce_precision(a, 8, 7)
    rest = a - one
    two = lax.reduce_precision(rest, 8, 7)
    return one.astype(bf16), two.astype(bf16), (rest - two).astype(bf16)


def parts_of(a, b):
    a1, a2, a3 = split_three(a * adapter_scale)
    b1, b2, b3 = split_three(b)
    return (
        jnp.concatenate([a1, a1, a2, a1, a2, a3], axis=-2),
        jnp.concatenate([b1, b2, b1, b3, b2, b1], axis=-2),
    )


def merge_kernel(w_ref, a_ref, b_ref, m_ref, out_ref, n_ref, v_ref):
    rows = w_ref.shape[1]

    def add(i, acc):
        at = pl.ds(pl.multiple_of(i * TILE, TILE), TILE)
        v = w_ref[0, at, :].astype(f32) + dot(a_ref[0, :, at], b_ref[0], TN)
        v_ref[at, :] = v
        return acc + jnp.sum(v * v, axis=0, keepdims=True)

    total = lax.fori_loop(0, rows // TILE, add, jnp.zeros(m_ref.shape, f32), unroll=2)
    norms = jnp.sqrt(total + column_eps)
    n_ref[...] = norms
    s = m_ref[...] / norms

    def put(i, carry):
        at = pl.ds(pl.multiple_of(i * TILE, TILE), TILE)
        out_ref[at, :] = (v_ref[at, :] * s).astype(bf16)
        return carry

    lax.fori_loop(0, rows // TILE, put, 0, unroll=2)


def merge(w, a, b, m):
    k, rows, cols = w.shape
    a_cat, b_cat = parts_of(a, b)
    wide = a_cat.shape[1]
    place = lambda i, h: (0, h * k + i)
    return pl.pallas_call(
        merge_kernel,
        grid=(k, cols // HDIM),
        in_specs=[
            pl.BlockSpec((1, rows, HDIM), lambda i, h: (i, 0, h)),
            pl.BlockSpec((1, wide, rows), lambda i, h: (i, 0, 0)),
            pl.BlockSpec((1, wide, HDIM), lambda i, h: (i, 0, h)),
            pl.BlockSpec((1, HDIM), place),
        ],
        out_specs=[pl.BlockSpec((rows, HDIM), place), pl.BlockSpec((1, HDIM), place)],
        out_shape=[
            jax.ShapeDtypeStruct((rows, k * cols), bf16),
            jax.ShapeDtypeStruct((1, k * cols), f32),
        ],
        scratch_shapes=[pltpu.VMEM((rows, HDIM), f32)],
        compiler_params=pltpu.CompilerParams(vmem_limit_bytes=48 * 2**20),
        cost_estimate=pl.CostEstimate(
            flops=2 * k * rows * cols * wide, bytes_accessed=4 * k * rows * cols, transcendentals=0
        ),
        name="merge",
    )(w, a_cat, b_cat, m)


def merge_rows_kernel(w_ref, a_ref, b_ref, m_ref, out_ref, n_ref):
    out_ref = out_ref.at[0]
    v = w_ref[0].astype(f32) + dot(b_ref[0], a_ref[0], TN)
    norms = jnp.sqrt(jnp.sum(v * v, axis=1, keepdims=True) + column_eps)
    n_ref[0] = norms
    out_ref[0] = (v * (m_ref[0] / norms)).astype(bf16)


def merge_rows(w, a, b, m, mates):
    k, cols, rows = w.shape
    a_cat, b_cat = parts_of(a, b)
    wide = a_cat.shape[1]
    return pl.pallas_call(
        merge_rows_kernel,
        grid=(k,),
        in_specs=[
            pl.BlockSpec((1, cols, rows), lambda i: (i, 0, 0)),
            pl.BlockSpec((1, wide, rows), lambda i: (i, 0, 0)),
            pl.BlockSpec((1, wide, cols), lambda i: (i, 0, 0)),
            pl.BlockSpec((1, cols, 1), lambda i: (i, 0, 0)),
        ],
        out_specs=[
            pl.BlockSpec((1, 1, cols, rows), lambda i: (0, i, 0, 0)),
            pl.BlockSpec((1, cols, 1), lambda i: (i, 0, 0)),
        ],
        out_shape=[
            jax.ShapeDtypeStruct((mates, k, cols, rows), bf16),
            jax.ShapeDtypeStruct((k, cols, 1), f32),
        ],
        compiler_params=pltpu.CompilerParams(vmem_limit_bytes=56 * 2**20),
        cost_estimate=pl.CostEstimate(
            flops=2 * k * rows * cols * wide, bytes_accessed=4 * k * rows * cols, transcendentals=0
        ),
        name="merge_rows",
    )(w, a_cat, b_cat, m)


def turned(u, cosine, sine):
    return u * cosine + pltpu.roll(u, HDIM // 2, 1) * sine


def forward_kernel(
    pre, cosine, sine, begin, q_out, k_out, v_out, att_out, mixed_t, lse_out, v_t
):
    count = pre.shape[0]
    scale = HDIM**-0.5 * log2_e
    for i in range(count // TILE):
        at = pl.ds(i * TILE, TILE)
        cos, sin = cosine[at, :], sine[at, :]
        q_out[at, :] = turned(pre[at, :HDIM], cos, sin).astype(bf16)
        k_out[at, :] = turned(pre[at, HDIM : 2 * HDIM], cos, sin).astype(bf16)
        v = pre[at, 2 * HDIM :]
        v_out[at, :] = v.astype(bf16)
        v_t[:, at] = v.T.astype(bf16)
    for i in range(count // TILE):
        rows = pl.ds(i * TILE, TILE)
        q = q_out[rows, :]
        start = begin[:, rows]

        def visit(j, state, diagonal):
            top, total, mixed = state
            keys = pl.ds(pl.multiple_of(j * TILE, TILE), TILE)
            s = dot(k_out[keys, :], q, NT) * scale
            place = j * TILE + lax.broadcasted_iota(jnp.int32, (TILE, TILE), 0)
            allowed = place >= start
            if diagonal:
                mine = i * TILE + lax.broadcasted_iota(jnp.int32, (TILE, TILE), 1)
                allowed = allowed & (place <= mine)
            s = jnp.where(allowed, s, far_negative)
            high = jnp.maximum(top, jnp.max(s, axis=0, keepdims=True))
            keep = jnp.exp2(top - high)
            p = jnp.exp2(s - high)
            total = total * keep + jnp.sum(p, axis=0, keepdims=True)
            mixed = mixed * keep + dot(v_t[:, keys], p.astype(bf16))
            return high, total, mixed

        state = (
            jnp.full((1, TILE), far_negative, f32),
            jnp.zeros((1, TILE), f32),
            jnp.zeros((HDIM, TILE), f32),
        )
        state = visit(i, state, True)
        for j in range(i):
            state = visit(j, state, False)
        top, total, mixed = state
        mixed = mixed / total
        mixed_t[:, rows] = mixed
        att_out[rows, :] = mixed.T.astype(bf16)
        lse_out[0, :, rows] = top + jnp.log2(total)


def backward_kernel(
    q_ref, k_ref, v_ref, pre, cosine, sine, begin, grad_att, mixed_t, lse,
    g_out, gm_out, dk, dv, k_t,
):
    count = q_ref.shape[0]
    scale = HDIM**-0.5
    dk[...] = jnp.zeros_like(dk)
    dv[...] = jnp.zeros_like(dv)
    for i in range(count // TILE):
        at = pl.ds(i * TILE, TILE)
        k_t[:, at] = k_ref[at, :].astype(f32).T.astype(bf16)
    gm_q = jnp.zeros((1, HDIM), f32)
    for i in range(count // TILE):
        rows = pl.ds(i * TILE, TILE)
        q = q_ref[rows, :]
        d_mixed = grad_att[rows, :]
        delta = jnp.sum(d_mixed.astype(f32).T * mixed_t[:, rows], axis=0, keepdims=True)
        start = begin[:, rows]
        high = lse[0, :, rows]
        dq_t = jnp.zeros((HDIM, TILE), f32)
        for j in range(i + 1):
            keys = pl.ds(j * TILE, TILE)
            s = dot(k_ref[keys, :], q, NT) * (scale * log2_e)
            place = j * TILE + lax.broadcasted_iota(jnp.int32, (TILE, TILE), 0)
            allowed = place >= start
            if j == i:
                mine = i * TILE + lax.broadcasted_iota(jnp.int32, (TILE, TILE), 1)
                allowed = allowed & (place <= mine)
            p = jnp.where(allowed, jnp.exp2(s - high), 0.0)
            dp = dot(v_ref[keys, :], d_mixed, NT)
            ds = (p * (dp - delta)).astype(bf16)
            dv[keys, :] += dot(p.astype(bf16), d_mixed)
            dk[keys, :] += dot(ds, q)
            dq_t = dq_t + dot(k_t[:, keys], ds)
        gq = turned(dq_t.T * scale, cosine[rows, :], -sine[rows, :]).astype(bf16)
        g_out[rows, :HDIM] = gq
        gm_q = gm_q + jnp.sum(gq.astype(f32) * pre[rows, :HDIM], axis=0, keepdims=True)
    gm_k = jnp.zeros((1, HDIM), f32)
    gm_v = jnp.zeros((1, HDIM), f32)
    for i in range(count // TILE):
        at = pl.ds(i * TILE, TILE)
        gk = turned(dk[at, :] * scale, cosine[at, :], -sine[at, :]).astype(bf16)
        g_out[at, HDIM : 2 * HDIM] = gk
        gm_k = gm_k + jnp.sum(gk.astype(f32) * pre[at, HDIM : 2 * HDIM], axis=0, keepdims=True)
        gv = dv[at, :].astype(bf16)
        g_out[at, 2 * HDIM :] = gv
        gm_v = gm_v + jnp.sum(gv.astype(f32) * pre[at, 2 * HDIM :], axis=0, keepdims=True)
    gm_out[0:1, :HDIM] = gm_q
    gm_out[0:1, HDIM : 2 * HDIM] = gm_k
    gm_out[0:1, 2 * HDIM :] = gm_v


def attention_forward(triple, cosine, sine, begin):
    count, width = triple.shape[0], triple.shape[1] // 3
    heads = width // HDIM
    whole = lambda h: (0, 0)
    head = lambda h: (0, h)
    tall = lambda at: pl.BlockSpec((count, HDIM), at)
    return pl.pallas_call(
        forward_kernel,
        grid=(heads,),
        in_specs=[
            pl.BlockSpec((count, 3 * HDIM), head),
            tall(whole),
            tall(whole),
            pl.BlockSpec((1, count), whole),
        ],
        out_specs=[
            tall(head),
            tall(head),
            tall(head),
            tall(head),
            pl.BlockSpec((HDIM, count), lambda h: (h, 0)),
            pl.BlockSpec((1, 1, count), lambda h: (h, 0, 0)),
        ],
        out_shape=[jax.ShapeDtypeStruct((count, width), bf16)] * 4
        + [
            jax.ShapeDtypeStruct((width, count), f32),
            jax.ShapeDtypeStruct((heads, 1, count), f32),
        ],
        scratch_shapes=[pltpu.VMEM((HDIM, count), bf16)],
        compiler_params=pltpu.CompilerParams(vmem_limit_bytes=48 * 2**20),
        cost_estimate=pl.CostEstimate(
            flops=2 * count * count * width, bytes_accessed=30 * count * width, transcendentals=0
        ),
        name="attend",
    )(triple, cosine, sine, begin)


def attention_backward(q, k, v, triple, cosine, sine, begin, grad_att, mixed_t, lse):
    count, width = q.shape
    heads = width // HDIM
    whole = lambda h: (0, 0)
    head = lambda h: (0, h)
    tall = lambda at: pl.BlockSpec((count, HDIM), at)
    return pl.pallas_call(
        backward_kernel,
        grid=(heads,),
        in_specs=[
            tall(head),
            tall(head),
            tall(head),
            pl.BlockSpec((count, 3 * HDIM), head),
            tall(whole),
            tall(whole),
            pl.BlockSpec((1, count), whole),
            tall(head),
            pl.BlockSpec((HDIM, count), lambda h: (h, 0)),
            pl.BlockSpec((1, 1, count), lambda h: (h, 0, 0)),
        ],
        out_specs=[pl.BlockSpec((count, 3 * HDIM), head), pl.BlockSpec((8, 3 * HDIM), head)],
        out_shape=[
            jax.ShapeDtypeStruct((count, 3 * width), bf16),
            jax.ShapeDtypeStruct((8, 3 * width), f32),
        ],
        scratch_shapes=[
            pltpu.VMEM((count, HDIM), f32),
            pltpu.VMEM((count, HDIM), f32),
            pltpu.VMEM((HDIM, count), bf16),
        ],
        compiler_params=pltpu.CompilerParams(vmem_limit_bytes=48 * 2**20),
        cost_estimate=pl.CostEstimate(
            flops=5 * count * count * width, bytes_accessed=40 * count * width, transcendentals=0
        ),
        name="attend_back",
    )(q, k, v, triple, cosine, sine, begin, grad_att, mixed_t, lse)


def feed_kernel(
    gu_ref, down_ref, h_pair, h_other, d_pair, d_other, acts_out, g_out, gm_out, h_ref, d_ref
):
    half = h_pair.shape[0]

    @pl.when((pl.program_id(0) == 0) & (pl.program_id(1) == 0))
    def _():
        h_ref[:half] = h_pair[...]
        h_ref[half:] = h_other[...]
        d_ref[:half] = d_pair[...]
        d_ref[half:] = d_other[...]

    h = h_ref[...]
    gate = dot(gu_ref[0, 0], h, NT)
    upward = dot(gu_ref[0, 1], h, NT)
    d_act = dot(down_ref[...], d_ref[...], NT)
    sigmoid_gate = jax.nn.sigmoid(gate)
    silu = gate * sigmoid_gate
    acts_out[...] = (silu * upward).astype(bf16)
    d_gate = (d_act * upward * sigmoid_gate * (1.0 + gate * (1.0 - sigmoid_gate))).astype(bf16)
    d_upward = (d_act * silu).astype(bf16)
    g_out[0, 0] = d_gate
    g_out[0, 1] = d_upward
    gm_out[0, 0] = jnp.sum(d_gate.astype(f32) * gate, axis=1, keepdims=True)
    gm_out[0, 1] = jnp.sum(d_upward.astype(f32) * upward, axis=1, keepdims=True)


def feed_forward(gu, down, h, d, mates):
    rows, width = 2 * h[0].shape[0], h[0].shape[1]
    hidden = down.shape[0] // mates
    unit = hidden // max(1, hidden // 352)
    steps = hidden // unit
    flat = lambda k, j: (k * steps + j, 0)
    deep = lambda k, j: (k, 0, j, 0)
    whole = lambda k, j: (0, 0)
    once = pl.BlockSpec((rows // 2, width), whole, pipeline_mode=pl.Buffered(1))
    acts, g, gm, h_all, d_all = pl.pallas_call(
        feed_kernel,
        grid=(mates, steps),
        in_specs=[
            pl.BlockSpec((1, 2, unit, width), deep),
            pl.BlockSpec((unit, width), flat),
            once,
            once,
            once,
            once,
        ],
        out_specs=[
            pl.BlockSpec((unit, rows), flat),
            pl.BlockSpec((1, 2, unit, rows), deep),
            pl.BlockSpec((1, 2, unit, 1), deep),
            pl.BlockSpec((rows, width), whole),
            pl.BlockSpec((rows, width), whole),
        ],
        out_shape=[
            jax.ShapeDtypeStruct((mates * hidden, rows), bf16),
            jax.ShapeDtypeStruct((mates, 2, hidden, rows), bf16),
            jax.ShapeDtypeStruct((mates, 2, hidden, 1), f32),
            jax.ShapeDtypeStruct((rows, width), bf16),
            jax.ShapeDtypeStruct((rows, width), bf16),
        ],
        compiler_params=pltpu.CompilerParams(vmem_limit_bytes=58 * 2**20),
        cost_estimate=pl.CostEstimate(
            flops=6 * mates * hidden * rows * width,
            bytes_accessed=6 * mates * hidden * width + 4 * rows * width,
            transcendentals=0,
        ),
        name="feed_forward",
    )(gu.reshape(mates, 2, hidden, width), down, *h, *d)
    return acts, g.reshape(2 * mates * hidden, rows), gm, h_all, d_all


def back_kernel(
    core, g_ref, h_ref, w_ref, spread, s_ref, over_n, sums, m_ref, xa_ref, aw_ref,
    own_out, other_out, ga_out, gb_out, gg_out, gm_out,
):
    step = pl.program_id(0)
    length = own_out.shape[1]
    g = g_ref[...]
    h = h_ref[...]
    s = s_ref[...]
    dh = dot(g, w_ref[...], NT)
    low = dh.astype(bf16)

    @pl.when(core[0] == 0)
    def _():
        own_out[0] = low[:length]
        other_out[0] = low[length:]

    @pl.when(core[0] != 0)
    def _():
        own_out[0] = low[length:]
        other_out[0] = low[:length]

    p = dot((spread[...] * s).astype(bf16), g, NT).astype(bf16)
    ga = dot(p, h)
    gb = dot(xa_ref[...], g)
    gg = jnp.sum(dh * h.astype(f32), axis=0, keepdims=True)

    @pl.when(step == 0)
    def _():
        gm = sums[0:1, :] / m_ref[...]
        gm_out[...] = gm
        tilt = (spread[...] * (gm * over_n[...])).astype(bf16)
        ga_out[...] = ga - dot(tilt, w_ref[...], NT)
        gb_out[...] = gb * s - aw_ref[...] * (gm * over_n[...])
        gg_out[...] = gg

    @pl.when(step > 0)
    def _():
        ga_out[...] += ga
        gb_out[...] += gb * s
        gg_out[...] += gg


def back_qkv(g, h, w, spread, m, n, sums, xa, aw):
    chips = lax.axis_size("blk") // 2
    core = (lax.axis_index("blk") % 2).astype(jnp.int32).reshape(1)
    count, cols = g.shape
    width = h.shape[1]
    pair = count // chips
    wide = spread.shape[0]
    rows = lambda i, core: (i, 0)
    whole = lambda i, core: (0, 0)
    deep = lambda i, core: (i, 0, 0)
    return pl.pallas_call(
        back_kernel,
        grid_spec=pltpu.PrefetchScalarGridSpec(
            num_scalar_prefetch=1,
            grid=(chips,),
            in_specs=[
                pl.BlockSpec((pair, cols), rows),
                pl.BlockSpec((pair, width), rows),
                pl.BlockSpec((width, cols), whole),
                pl.BlockSpec((wide, cols), whole),
                pl.BlockSpec((1, cols), whole),
                pl.BlockSpec((1, cols), whole),
                pl.BlockSpec((8, cols), whole),
                pl.BlockSpec((1, cols), whole),
                pl.BlockSpec((None, wide, pair), deep),
                pl.BlockSpec((wide, cols), whole),
            ],
            out_specs=[
                pl.BlockSpec((1, pair // 2, width), deep),
                pl.BlockSpec((1, pair // 2, width), deep),
                pl.BlockSpec((wide, width), whole),
                pl.BlockSpec((wide, cols), whole),
                pl.BlockSpec((1, width), whole),
                pl.BlockSpec((1, cols), whole),
            ],
        ),
        out_shape=[
            jax.ShapeDtypeStruct((chips, pair // 2, width), bf16),
            jax.ShapeDtypeStruct((chips, pair // 2, width), bf16),
            jax.ShapeDtypeStruct((wide, width), f32),
            jax.ShapeDtypeStruct((wide, cols), f32),
            jax.ShapeDtypeStruct((1, width), f32),
            jax.ShapeDtypeStruct((1, cols), f32),
        ],
        compiler_params=pltpu.CompilerParams(vmem_limit_bytes=56 * 2**20),
        cost_estimate=pl.CostEstimate(
            flops=3 * count * cols * width, bytes_accessed=8 * count * width, transcendentals=0
        ),
        name="back_qkv",
    )(core, g, h, w, spread, m / n, 1.0 / n, sums, m, xa, aw)


def normalize(values, gain):
    inverse = lax.rsqrt(jnp.mean(values * values, axis=-1, keepdims=True) + norm_eps)
    return (values * inverse * gain, inverse)


def normalize_back(values, inverse, gain, grad):
    unit = values * inverse
    scaled = grad * gain
    return inverse * (scaled - unit * jnp.mean(scaled * unit, axis=-1, keepdims=True))


def quad_halve(parts):
    half = parts.shape[0] // 2
    return parts[:half].astype(f32) + swap(parts[half:], "blk", 1).astype(f32)


def quad_finish(mine):
    half = mine.shape[0] // 2
    return mine[:half] + swap(mine[half:].astype(bf16), "blk", 2).astype(f32)


def step_chips(array, first, last, by):
    pairs = [(2 * i + c, 2 * (i + by) + c) for i in range(first, last + 1) for c in range(2)]
    return lax.ppermute(array, "blk", pairs)


def chips_step(total, t, state):
    chips = total.shape[0]
    chip = lax.axis_index("blk") // 2
    pick = lambda c: lax.dynamic_index_in_dim(
        total, jnp.clip(c, 0, chips - 1), 0, keepdims=False
    )
    up, down = pick(chips - t + chip), pick(t - chips + chip)
    if t > 1:
        up = (up.astype(f32) + state[0].astype(f32)).astype(bf16)
        down = (down.astype(f32) + state[1].astype(f32)).astype(bf16)
    up, down = after((up, down))
    return step_chips(up, 0, t - 1, 1), step_chips(down, chips - t, chips - 1, -1)


def chips_end(total, state):
    chip = lax.axis_index("blk") // 2
    own = lax.dynamic_index_in_dim(total, chip, 0, keepdims=False)
    return own.astype(f32) + state[0].astype(f32) + state[1].astype(f32)


def dp_start(piece):
    half = piece.shape[0] // 2
    return piece[None, :half], piece[None, half:]


def dp_steps(state, first=None, last=None):
    bits = [1 << i for i in range(lax.axis_size("dp").bit_length() - 1)]
    one, two = state
    for step in range(len(bits))[first:last]:
        one = jnp.concatenate([one, swap(one, "dp", bits[step])], axis=0)
        two = jnp.concatenate([two, swap(two, "dp", bits[::-1][step])], axis=0)
    return one, two


def dp_last(state):
    bits = [1 << i for i in range(lax.axis_size("dp").bit_length() - 1)]
    one, two = state
    return jnp.concatenate(
        [one, swap(one, "dp", bits[-1]), two, swap(two, "dp", bits[0])], axis=0
    )


def dp_places():
    groups = lax.axis_size("dp")
    bits = groups.bit_length() - 1
    who = jnp.arange(groups, dtype=jnp.int32) ^ lax.axis_index("dp")
    turned = sum(((who >> i) & 1) << (bits - 1 - i) for i in range(bits))
    return jnp.stack([who, turned + groups]).astype(jnp.int32)


def lay_kernel(places, one, two, into, out):
    place = out.at[0, 0] if len(out.shape) == 5 else out.at[0, 0, 0]
    place[0] = one[0]
    place[1] = two[0]


def dp_lay(state, into, at):
    groups, half, width = state.shape[0] // 2, state.shape[1], state.shape[2]
    shape = into.shape
    if isinstance(at, tuple):
        split = into.reshape(shape[0], shape[1], groups, 2, half, width)
        block = (1, 1, 1, 2, half, width)
        where = lambda c, places: (at[0], at[1], c, 0, 0, 0)
        second = jnp.zeros((1, groups), jnp.int32)
    else:
        split = into.reshape(groups, 2, 2, half, width)
        block = (1, 1, 2, half, width)
        where = lambda c, places: (c, places[2, c], 0, 0, 0)
        second = jnp.full((1, groups), at, jnp.int32)
    out = pl.pallas_call(
        lay_kernel,
        grid_spec=pltpu.PrefetchScalarGridSpec(
            num_scalar_prefetch=1,
            grid=(groups,),
            in_specs=[
                pl.BlockSpec((1, half, width), lambda c, places: (places[0, c], 0, 0)),
                pl.BlockSpec((1, half, width), lambda c, places: (places[1, c], 0, 0)),
                pl.BlockSpec(memory_space=pl.ANY),
            ],
            out_specs=pl.BlockSpec(block, where),
        ),
        out_shape=jax.ShapeDtypeStruct(split.shape, into.dtype),
        input_output_aliases={3: 0},
        name="lay",
    )(jnp.concatenate([dp_places(), second]), state, state, split)
    return out.reshape(shape)


def total_sum(buffer, between):
    stages = [("blk", 2, 1), ("dp", lax.axis_size("dp"), 1), ("blk", lax.axis_size("blk") // 2, 2)]
    for number, (axis, ways, unit) in enumerate(stages):
        part = buffer.shape[1] // ways
        mine = (lax.axis_index(axis) // unit) % ways
        cut = lambda d: lax.dynamic_slice_in_dim(buffer, (mine ^ d) * part, part, 1)
        arrived = [swap(cut(d), axis, d * unit) for d in range(1, ways)]
        buffer = between(functools.reduce(jnp.add, arrived, cut(0)), number)
    for number, (axis, ways, unit) in enumerate(stages[::-1]):
        part = buffer.shape[1]
        mine = (lax.axis_index(axis) // unit) % ways
        whole = blank((buffer.shape[0], ways * part), f32)
        for d in range(ways):
            piece = swap(buffer, axis, d * unit) if d else buffer
            whole = lax.dynamic_update_slice_in_dim(whole, piece, (mine ^ d) * part, 1)
        buffer = between(whole, 3 + number)
    return buffer


def packed_up(tables, vectors):
    devices = lax.axis_size("dp") * lax.axis_size("blk")
    joined = jnp.concatenate([*tables, *[v.reshape(16, -1) for v in vectors]], axis=1)
    return jnp.pad(joined, ((0, 0), (0, -joined.shape[1] % (128 * devices))))


def unpacked(joined, tables, vectors):
    out, at = [], 0
    for t in (*tables, *vectors):
        size = t.size // 16
        out.append(joined[:, at : at + size].reshape(t.shape))
        at += size
    return out[: len(tables)], out[len(tables) :]


def per_device(
    tokens,
    cotangent,
    document_length_list,
    attention_norm_gain,
    feedforward_norm_gain,
    frozen_query_key_value,
    query_key_value_downmap,
    query_key_value_upmap,
    query_key_value_norm,
    frozen_output_weight,
    output_adapter_downmap,
    output_adapter_upmap,
    output_column_norm,
    frozen_gate_up_weight,
    gate_up_adapter_downmap,
    gate_up_adapter_upmap,
    gate_up_column_norm,
    frozen_down_weight,
    down_adapter_downmap,
    down_adapter_upmap,
    down_column_norm,
):
    length = tokens.shape[0]
    members, groups = lax.axis_size("blk"), lax.axis_size("dp")
    me, line = lax.axis_index("blk"), lax.axis_index("dp")
    count = length * members
    mates = members // QUAD
    wide = frozen_output_weight.shape[1]
    heads = wide // HDIM
    hidden = frozen_gate_up_weight.shape[2]
    lens_row = document_length_list[0]
    rank = ADAPTER_RANK
    flip = lambda a: jnp.swapaxes(a, -1, -2)

    def home(array, axis, width, who=None):
        return lax.dynamic_slice_in_dim(array, (me if who is None else who) * width, width, axis)

    def by_head(array):
        split = array.reshape(3, array.shape[1], heads, HDIM)
        return jnp.transpose(split, (1, 2, 0, 3)).reshape(array.shape[1], 3 * wide)

    def by_three(array):
        split = array.reshape(array.shape[0], heads, 3, HDIM)
        return jnp.transpose(split, (2, 0, 1, 3)).reshape(3, array.shape[0], wide)

    x_full = tokens.astype(f32)
    normed_one, inverse_one = normalize(x_full, attention_norm_gain)
    h_one = normed_one.astype(bf16)
    h_all = lax.all_gather(h_one, "blk", axis=0, tiled=True)

    w_out, n_out = merge(
        after(frozen_output_weight, h_one)[None],
        flip(output_adapter_downmap)[None],
        home(output_adapter_upmap, 1, wide)[None],
        home(output_column_norm, 0, wide)[None],
    )
    gu, n_gu = merge_rows(
        flip(frozen_gate_up_weight),
        flip(gate_up_adapter_downmap),
        home(gate_up_adapter_upmap, 2, hidden),
        home(gate_up_column_norm, 1, hidden)[:, :, None],
        mates,
    )
    b_qkv = home(query_key_value_upmap, 2, wide)
    m_qkv = by_head(home(query_key_value_norm, 1, wide)[:, None, :])
    w_qkv, n_qkv = merge(frozen_query_key_value, flip(query_key_value_downmap), b_qkv, m_qkv)
    w_down, n_down = merge(
        frozen_down_weight[None],
        flip(down_adapter_downmap)[None],
        home(down_adapter_upmap, 1, wide)[None],
        home(down_column_norm, 0, wide)[None],
    )
    places, begins, end = begins_of(lens_row, count)
    half = HDIM // 2
    freq = rope_base ** (-(jnp.arange(half, dtype=f32) * 2.0 / HDIM))
    angle = (places - begins).astype(f32)[:, None] * freq[None, :]
    cosine, sine = jnp.cos(angle), jnp.sin(angle)
    cosine = jnp.concatenate([cosine, cosine], axis=1)
    sine = jnp.concatenate([-sine, sine], axis=1)
    begin = begins[None, :]
    valid = (me * length + jnp.arange(length, dtype=jnp.int32)) < end
    d_final = cotangent.astype(f32) * valid.astype(f32)[:, None]
    d_final_low = d_final.astype(bf16)

    def spread_rows(chunks):
        got = lax.all_to_all(chunks, "blk", 0, 0, tiled=True)
        return jnp.transpose(got, (1, 0, 2)).reshape(chunks.shape[1], members * wide)

    def spread_rows(chunks):
        got = lax.all_to_all(chunks, "blk", 0, 0, tiled=True)
        return jnp.transpose(got, (1, 0, 2)).reshape(chunks.shape[1], members * wide)

    w_out, gu = after((w_out, gu), w_qkv, w_down, cosine, sine)
    piece = MODEL_WIDTH // (2 * groups)
    core = me % 2
    pair = lax.dynamic_slice_in_dim(w_out, 2 * line * piece, 2 * piece, 0)
    pair = pair.reshape(1, 2, piece, wide)
    mine = spread_rows(jnp.tile(pair, (members // 2, 1, 1, 1)).reshape(members, piece, wide))
    mine = dp_steps(dp_start(mine), 0, 1)
    piece = mates * hidden // groups
    per_shard = groups // mates
    turn = line // per_shard
    shards = lax.dynamic_slice_in_dim(
        after(w_down, w_out).reshape(mates, QUAD, hidden, wide),
        (line % per_shard) * piece,
        piece,
        2,
    )
    chosen = jnp.stack(
        [
            functools.reduce(
                lambda rest, k: jnp.where(turn == k, shards[q ^ k], rest),
                range(1, mates),
                shards[q],
            )
            for q in range(mates)
        ]
    ).reshape(members, piece, wide)
    own = jnp.concatenate([n_out[0], n_gu[0, :, 0], n_gu[1, :, 0], n_down[0]])
    own = jnp.pad(own, (0, -own.shape[0] % wide)).reshape(-1, wide)
    own_high = lax.reduce_precision(own, 8, 7)
    riders = jnp.concatenate([own_high, own - own_high], axis=0).astype(bf16)
    extra = -riders.shape[0] % 16
    riders = jnp.pad(riders, ((0, extra), (0, 0)))
    riders = jnp.broadcast_to(riders[None], (members, *riders.shape))
    rows_down = spread_rows(jnp.concatenate([chosen, riders], axis=1))
    norm_rows = rows_down[piece:].astype(f32)
    norms = norm_rows[: own.shape[0]] + norm_rows[own.shape[0] : 2 * own.shape[0]]
    norms = jnp.transpose(norms.reshape(own.shape[0], members, wide), (1, 0, 2))
    norms = norms.reshape(members, own.shape[0] * wide)
    rows_down = rows_down[:piece]
    piece_gu = hidden // groups
    gu_part = lax.dynamic_slice(
        gu, (0, 0, line * piece_gu, 0), (1, 2, piece_gu, MODEL_WIDTH)
    ).reshape(2, piece_gu, MODEL_WIDTH)
    gate_part = after(gu_part[0], rows_down)
    gate_parts = [swap(gate_part, "blk", QUAD * k) for k in range(1, mates)]
    h_all, d_final_low, mine, rows_down = after((h_all, d_final_low, mine, rows_down), cosine)

    mine = dp_last(dp_steps(mine, 1, -1))
    down_rows = lax.all_gather(rows_down, "dp", axis=0, tiled=True)
    triple = dot(h_all, w_qkv)
    q, k, v, attended_heads, mixed_t, lse = attention_forward(triple, cosine, sine, begin)


    attended_heads = after(attended_heads, mine, gate_parts)
    mine, d_final_low, gate_parts = after((mine, d_final_low, gate_parts), attended_heads)
    over = swap(mine, "blk", 1)
    up_part = after(gu_part[1], attended_heads)
    up_parts = [swap(up_part, "blk", QUAD * k) for k in range(1, mates)]
    gate_states = [dp_steps(dp_start(g), 0, 1) for g in gate_parts]
    out_full = blank((groups, 2, MODEL_WIDTH // (2 * groups), MODEL_WIDTH), bf16)
    out_full = dp_lay(mine, out_full, core)
    out_full = dp_lay(over, out_full, 1 - core).reshape(MODEL_WIDTH, MODEL_WIDTH)
    attended = lax.all_to_all(
        attended_heads.reshape(members, length, wide), "blk", 0, 0, tiled=True
    )
    a_low = flip(query_key_value_downmap).astype(bf16).reshape(3 * rank, MODEL_WIDTH)
    h_all_late = after(h_all, attended_heads)
    xa_qkv = dot(a_low, h_all_late, NT).astype(bf16)
    chips = members // 2
    xa_qkv = jnp.transpose(xa_qkv.reshape(3 * rank, chips, 2 * length), (1, 0, 2))
    aw_qkv = dot(a_low, w_qkv)
    row = lax.broadcasted_iota(jnp.int32, (3 * rank, 3 * wide), 0) // rank
    column = (lax.broadcasted_iota(jnp.int32, (3 * rank, 3 * wide), 1) // HDIM) % 3
    own_block = row == column
    spread_qkv = jnp.where(own_block, jnp.tile(by_head(b_qkv), (3, 1)), 0.0)
    attended = after(
        attended, xa_qkv, aw_qkv, spread_qkv, out_full, gate_states, up_parts
    )

    attended = jnp.transpose(attended, (1, 0, 2)).reshape(length, MODEL_WIDTH)
    a_out_low = flip(output_adapter_downmap).astype(bf16)
    y_out = dot(jnp.concatenate([attended, a_out_low], axis=0), out_full)
    y_out, aw_out = y_out[:length], y_out[length:]
    residual = x_full + y_out
    normed_two, inverse_two = normalize(residual, feedforward_norm_gain)
    h_two = normed_two.astype(bf16)
    up_parts, d_final_low, gate_states = after((up_parts, d_final_low, gate_states), attended)
    gate_states = [dp_last(dp_steps(state, 1, -1)) for state in gate_states]
    d_final_pair = jnp.concatenate([d_final_low, swap(d_final_low, "blk", 2)], axis=0)
    up_states = [dp_steps(dp_start(g), 0, 1) for g in up_parts]
    h_two = after(h_two, up_states, d_final_pair)

    attended_late = after(attended, h_two)
    xa_out = dot(a_out_low, attended_late, NT).astype(bf16)
    up_states = [dp_last(dp_steps(after(state, h_two), 1, -1)) for state in up_states]
    d_final_pair = after(d_final_pair, h_two)
    d_final_parts = (d_final_pair, swap(d_final_pair, "blk", 1))
    for k_ in range(1, mates):
        gu = dp_lay(gate_states[k_ - 1], gu, (k_, 0))
        gu = dp_lay(up_states[k_ - 1], gu, (k_, 1))
    gu = gu.reshape(mates * 2 * hidden, MODEL_WIDTH)
    a_gu_low = flip(gate_up_adapter_downmap).astype(bf16).reshape(2 * rank, MODEL_WIDTH)
    norms_out = norms[:, :wide].reshape(-1)
    norms_down = norms[:, wide + 2 * hidden : 2 * wide + 2 * hidden].reshape(-1)

    h_two_pair = jnp.concatenate([h_two, swap(h_two, "blk", 2)], axis=0)
    h_two_parts = after((h_two_pair, swap(h_two_pair, "blk", 1)), xa_out, gu, down_rows)
    acts, g_gu, gm_gu, h_two_all, d_final_all = feed_forward(
        gu, down_rows, h_two_parts, d_final_parts, mates
    )
    dh_parts = dot(g_gu, gu, TN).astype(bf16)
    dh_half = quad_halve(dh_parts)
    dh_two = quad_finish(dh_half)

    acts_late, down_late, h_two_late, gu_late = after(
        (acts, down_rows, h_two_all, gu), dh_half
    )
    y_parts = dot(acts_late, down_late, TN).astype(bf16)
    a_down_low = flip(down_adapter_downmap).astype(bf16)
    order = [me ^ (QUAD * k_) for k_ in range(mates)]
    low = jnp.concatenate([home(a_down_low, 1, hidden, who) for who in order], axis=1)
    xa_down = dot(low, acts_late).astype(bf16)
    aw_down = dot(low, down_late)
    xa_gu = dot(a_gu_low, h_two_late, NT).astype(bf16)
    aw_gu = dot(a_gu_low, gu_late, NT)
    dh_two = after(dh_two, y_parts, xa_down, aw_down, xa_gu, aw_gu)

    d_norm_two = normalize_back(residual, inverse_two, feedforward_norm_gain, dh_two)
    d_residual = d_final + d_norm_two
    g_out = d_residual.astype(bf16)
    d_attended = dot(g_out, out_full, NT).astype(bf16)
    d_parts = jnp.transpose(d_attended.reshape(length, members, wide), (1, 0, 2))
    d_heads = lax.all_to_all(d_parts, "blk", 0, 0, tiled=True).reshape(count, wide)

    y_down = quad_finish(quad_halve(after(y_parts, d_parts)))
    result = (residual + y_down).astype(bf16)
    g_late, h_two_late, gu_late, gm_gu = after((g_gu, h_two_all, gu, gm_gu), d_parts)

    def joined(pick):
        return jnp.concatenate([pick(who, i) for who in order for i in range(2)], axis=-1)

    m_gu = joined(lambda who, i: home(gate_up_column_norm[i], 0, hidden, who))
    n_gu_all = joined(
        lambda who, i: lax.dynamic_slice(norms, (who, wide + i * hidden), (1, hidden))[0]
    )
    b_gu = joined(lambda who, i: home(gate_up_adapter_upmap[i], 1, hidden, who))
    s_gu = m_gu / n_gu_all
    gm_gu = gm_gu.reshape(-1) / m_gu
    row = lax.broadcasted_iota(jnp.int32, (2 * rank, b_gu.shape[1]), 0) // rank
    column = (lax.broadcasted_iota(jnp.int32, (2 * rank, b_gu.shape[1]), 1) // hidden) % 2
    own_gu = row == column
    spread = jnp.where(own_gu, jnp.tile(b_gu, (2, 1)), 0.0)
    p_gu = dot((spread * s_gu).astype(bf16), g_late).astype(bf16)
    tilt = (spread * (gm_gu / n_gu_all)).astype(bf16)
    gb_gu = adapter_scale * (dot(xa_gu, g_late, NT) * s_gu - aw_gu * (gm_gu / n_gu_all))
    gb_gu = jnp.sum(jnp.where(own_gu, gb_gu, 0.0).reshape(2, rank, -1), axis=0)
    d_heads = after(d_heads, p_gu, tilt, gb_gu)

    g_three, gm_heads = attention_backward(
        q, k, v, triple, cosine, sine, begin, d_heads, mixed_t, lse
    )
    gm_down = jnp.sum(d_final_low.astype(f32) * y_down, axis=0) / down_column_norm
    g_three = after(g_three, gm_down)
    own_rows, other_rows, grad_a, grad_b, grad_g_attn, gm = back_qkv(
        g_three, h_all, w_qkv, spread_qkv, m_qkv, n_qkv, gm_heads, xa_qkv, aw_qkv
    )
    gm_quad = gm_down + swap(gm_down, "blk", 1)
    total = (own_rows.astype(f32) + swap(other_rows, "blk", 1).astype(f32)).astype(bf16)
    total, gm_quad = after((total, gm_quad))
    state = chips_step(total, 1, None)
    gm_quad = gm_quad + swap(gm_quad, "blk", 2)
    acts_late, d_final_late, dh_late, unit_two, g_out, out_late = after(
        (acts, d_final_all, dh_two, residual * inverse_two, g_out, out_full), gm_quad
    )
    grad_g_ffn = jnp.sum(dh_late * unit_two, axis=0)
    gm_out = jnp.sum(g_out.astype(f32) * y_out, axis=0) / output_column_norm
    s_out = output_column_norm / norms_out
    p_out = dot((output_adapter_upmap * s_out).astype(bf16), g_out, NT).astype(bf16)
    tilt_out = (output_adapter_upmap * (gm_out / norms_out)).astype(bf16)
    ga_out = adapter_scale * (dot(p_out, attended) - dot(tilt_out, out_late, NT))
    gb_out = adapter_scale * (dot(xa_out, g_out) * s_out - aw_out * (gm_out / norms_out))
    s_down = down_column_norm / norms_down
    p_down = dot((down_adapter_upmap * s_down).astype(bf16), d_final_late, NT).astype(bf16)
    state = after(state, ga_out, gb_out, grad_g_ffn, p_down, gm_quad)

    gm_quad, p_down, p_gu, tilt = after((gm_quad, p_down, p_gu, tilt), state)
    ga_gu = adapter_scale * (dot(p_gu, h_two_late) - dot(tilt, gu_late))
    tilt_down = (down_adapter_upmap * (gm_quad / norms_down)).astype(bf16)
    ga_down = adapter_scale * (dot(p_down, acts_late, NT) - dot(tilt_down, down_rows, NT))
    gb_down = adapter_scale * (
        dot(xa_down, d_final_late) * s_down - aw_down * (gm_quad / norms_down)
    )
    room = -hidden % 128
    place = jnp.stack(order)[:, None] == jnp.arange(members)[None, :]

    def spread_shards(array):
        array = jnp.pad(array, [(0, 0)] * (array.ndim - 1) + [(0, room)])
        return sum(
            jnp.where(place[k_][:, None], array[..., k_, None, :], 0.0) for k_ in range(mates)
        )

    gb_both = jnp.swapaxes(gb_gu.reshape(rank, mates, 2, hidden), 1, 2)
    tall = jnp.stack([gb_both[:, 0], gb_both[:, 1], ga_down.reshape(rank, mates, hidden)])
    tall = spread_shards(tall).reshape(3, rank, -1)
    thin = spread_shards(jnp.swapaxes(gm_gu.reshape(mates, 2, hidden), 0, 1)).reshape(2, -1)
    grad_b = jnp.sum(jnp.where(own_block, grad_b, 0.0).reshape(3, rank, 3 * wide), axis=0)
    mine_only = jnp.arange(members)[:, None] == me
    b_all = jnp.where(mine_only, by_three(adapter_scale * grad_b)[:, :, None, :], 0.0)
    b_all = b_all.reshape(3, rank, MODEL_WIDTH)
    m_all = jnp.where(mine_only, by_three(gm)[:, 0][:, None, :], 0.0).reshape(3, MODEL_WIDTH)
    grad_g_attn = grad_g_attn[0] / attention_norm_gain
    grad_a = adapter_scale * grad_a
    tables = (
        [grad_a[i * rank : (i + 1) * rank] for i in range(3)]
        + [b_all[i] for i in range(3)]
        + [ga_out, gb_out, ga_gu[:rank], ga_gu[rank:], gb_down]
        + [tall[0], tall[1], tall[2]]
    )
    vectors = [grad_g_attn, grad_g_ffn, gm_out, gm_down, m_all[0], m_all[1], m_all[2]]
    vectors += [thin[0], thin[1]]
    packed = packed_up(tables, vectors)
    for t in range(2, chips - 1):
        state = chips_step(total, t, state)
    ends = {}

    def between(buffer, stage):
        if stage == 0:
            ends[1] = after(state, buffer)
        if stage == 1:
            buffer = after(buffer, ends[1])
        if stage == 3:
            ends[0] = chips_step(total, chips - 1, after(ends[1], buffer))
        return buffer

    tables, vectors = unpacked(total_sum(packed, between), tables, vectors)
    d_norm_one = normalize_back(
        x_full, inverse_one, attention_norm_gain, chips_end(total, ends[0])
    )
    grad_input = d_residual + d_norm_one
    dense = lambda array: array.reshape(-1, members, hidden + room)[:, :, :hidden].reshape(
        array.shape[:-1] + (members * hidden,)
    )
    a_out, b_out, a_gate, a_up, b_down = tables[6:11]
    b_gate, b_up, a_down = [dense(t) for t in tables[11:]]
    return (
        result,
        grad_input,
        vectors[0],
        vectors[1],
        flip(jnp.stack(tables[:3])),
        jnp.stack(tables[3:6]),
        jnp.stack(vectors[4:7]),
        flip(a_out),
        b_out,
        vectors[2],
        flip(jnp.stack([a_gate, a_up])),
        jnp.stack([b_gate, b_up]),
        jnp.stack([dense(v) for v in vectors[7:]]),
        flip(a_down),
        b_down,
        vectors[3],
    )


def solution(mesh):
    rows, none = P(("dp", "blk"), None), P()
    in_specs = (
        rows,
        rows,
        P("dp", None),
        none,
        none,
        P(None, None, "blk"),
        none,
        none,
        none,
        P(None, "blk"),
        none,
        none,
        none,
        P(None, None, "blk"),
        none,
        none,
        none,
        P(None, "blk"),
        none,
        none,
        none,
    )
    out_specs = (rows, rows) + (none,) * 14
    return jax.shard_map(
        per_device, mesh=mesh, in_specs=in_specs, out_specs=out_specs, check_vma=False
    )
```

```python
import functools

import jax
import jax.numpy as jnp
from jax import lax
from jax.experimental import pallas as pl
from jax.experimental.pallas import tpu as pltpu
from jax.sharding import PartitionSpec as P

MODEL_WIDTH = 2048
HEADS = 16
ADAPTER_RANK = 16
ALPHA = 32
HDIM = 128
TILE = 256
QUAD = 4

norm_eps = 1e-05
column_eps = 1e-06
rope_base = 10000.0
far_negative = -1e30
log2_e = 1.4426950408889634
adapter_scale = ALPHA / ADAPTER_RANK
bf16 = jnp.bfloat16
f32 = jnp.float32
NT = (((1,), (1,)), ((), ()))
TN = (((0,), (0,)), ((), ()))
NN = (((1,), (0,)), ((), ()))


def dot(a, b, dims=NN):
    return lax.dot_general(a, b, dims, preferred_element_type=f32)


def after(array, *earlier):
    return lax.optimization_barrier((array, *earlier))[0]


def blank(shape, dtype):
    return pl.pallas_call(
        lambda out: None,
        out_shape=jax.ShapeDtypeStruct(shape, dtype),
        out_specs=pl.BlockSpec(memory_space=pl.ANY),
        name="blank",
    )()


def swap(array, axis, bit):
    return lax.ppermute(array, axis, [(i, i ^ bit) for i in range(lax.axis_size(axis))])


def axis_sum(array, axis):
    bit = 1
    while bit < lax.axis_size(axis):
        array = array + swap(array, axis, bit)
        bit *= 2
    return array


def begins_of(lens_row, count):
    places = jnp.arange(count, dtype=jnp.int32)
    ends = jnp.cumsum(lens_row, dtype=jnp.int32)
    after = (places[:, None] >= ends[None, :]).astype(jnp.int32)
    return places, jnp.sum(after * lens_row[None, :], axis=1, dtype=jnp.int32), ends[-1]


def split_three(a):
    one = lax.reduce_precision(a, 8, 7)
    rest = a - one
    two = lax.reduce_precision(rest, 8, 7)
    return one.astype(bf16), two.astype(bf16), (rest - two).astype(bf16)


def parts_of(a, b):
    a1, a2, a3 = split_three(a * adapter_scale)
    b1, b2, b3 = split_three(b)
    return (
        jnp.concatenate([a1, a1, a2, a1, a2, a3], axis=-2),
        jnp.concatenate([b1, b2, b1, b3, b2, b1], axis=-2),
    )


def merge_kernel(w_ref, a_ref, b_ref, m_ref, out_ref, n_ref, v_ref):
    rows = w_ref.shape[1]

    def add(i, acc):
        at = pl.ds(pl.multiple_of(i * TILE, TILE), TILE)
        v = w_ref[0, at, :].astype(f32) + dot(a_ref[0, :, at], b_ref[0], TN)
        v_ref[at, :] = v
        return acc + jnp.sum(v * v, axis=0, keepdims=True)

    total = lax.fori_loop(0, rows // TILE, add, jnp.zeros(m_ref.shape, f32), unroll=2)
    norms = jnp.sqrt(total + column_eps)
    n_ref[...] = norms
    s = m_ref[...] / norms

    def put(i, carry):
        at = pl.ds(pl.multiple_of(i * TILE, TILE), TILE)
        out_ref[at, :] = (v_ref[at, :] * s).astype(bf16)
        return carry

    lax.fori_loop(0, rows // TILE, put, 0, unroll=2)


def merge(w, a, b, m):
    k, rows, cols = w.shape
    a_cat, b_cat = parts_of(a, b)
    wide = a_cat.shape[1]
    place = lambda i, h: (0, h * k + i)
    return pl.pallas_call(
        merge_kernel,
        grid=(k, cols // HDIM),
        in_specs=[
            pl.BlockSpec((1, rows, HDIM), lambda i, h: (i, 0, h)),
            pl.BlockSpec((1, wide, rows), lambda i, h: (i, 0, 0)),
            pl.BlockSpec((1, wide, HDIM), lambda i, h: (i, 0, h)),
            pl.BlockSpec((1, HDIM), place),
        ],
        out_specs=[pl.BlockSpec((rows, HDIM), place), pl.BlockSpec((1, HDIM), place)],
        out_shape=[
            jax.ShapeDtypeStruct((rows, k * cols), bf16),
            jax.ShapeDtypeStruct((1, k * cols), f32),
        ],
        scratch_shapes=[pltpu.VMEM((rows, HDIM), f32)],
        compiler_params=pltpu.CompilerParams(vmem_limit_bytes=48 * 2**20),
        cost_estimate=pl.CostEstimate(
            flops=2 * k * rows * cols * wide, bytes_accessed=4 * k * rows * cols, transcendentals=0
        ),
        name="merge",
    )(w, a_cat, b_cat, m)


def merge_rows_kernel(w_ref, a_ref, b_ref, m_ref, out_ref, n_ref):
    out_ref = out_ref.at[0]
    v = w_ref[0].astype(f32) + dot(b_ref[0], a_ref[0], TN)
    norms = jnp.sqrt(jnp.sum(v * v, axis=1, keepdims=True) + column_eps)
    n_ref[0] = norms
    out_ref[0] = (v * (m_ref[0] / norms)).astype(bf16)


def merge_rows(w, a, b, m, mates):
    k, cols, rows = w.shape
    a_cat, b_cat = parts_of(a, b)
    wide = a_cat.shape[1]
    return pl.pallas_call(
        merge_rows_kernel,
        grid=(k,),
        in_specs=[
            pl.BlockSpec((1, cols, rows), lambda i: (i, 0, 0)),
            pl.BlockSpec((1, wide, rows), lambda i: (i, 0, 0)),
            pl.BlockSpec((1, wide, cols), lambda i: (i, 0, 0)),
            pl.BlockSpec((1, cols, 1), lambda i: (i, 0, 0)),
        ],
        out_specs=[
            pl.BlockSpec((1, 1, cols, rows), lambda i: (0, i, 0, 0)),
            pl.BlockSpec((1, cols, 1), lambda i: (i, 0, 0)),
        ],
        out_shape=[
            jax.ShapeDtypeStruct((mates, k, cols, rows), bf16),
            jax.ShapeDtypeStruct((k, cols, 1), f32),
        ],
        compiler_params=pltpu.CompilerParams(vmem_limit_bytes=56 * 2**20),
        cost_estimate=pl.CostEstimate(
            flops=2 * k * rows * cols * wide, bytes_accessed=4 * k * rows * cols, transcendentals=0
        ),
        name="merge_rows",
    )(w, a_cat, b_cat, m)


def turned(u, cosine, sine):
    return u * cosine + pltpu.roll(u, HDIM // 2, 1) * sine


def forward_kernel(
    pre, cosine, sine, begin, q_out, k_out, v_out, att_out, mixed_t, lse_out, v_t
):
    count = pre.shape[0]
    scale = HDIM**-0.5 * log2_e
    for i in range(count // TILE):
        at = pl.ds(i * TILE, TILE)
        cos, sin = cosine[at, :], sine[at, :]
        q_out[at, :] = turned(pre[at, :HDIM], cos, sin).astype(bf16)
        k_out[at, :] = turned(pre[at, HDIM : 2 * HDIM], cos, sin).astype(bf16)
        v = pre[at, 2 * HDIM :]
        v_out[at, :] = v.astype(bf16)
        v_t[:, at] = v.T.astype(bf16)
    for i in range(count // TILE):
        rows = pl.ds(i * TILE, TILE)
        q = q_out[rows, :]
        start = begin[:, rows]

        def visit(j, state, diagonal):
            top, total, mixed = state
            keys = pl.ds(pl.multiple_of(j * TILE, TILE), TILE)
            s = dot(k_out[keys, :], q, NT) * scale
            place = j * TILE + lax.broadcasted_iota(jnp.int32, (TILE, TILE), 0)
            allowed = place >= start
            if diagonal:
                mine = i * TILE + lax.broadcasted_iota(jnp.int32, (TILE, TILE), 1)
                allowed = allowed & (place <= mine)
            s = jnp.where(allowed, s, far_negative)
            high = jnp.maximum(top, jnp.max(s, axis=0, keepdims=True))
            keep = jnp.exp2(top - high)
            p = jnp.exp2(s - high)
            total = total * keep + jnp.sum(p, axis=0, keepdims=True)
            mixed = mixed * keep + dot(v_t[:, keys], p.astype(bf16))
            return high, total, mixed

        state = (
            jnp.full((1, TILE), far_negative, f32),
            jnp.zeros((1, TILE), f32),
            jnp.zeros((HDIM, TILE), f32),
        )
        state = visit(i, state, True)
        for j in range(i):
            state = visit(j, state, False)
        top, total, mixed = state
        mixed = mixed / total
        mixed_t[:, rows] = mixed
        att_out[rows, :] = mixed.T.astype(bf16)
        lse_out[0, :, rows] = top + jnp.log2(total)


def backward_kernel(
    q_ref, k_ref, v_ref, pre, cosine, sine, begin, grad_att, mixed_t, lse,
    g_out, gm_out, dk, dv, k_t,
):
    count = q_ref.shape[0]
    scale = HDIM**-0.5
    dk[...] = jnp.zeros_like(dk)
    dv[...] = jnp.zeros_like(dv)
    for i in range(count // TILE):
        at = pl.ds(i * TILE, TILE)
        k_t[:, at] = k_ref[at, :].astype(f32).T.astype(bf16)
    gm_q = jnp.zeros((1, HDIM), f32)
    for i in range(count // TILE):
        rows = pl.ds(i * TILE, TILE)
        q = q_ref[rows, :]
        d_mixed = grad_att[rows, :]
        delta = jnp.sum(d_mixed.astype(f32).T * mixed_t[:, rows], axis=0, keepdims=True)
        start = begin[:, rows]
        high = lse[0, :, rows]
        dq_t = jnp.zeros((HDIM, TILE), f32)
        for j in range(i + 1):
            keys = pl.ds(j * TILE, TILE)
            s = dot(k_ref[keys, :], q, NT) * (scale * log2_e)
            place = j * TILE + lax.broadcasted_iota(jnp.int32, (TILE, TILE), 0)
            allowed = place >= start
            if j == i:
                mine = i * TILE + lax.broadcasted_iota(jnp.int32, (TILE, TILE), 1)
                allowed = allowed & (place <= mine)
            p = jnp.where(allowed, jnp.exp2(s - high), 0.0)
            dp = dot(v_ref[keys, :], d_mixed, NT)
            ds = (p * (dp - delta)).astype(bf16)
            dv[keys, :] += dot(p.astype(bf16), d_mixed)
            dk[keys, :] += dot(ds, q)
            dq_t = dq_t + dot(k_t[:, keys], ds)
        gq = turned(dq_t.T * scale, cosine[rows, :], -sine[rows, :]).astype(bf16)
        g_out[rows, :HDIM] = gq
        gm_q = gm_q + jnp.sum(gq.astype(f32) * pre[rows, :HDIM], axis=0, keepdims=True)
    gm_k = jnp.zeros((1, HDIM), f32)
    gm_v = jnp.zeros((1, HDIM), f32)
    for i in range(count // TILE):
        at = pl.ds(i * TILE, TILE)
        gk = turned(dk[at, :] * scale, cosine[at, :], -sine[at, :]).astype(bf16)
        g_out[at, HDIM : 2 * HDIM] = gk
        gm_k = gm_k + jnp.sum(gk.astype(f32) * pre[at, HDIM : 2 * HDIM], axis=0, keepdims=True)
        gv = dv[at, :].astype(bf16)
        g_out[at, 2 * HDIM :] = gv
        gm_v = gm_v + jnp.sum(gv.astype(f32) * pre[at, 2 * HDIM :], axis=0, keepdims=True)
    gm_out[0:1, :HDIM] = gm_q
    gm_out[0:1, HDIM : 2 * HDIM] = gm_k
    gm_out[0:1, 2 * HDIM :] = gm_v


def attention_forward(triple, cosine, sine, begin):
    count, width = triple.shape[0], triple.shape[1] // 3
    heads = width // HDIM
    whole = lambda h: (0, 0)
    head = lambda h: (0, h)
    tall = lambda at: pl.BlockSpec((count, HDIM), at)
    return pl.pallas_call(
        forward_kernel,
        grid=(heads,),
        in_specs=[
            pl.BlockSpec((count, 3 * HDIM), head),
            tall(whole),
            tall(whole),
            pl.BlockSpec((1, count), whole),
        ],
        out_specs=[
            tall(head),
            tall(head),
            tall(head),
            tall(head),
            pl.BlockSpec((HDIM, count), lambda h: (h, 0)),
            pl.BlockSpec((1, 1, count), lambda h: (h, 0, 0)),
        ],
        out_shape=[jax.ShapeDtypeStruct((count, width), bf16)] * 4
        + [
            jax.ShapeDtypeStruct((width, count), f32),
            jax.ShapeDtypeStruct((heads, 1, count), f32),
        ],
        scratch_shapes=[pltpu.VMEM((HDIM, count), bf16)],
        compiler_params=pltpu.CompilerParams(vmem_limit_bytes=48 * 2**20),
        cost_estimate=pl.CostEstimate(
            flops=2 * count * count * width, bytes_accessed=30 * count * width, transcendentals=0
        ),
        name="attend",
    )(triple, cosine, sine, begin)


def attention_backward(q, k, v, triple, cosine, sine, begin, grad_att, mixed_t, lse):
    count, width = q.shape
    heads = width // HDIM
    whole = lambda h: (0, 0)
    head = lambda h: (0, h)
    tall = lambda at: pl.BlockSpec((count, HDIM), at)
    return pl.pallas_call(
        backward_kernel,
        grid=(heads,),
        in_specs=[
            tall(head),
            tall(head),
            tall(head),
            pl.BlockSpec((count, 3 * HDIM), head),
            tall(whole),
            tall(whole),
            pl.BlockSpec((1, count), whole),
            tall(head),
            pl.BlockSpec((HDIM, count), lambda h: (h, 0)),
            pl.BlockSpec((1, 1, count), lambda h: (h, 0, 0)),
        ],
        out_specs=[pl.BlockSpec((count, 3 * HDIM), head), pl.BlockSpec((8, 3 * HDIM), head)],
        out_shape=[
            jax.ShapeDtypeStruct((count, 3 * width), bf16),
            jax.ShapeDtypeStruct((8, 3 * width), f32),
        ],
        scratch_shapes=[
            pltpu.VMEM((count, HDIM), f32),
            pltpu.VMEM((count, HDIM), f32),
            pltpu.VMEM((HDIM, count), bf16),
        ],
        compiler_params=pltpu.CompilerParams(vmem_limit_bytes=48 * 2**20),
        cost_estimate=pl.CostEstimate(
            flops=5 * count * count * width, bytes_accessed=40 * count * width, transcendentals=0
        ),
        name="attend_back",
    )(q, k, v, triple, cosine, sine, begin, grad_att, mixed_t, lse)


def feed_kernel(
    gu_ref, down_ref, h_pair, h_other, d_pair, d_other, acts_out, g_out, gm_out, h_ref, d_ref
):
    half = h_pair.shape[0]

    @pl.when((pl.program_id(0) == 0) & (pl.program_id(1) == 0))
    def _():
        h_ref[:half] = h_pair[...]
        h_ref[half:] = h_other[...]
        d_ref[:half] = d_pair[...]
        d_ref[half:] = d_other[...]

    h = h_ref[...]
    gate = dot(gu_ref[0, 0], h, NT)
    upward = dot(gu_ref[0, 1], h, NT)
    d_act = dot(down_ref[...], d_ref[...], NT)
    sigmoid_gate = jax.nn.sigmoid(gate)
    silu = gate * sigmoid_gate
    acts_out[...] = (silu * upward).astype(bf16)
    d_gate = (d_act * upward * sigmoid_gate * (1.0 + gate * (1.0 - sigmoid_gate))).astype(bf16)
    d_upward = (d_act * silu).astype(bf16)
    g_out[0, 0] = d_gate
    g_out[0, 1] = d_upward
    gm_out[0, 0] = jnp.sum(d_gate.astype(f32) * gate, axis=1, keepdims=True)
    gm_out[0, 1] = jnp.sum(d_upward.astype(f32) * upward, axis=1, keepdims=True)


def feed_forward(gu, down, h, d, mates):
    rows, width = 2 * h[0].shape[0], h[0].shape[1]
    hidden = down.shape[0] // mates
    unit = hidden // max(1, hidden // 352)
    steps = hidden // unit
    flat = lambda k, j: (k * steps + j, 0)
    deep = lambda k, j: (k, 0, j, 0)
    whole = lambda k, j: (0, 0)
    once = pl.BlockSpec((rows // 2, width), whole, pipeline_mode=pl.Buffered(1))
    acts, g, gm, h_all, d_all = pl.pallas_call(
        feed_kernel,
        grid=(mates, steps),
        in_specs=[
            pl.BlockSpec((1, 2, unit, width), deep),
            pl.BlockSpec((unit, width), flat),
            once,
            once,
            once,
            once,
        ],
        out_specs=[
            pl.BlockSpec((unit, rows), flat),
            pl.BlockSpec((1, 2, unit, rows), deep),
            pl.BlockSpec((1, 2, unit, 1), deep),
            pl.BlockSpec((rows, width), whole),
            pl.BlockSpec((rows, width), whole),
        ],
        out_shape=[
            jax.ShapeDtypeStruct((mates * hidden, rows), bf16),
            jax.ShapeDtypeStruct((mates, 2, hidden, rows), bf16),
            jax.ShapeDtypeStruct((mates, 2, hidden, 1), f32),
            jax.ShapeDtypeStruct((rows, width), bf16),
            jax.ShapeDtypeStruct((rows, width), bf16),
        ],
        compiler_params=pltpu.CompilerParams(vmem_limit_bytes=58 * 2**20),
        cost_estimate=pl.CostEstimate(
            flops=6 * mates * hidden * rows * width,
            bytes_accessed=6 * mates * hidden * width + 4 * rows * width,
            transcendentals=0,
        ),
        name="feed_forward",
    )(gu.reshape(mates, 2, hidden, width), down, *h, *d)
    return acts, g.reshape(2 * mates * hidden, rows), gm, h_all, d_all


def back_kernel(
    core, g_ref, h_ref, w_ref, spread, s_ref, over_n, sums, m_ref, xa_ref, aw_ref,
    own_out, other_out, ga_out, gb_out, gg_out, gm_out,
):
    step = pl.program_id(0)
    length = own_out.shape[1]
    g = g_ref[...]
    h = h_ref[...]
    s = s_ref[...]
    dh = dot(g, w_ref[...], NT)
    low = dh.astype(bf16)

    @pl.when(core[0] == 0)
    def _():
        own_out[0] = low[:length]
        other_out[0] = low[length:]

    @pl.when(core[0] != 0)
    def _():
        own_out[0] = low[length:]
        other_out[0] = low[:length]

    p = dot((spread[...] * s).astype(bf16), g, NT).astype(bf16)
    ga = dot(p, h)
    gb = dot(xa_ref[...], g)
    gg = jnp.sum(dh * h.astype(f32), axis=0, keepdims=True)

    @pl.when(step == 0)
    def _():
        gm = sums[0:1, :] / m_ref[...]
        gm_out[...] = gm
        tilt = (spread[...] * (gm * over_n[...])).astype(bf16)
        ga_out[...] = ga - dot(tilt, w_ref[...], NT)
        gb_out[...] = gb * s - aw_ref[...] * (gm * over_n[...])
        gg_out[...] = gg

    @pl.when(step > 0)
    def _():
        ga_out[...] += ga
        gb_out[...] += gb * s
        gg_out[...] += gg


def back_qkv(g, h, w, spread, m, n, sums, xa, aw):
    chips = lax.axis_size("blk") // 2
    core = (lax.axis_index("blk") % 2).astype(jnp.int32).reshape(1)
    count, cols = g.shape
    width = h.shape[1]
    pair = count // chips
    wide = spread.shape[0]
    rows = lambda i, core: (i, 0)
    whole = lambda i, core: (0, 0)
    deep = lambda i, core: (i, 0, 0)
    return pl.pallas_call(
        back_kernel,
        grid_spec=pltpu.PrefetchScalarGridSpec(
            num_scalar_prefetch=1,
            grid=(chips,),
            in_specs=[
                pl.BlockSpec((pair, cols), rows),
                pl.BlockSpec((pair, width), rows),
                pl.BlockSpec((width, cols), whole),
                pl.BlockSpec((wide, cols), whole),
                pl.BlockSpec((1, cols), whole),
                pl.BlockSpec((1, cols), whole),
                pl.BlockSpec((8, cols), whole),
                pl.BlockSpec((1, cols), whole),
                pl.BlockSpec((None, wide, pair), deep),
                pl.BlockSpec((wide, cols), whole),
            ],
            out_specs=[
                pl.BlockSpec((1, pair // 2, width), deep),
                pl.BlockSpec((1, pair // 2, width), deep),
                pl.BlockSpec((wide, width), whole),
                pl.BlockSpec((wide, cols), whole),
                pl.BlockSpec((1, width), whole),
                pl.BlockSpec((1, cols), whole),
            ],
        ),
        out_shape=[
            jax.ShapeDtypeStruct((chips, pair // 2, width), bf16),
            jax.ShapeDtypeStruct((chips, pair // 2, width), bf16),
            jax.ShapeDtypeStruct((wide, width), f32),
            jax.ShapeDtypeStruct((wide, cols), f32),
            jax.ShapeDtypeStruct((1, width), f32),
            jax.ShapeDtypeStruct((1, cols), f32),
        ],
        compiler_params=pltpu.CompilerParams(vmem_limit_bytes=56 * 2**20),
        cost_estimate=pl.CostEstimate(
            flops=3 * count * cols * width, bytes_accessed=8 * count * width, transcendentals=0
        ),
        name="back_qkv",
    )(core, g, h, w, spread, m / n, 1.0 / n, sums, m, xa, aw)


def normalize(values, gain):
    inverse = lax.rsqrt(jnp.mean(values * values, axis=-1, keepdims=True) + norm_eps)
    return (values * inverse * gain, inverse)


def normalize_back(values, inverse, gain, grad):
    unit = values * inverse
    scaled = grad * gain
    return inverse * (scaled - unit * jnp.mean(scaled * unit, axis=-1, keepdims=True))


def quad_halve(parts):
    half = parts.shape[0] // 2
    return parts[:half].astype(f32) + swap(parts[half:], "blk", 1).astype(f32)


def quad_finish(mine):
    half = mine.shape[0] // 2
    return mine[:half] + swap(mine[half:].astype(bf16), "blk", 2).astype(f32)


def step_chips(array, first, last, by):
    pairs = [(2 * i + c, 2 * (i + by) + c) for i in range(first, last + 1) for c in range(2)]
    return lax.ppermute(array, "blk", pairs)


def chips_step(total, t, state):
    chips = total.shape[0]
    chip = lax.axis_index("blk") // 2
    pick = lambda c: lax.dynamic_index_in_dim(
        total, jnp.clip(c, 0, chips - 1), 0, keepdims=False
    )
    up, down = pick(chips - t + chip), pick(t - chips + chip)
    if t > 1:
        up = (up.astype(f32) + state[0].astype(f32)).astype(bf16)
        down = (down.astype(f32) + state[1].astype(f32)).astype(bf16)
    up, down = after((up, down))
    return step_chips(up, 0, t - 1, 1), step_chips(down, chips - t, chips - 1, -1)


def chips_end(total, state):
    chip = lax.axis_index("blk") // 2
    own = lax.dynamic_index_in_dim(total, chip, 0, keepdims=False)
    return own.astype(f32) + state[0].astype(f32) + state[1].astype(f32)


def dp_start(piece):
    half = piece.shape[0] // 2
    return piece[None, :half], piece[None, half:]


def dp_steps(state, first=None, last=None):
    bits = [1 << i for i in range(lax.axis_size("dp").bit_length() - 1)]
    one, two = state
    for step in range(len(bits))[first:last]:
        one = jnp.concatenate([one, swap(one, "dp", bits[step])], axis=0)
        two = jnp.concatenate([two, swap(two, "dp", bits[::-1][step])], axis=0)
    return one, two


def dp_last(state):
    bits = [1 << i for i in range(lax.axis_size("dp").bit_length() - 1)]
    one, two = state
    return jnp.concatenate(
        [one, swap(one, "dp", bits[-1]), two, swap(two, "dp", bits[0])], axis=0
    )


def dp_places():
    groups = lax.axis_size("dp")
    bits = groups.bit_length() - 1
    who = jnp.arange(groups, dtype=jnp.int32) ^ lax.axis_index("dp")
    turned = sum(((who >> i) & 1) << (bits - 1 - i) for i in range(bits))
    return jnp.stack([who, turned + groups]).astype(jnp.int32)


def lay_kernel(places, one, two, into, out):
    place = out.at[0, 0] if len(out.shape) == 5 else out.at[0, 0, 0]
    place[0] = one[0]
    place[1] = two[0]


def dp_lay(state, into, at):
    groups, half, width = state.shape[0] // 2, state.shape[1], state.shape[2]
    shape = into.shape
    if isinstance(at, tuple):
        split = into.reshape(shape[0], shape[1], groups, 2, half, width)
        block = (1, 1, 1, 2, half, width)
        where = lambda c, places: (at[0], at[1], c, 0, 0, 0)
        second = jnp.zeros((1, groups), jnp.int32)
    else:
        split = into.reshape(groups, 2, 2, half, width)
        block = (1, 1, 2, half, width)
        where = lambda c, places: (c, places[2, c], 0, 0, 0)
        second = jnp.full((1, groups), at, jnp.int32)
    out = pl.pallas_call(
        lay_kernel,
        grid_spec=pltpu.PrefetchScalarGridSpec(
            num_scalar_prefetch=1,
            grid=(groups,),
            in_specs=[
                pl.BlockSpec((1, half, width), lambda c, places: (places[0, c], 0, 0)),
                pl.BlockSpec((1, half, width), lambda c, places: (places[1, c], 0, 0)),
                pl.BlockSpec(memory_space=pl.ANY),
            ],
            out_specs=pl.BlockSpec(block, where),
        ),
        out_shape=jax.ShapeDtypeStruct(split.shape, into.dtype),
        input_output_aliases={3: 0},
        name="lay",
    )(jnp.concatenate([dp_places(), second]), state, state, split)
    return out.reshape(shape)


def total_sum(buffer, between):
    stages = [("blk", 2, 1), ("dp", lax.axis_size("dp"), 1), ("blk", lax.axis_size("blk") // 2, 2)]
    for number, (axis, ways, unit) in enumerate(stages):
        part = buffer.shape[1] // ways
        mine = (lax.axis_index(axis) // unit) % ways
        cut = lambda d: lax.dynamic_slice_in_dim(buffer, (mine ^ d) * part, part, 1)
        arrived = [swap(cut(d), axis, d * unit) for d in range(1, ways)]
        buffer = between(functools.reduce(jnp.add, arrived, cut(0)), number)
    for number, (axis, ways, unit) in enumerate(stages[::-1]):
        part = buffer.shape[1]
        mine = (lax.axis_index(axis) // unit) % ways
        whole = blank((buffer.shape[0], ways * part), f32)
        for d in range(ways):
            piece = swap(buffer, axis, d * unit) if d else buffer
            whole = lax.dynamic_update_slice_in_dim(whole, piece, (mine ^ d) * part, 1)
        buffer = between(whole, 3 + number)
    return buffer


def packed_up(tables, vectors):
    devices = lax.axis_size("dp") * lax.axis_size("blk")
    joined = jnp.concatenate([*tables, *[v.reshape(16, -1) for v in vectors]], axis=1)
    return jnp.pad(joined, ((0, 0), (0, -joined.shape[1] % (128 * devices))))


def unpacked(joined, tables, vectors):
    out, at = [], 0
    for t in (*tables, *vectors):
        size = t.size // 16
        out.append(joined[:, at : at + size].reshape(t.shape))
        at += size
    return out[: len(tables)], out[len(tables) :]


def per_device(
    tokens,
    cotangent,
    document_length_list,
    attention_norm_gain,
    feedforward_norm_gain,
    frozen_query_key_value,
    query_key_value_downmap,
    query_key_value_upmap,
    query_key_value_norm,
    frozen_output_weight,
    output_adapter_downmap,
    output_adapter_upmap,
    output_column_norm,
    frozen_gate_up_weight,
    gate_up_adapter_downmap,
    gate_up_adapter_upmap,
    gate_up_column_norm,
    frozen_down_weight,
    down_adapter_downmap,
    down_adapter_upmap,
    down_column_norm,
):
    length = tokens.shape[0]
    members, groups = lax.axis_size("blk"), lax.axis_size("dp")
    me, line = lax.axis_index("blk"), lax.axis_index("dp")
    count = length * members
    mates = members // QUAD
    wide = frozen_output_weight.shape[1]
    heads = wide // HDIM
    hidden = frozen_gate_up_weight.shape[2]
    lens_row = document_length_list[0]
    rank = ADAPTER_RANK
    flip = lambda a: jnp.swapaxes(a, -1, -2)

    def home(array, axis, width, who=None):
        return lax.dynamic_slice_in_dim(array, (me if who is None else who) * width, width, axis)

    def by_head(array):
        split = array.reshape(3, array.shape[1], heads, HDIM)
        return jnp.transpose(split, (1, 2, 0, 3)).reshape(array.shape[1], 3 * wide)

    def by_three(array):
        split = array.reshape(array.shape[0], heads, 3, HDIM)
        return jnp.transpose(split, (2, 0, 1, 3)).reshape(3, array.shape[0], wide)

    x_full = tokens.astype(f32)
    normed_one, inverse_one = normalize(x_full, attention_norm_gain)
    h_one = normed_one.astype(bf16)
    h_all = lax.all_gather(h_one, "blk", axis=0, tiled=True)

    w_out, n_out = merge(
        after(frozen_output_weight, h_one)[None],
        flip(output_adapter_downmap)[None],
        home(output_adapter_upmap, 1, wide)[None],
        home(output_column_norm, 0, wide)[None],
    )
    gu, n_gu = merge_rows(
        flip(frozen_gate_up_weight),
        flip(gate_up_adapter_downmap),
        home(gate_up_adapter_upmap, 2, hidden),
        home(gate_up_column_norm, 1, hidden)[:, :, None],
        mates,
    )
    b_qkv = home(query_key_value_upmap, 2, wide)
    m_qkv = by_head(home(query_key_value_norm, 1, wide)[:, None, :])
    w_qkv, n_qkv = merge(frozen_query_key_value, flip(query_key_value_downmap), b_qkv, m_qkv)
    w_down, n_down = merge(
        frozen_down_weight[None],
        flip(down_adapter_downmap)[None],
        home(down_adapter_upmap, 1, wide)[None],
        home(down_column_norm, 0, wide)[None],
    )
    places, begins, end = begins_of(lens_row, count)
    half = HDIM // 2
    freq = rope_base ** (-(jnp.arange(half, dtype=f32) * 2.0 / HDIM))
    angle = (places - begins).astype(f32)[:, None] * freq[None, :]
    cosine, sine = jnp.cos(angle), jnp.sin(angle)
    cosine = jnp.concatenate([cosine, cosine], axis=1)
    sine = jnp.concatenate([-sine, sine], axis=1)
    begin = begins[None, :]
    valid = (me * length + jnp.arange(length, dtype=jnp.int32)) < end
    d_final = cotangent.astype(f32) * valid.astype(f32)[:, None]
    d_final_low = d_final.astype(bf16)

    def spread_rows(chunks):
        got = lax.all_to_all(chunks, "blk", 0, 0, tiled=True)
        return jnp.transpose(got, (1, 0, 2)).reshape(chunks.shape[1], members * wide)

    def spread_rows(chunks):
        got = lax.all_to_all(chunks, "blk", 0, 0, tiled=True)
        return jnp.transpose(got, (1, 0, 2)).reshape(chunks.shape[1], members * wide)

    w_out, gu = after((w_out, gu), w_qkv, w_down, cosine, sine)
    piece = MODEL_WIDTH // (2 * groups)
    core = me % 2
    pair = lax.dynamic_slice_in_dim(w_out, 2 * line * piece, 2 * piece, 0)
    pair = pair.reshape(1, 2, piece, wide)
    mine = spread_rows(jnp.tile(pair, (members // 2, 1, 1, 1)).reshape(members, piece, wide))
    mine = dp_steps(dp_start(mine), 0, 1)
    piece = mates * hidden // groups
    per_shard = groups // mates
    turn = line // per_shard
    shards = lax.dynamic_slice_in_dim(
        after(w_down, w_out).reshape(mates, QUAD, hidden, wide),
        (line % per_shard) * piece,
        piece,
        2,
    )
    chosen = jnp.stack(
        [
            functools.reduce(
                lambda rest, k: jnp.where(turn == k, shards[q ^ k], rest),
                range(1, mates),
                shards[q],
            )
            for q in range(mates)
        ]
    ).reshape(members, piece, wide)
    own = jnp.concatenate([n_out[0], n_gu[0, :, 0], n_gu[1, :, 0], n_down[0]])
    own = jnp.pad(own, (0, -own.shape[0] % wide)).reshape(-1, wide)
    own_high = lax.reduce_precision(own, 8, 7)
    riders = jnp.concatenate([own_high, own - own_high], axis=0).astype(bf16)
    extra = -riders.shape[0] % 16
    riders = jnp.pad(riders, ((0, extra), (0, 0)))
    riders = jnp.broadcast_to(riders[None], (members, *riders.shape))
    rows_down = spread_rows(jnp.concatenate([chosen, riders], axis=1))
    norm_rows = rows_down[piece:].astype(f32)
    norms = norm_rows[: own.shape[0]] + norm_rows[own.shape[0] : 2 * own.shape[0]]
    norms = jnp.transpose(norms.reshape(own.shape[0], members, wide), (1, 0, 2))
    norms = norms.reshape(members, own.shape[0] * wide)
    rows_down = rows_down[:piece]
    piece_gu = hidden // groups
    gu_part = lax.dynamic_slice(
        gu, (0, 0, line * piece_gu, 0), (1, 2, piece_gu, MODEL_WIDTH)
    ).reshape(2, piece_gu, MODEL_WIDTH)
    gate_part = after(gu_part[0], rows_down)
    gate_parts = [swap(gate_part, "blk", QUAD * k) for k in range(1, mates)]
    h_all, d_final_low, mine, rows_down = after((h_all, d_final_low, mine, rows_down), cosine)

    mine = dp_last(dp_steps(mine, 1, -1))
    down_rows = lax.all_gather(rows_down, "dp", axis=0, tiled=True)
    triple = dot(h_all, w_qkv)
    q, k, v, attended_heads, mixed_t, lse = attention_forward(triple, cosine, sine, begin)


    attended_heads = after(attended_heads, mine, gate_parts)
    mine, d_final_low, gate_parts = after((mine, d_final_low, gate_parts), attended_heads)
    over = swap(mine, "blk", 1)
    up_part = after(gu_part[1], attended_heads)
    up_parts = [swap(up_part, "blk", QUAD * k) for k in range(1, mates)]
    gate_states = [dp_steps(dp_start(g), 0, 1) for g in gate_parts]
    out_full = blank((groups, 2, MODEL_WIDTH // (2 * groups), MODEL_WIDTH), bf16)
    out_full = dp_lay(mine, out_full, core)
    out_full = dp_lay(over, out_full, 1 - core).reshape(MODEL_WIDTH, MODEL_WIDTH)
    attended = lax.all_to_all(
        attended_heads.reshape(members, length, wide), "blk", 0, 0, tiled=True
    )
    a_low = flip(query_key_value_downmap).astype(bf16).reshape(3 * rank, MODEL_WIDTH)
    h_all_late = after(h_all, attended_heads)
    xa_qkv = dot(a_low, h_all_late, NT).astype(bf16)
    chips = members // 2
    xa_qkv = jnp.transpose(xa_qkv.reshape(3 * rank, chips, 2 * length), (1, 0, 2))
    aw_qkv = dot(a_low, w_qkv)
    row = lax.broadcasted_iota(jnp.int32, (3 * rank, 3 * wide), 0) // rank
    column = (lax.broadcasted_iota(jnp.int32, (3 * rank, 3 * wide), 1) // HDIM) % 3
    own_block = row == column
    spread_qkv = jnp.where(own_block, jnp.tile(by_head(b_qkv), (3, 1)), 0.0)
    attended = after(
        attended, xa_qkv, aw_qkv, spread_qkv, out_full, gate_states, up_parts
    )

    attended = jnp.transpose(attended, (1, 0, 2)).reshape(length, MODEL_WIDTH)
    a_out_low = flip(output_adapter_downmap).astype(bf16)
    y_out = dot(jnp.concatenate([attended, a_out_low], axis=0), out_full)
    y_out, aw_out = y_out[:length], y_out[length:]
    residual = x_full + y_out
    normed_two, inverse_two = normalize(residual, feedforward_norm_gain)
    h_two = normed_two.astype(bf16)
    up_parts, d_final_low, gate_states = after((up_parts, d_final_low, gate_states), attended)
    gate_states = [dp_last(dp_steps(state, 1, -1)) for state in gate_states]
    d_final_pair = jnp.concatenate([d_final_low, swap(d_final_low, "blk", 2)], axis=0)
    up_states = [dp_steps(dp_start(g), 0, 1) for g in up_parts]
    h_two = after(h_two, up_states)

    attended_late = after(attended, h_two)
    xa_out = dot(a_out_low, attended_late, NT).astype(bf16)
    up_states = [dp_last(dp_steps(after(state, h_two), 1, -1)) for state in up_states]
    d_final_pair = after(d_final_pair, h_two)
    d_final_parts = (d_final_pair, swap(d_final_pair, "blk", 1))
    for k_ in range(1, mates):
        gu = dp_lay(gate_states[k_ - 1], gu, (k_, 0))
        gu = dp_lay(up_states[k_ - 1], gu, (k_, 1))
    gu = gu.reshape(mates * 2 * hidden, MODEL_WIDTH)
    a_gu_low = flip(gate_up_adapter_downmap).astype(bf16).reshape(2 * rank, MODEL_WIDTH)
    norms_out = norms[:, :wide].reshape(-1)
    norms_down = norms[:, wide + 2 * hidden : 2 * wide + 2 * hidden].reshape(-1)

    h_two_pair = jnp.concatenate([h_two, swap(h_two, "blk", 2)], axis=0)
    h_two_parts = after((h_two_pair, swap(h_two_pair, "blk", 1)), xa_out, gu, down_rows)
    acts, g_gu, gm_gu, h_two_all, d_final_all = feed_forward(
        gu, down_rows, h_two_parts, d_final_parts, mates
    )
    dh_parts = dot(g_gu, gu, TN).astype(bf16)
    dh_half = quad_halve(dh_parts)
    dh_two = quad_finish(dh_half)

    acts_late, down_late, h_two_late, gu_late = after(
        (acts, down_rows, h_two_all, gu), dh_half
    )
    y_parts = dot(acts_late, down_late, TN).astype(bf16)
    a_down_low = flip(down_adapter_downmap).astype(bf16)
    order = [me ^ (QUAD * k_) for k_ in range(mates)]
    low = jnp.concatenate([home(a_down_low, 1, hidden, who) for who in order], axis=1)
    xa_down = dot(low, acts_late).astype(bf16)
    aw_down = dot(low, down_late)
    xa_gu = dot(a_gu_low, h_two_late, NT).astype(bf16)
    aw_gu = dot(a_gu_low, gu_late, NT)
    dh_two = after(dh_two, y_parts, xa_down, aw_down, xa_gu, aw_gu)

    d_norm_two = normalize_back(residual, inverse_two, feedforward_norm_gain, dh_two)
    d_residual = d_final + d_norm_two
    g_out = d_residual.astype(bf16)
    d_attended = dot(g_out, out_full, NT).astype(bf16)
    d_parts = jnp.transpose(d_attended.reshape(length, members, wide), (1, 0, 2))
    d_heads = lax.all_to_all(d_parts, "blk", 0, 0, tiled=True).reshape(count, wide)

    y_down = quad_finish(quad_halve(after(y_parts, d_parts)))
    result = (residual + y_down).astype(bf16)
    g_late, h_two_late, gu_late, gm_gu = after((g_gu, h_two_all, gu, gm_gu), d_parts)

    def joined(pick):
        return jnp.concatenate([pick(who, i) for who in order for i in range(2)], axis=-1)

    m_gu = joined(lambda who, i: home(gate_up_column_norm[i], 0, hidden, who))
    n_gu_all = joined(
        lambda who, i: lax.dynamic_slice(norms, (who, wide + i * hidden), (1, hidden))[0]
    )
    b_gu = joined(lambda who, i: home(gate_up_adapter_upmap[i], 1, hidden, who))
    s_gu = m_gu / n_gu_all
    gm_gu = gm_gu.reshape(-1) / m_gu
    row = lax.broadcasted_iota(jnp.int32, (2 * rank, b_gu.shape[1]), 0) // rank
    column = (lax.broadcasted_iota(jnp.int32, (2 * rank, b_gu.shape[1]), 1) // hidden) % 2
    own_gu = row == column
    spread = jnp.where(own_gu, jnp.tile(b_gu, (2, 1)), 0.0)
    p_gu = dot((spread * s_gu).astype(bf16), g_late).astype(bf16)
    tilt = (spread * (gm_gu / n_gu_all)).astype(bf16)
    gb_gu = adapter_scale * (dot(xa_gu, g_late, NT) * s_gu - aw_gu * (gm_gu / n_gu_all))
    gb_gu = jnp.sum(jnp.where(own_gu, gb_gu, 0.0).reshape(2, rank, -1), axis=0)
    d_heads = after(d_heads, p_gu, tilt, gb_gu)

    g_three, gm_heads = attention_backward(
        q, k, v, triple, cosine, sine, begin, d_heads, mixed_t, lse
    )
    gm_down = jnp.sum(d_final_low.astype(f32) * y_down, axis=0) / down_column_norm
    g_three = after(g_three, gm_down)
    own_rows, other_rows, grad_a, grad_b, grad_g_attn, gm = back_qkv(
        g_three, h_all, w_qkv, spread_qkv, m_qkv, n_qkv, gm_heads, xa_qkv, aw_qkv
    )
    gm_quad = gm_down + swap(gm_down, "blk", 1)
    total = (own_rows.astype(f32) + swap(other_rows, "blk", 1).astype(f32)).astype(bf16)
    total, gm_quad = after((total, gm_quad))
    state = chips_step(total, 1, None)
    gm_quad = gm_quad + swap(gm_quad, "blk", 2)
    acts_late, d_final_late, dh_late, unit_two, g_out, out_late = after(
        (acts, d_final_all, dh_two, residual * inverse_two, g_out, out_full), gm_quad
    )
    grad_g_ffn = jnp.sum(dh_late * unit_two, axis=0)
    gm_out = jnp.sum(g_out.astype(f32) * y_out, axis=0) / output_column_norm
    s_out = output_column_norm / norms_out
    p_out = dot((output_adapter_upmap * s_out).astype(bf16), g_out, NT).astype(bf16)
    tilt_out = (output_adapter_upmap * (gm_out / norms_out)).astype(bf16)
    ga_out = adapter_scale * (dot(p_out, attended) - dot(tilt_out, out_late, NT))
    gb_out = adapter_scale * (dot(xa_out, g_out) * s_out - aw_out * (gm_out / norms_out))
    s_down = down_column_norm / norms_down
    p_down = dot((down_adapter_upmap * s_down).astype(bf16), d_final_late, NT).astype(bf16)
    state = after(state, ga_out, gb_out, grad_g_ffn, p_down, gm_quad)

    gm_quad, p_down, p_gu, tilt = after((gm_quad, p_down, p_gu, tilt), state)
    ga_gu = adapter_scale * (dot(p_gu, h_two_late) - dot(tilt, gu_late))
    tilt_down = (down_adapter_upmap * (gm_quad / norms_down)).astype(bf16)
    ga_down = adapter_scale * (dot(p_down, acts_late, NT) - dot(tilt_down, down_rows, NT))
    gb_down = adapter_scale * (
        dot(xa_down, d_final_late) * s_down - aw_down * (gm_quad / norms_down)
    )
    room = -hidden % 128
    place = jnp.stack(order)[:, None] == jnp.arange(members)[None, :]

    def spread_shards(array):
        array = jnp.pad(array, [(0, 0)] * (array.ndim - 1) + [(0, room)])
        return sum(
            jnp.where(place[k_][:, None], array[..., k_, None, :], 0.0) for k_ in range(mates)
        )

    gb_both = jnp.swapaxes(gb_gu.reshape(rank, mates, 2, hidden), 1, 2)
    tall = jnp.stack([gb_both[:, 0], gb_both[:, 1], ga_down.reshape(rank, mates, hidden)])
    tall = spread_shards(tall).reshape(3, rank, -1)
    thin = spread_shards(jnp.swapaxes(gm_gu.reshape(mates, 2, hidden), 0, 1)).reshape(2, -1)
    grad_b = jnp.sum(jnp.where(own_block, grad_b, 0.0).reshape(3, rank, 3 * wide), axis=0)
    mine_only = jnp.arange(members)[:, None] == me
    b_all = jnp.where(mine_only, by_three(adapter_scale * grad_b)[:, :, None, :], 0.0)
    b_all = b_all.reshape(3, rank, MODEL_WIDTH)
    m_all = jnp.where(mine_only, by_three(gm)[:, 0][:, None, :], 0.0).reshape(3, MODEL_WIDTH)
    grad_g_attn = grad_g_attn[0] / attention_norm_gain
    grad_a = adapter_scale * grad_a
    tables = (
        [grad_a[i * rank : (i + 1) * rank] for i in range(3)]
        + [b_all[i] for i in range(3)]
        + [ga_out, gb_out, ga_gu[:rank], ga_gu[rank:], gb_down]
        + [tall[0], tall[1], tall[2]]
    )
    vectors = [grad_g_attn, grad_g_ffn, gm_out, gm_down, m_all[0], m_all[1], m_all[2]]
    vectors += [thin[0], thin[1]]
    packed = packed_up(tables, vectors)
    for t in range(2, chips - 1):
        state = chips_step(total, t, state)
    ends = {}

    def between(buffer, stage):
        if stage == 0:
            ends[1] = after(state, buffer)
        if stage == 1:
            buffer = after(buffer, ends[1])
        if stage == 3:
            ends[0] = chips_step(total, chips - 1, after(ends[1], buffer))
        return buffer

    tables, vectors = unpacked(total_sum(packed, between), tables, vectors)
    d_norm_one = normalize_back(
        x_full, inverse_one, attention_norm_gain, chips_end(total, ends[0])
    )
    grad_input = d_residual + d_norm_one
    dense = lambda array: array.reshape(-1, members, hidden + room)[:, :, :hidden].reshape(
        array.shape[:-1] + (members * hidden,)
    )
    a_out, b_out, a_gate, a_up, b_down = tables[6:11]
    b_gate, b_up, a_down = [dense(t) for t in tables[11:]]
    return (
        result,
        grad_input,
        vectors[0],
        vectors[1],
        flip(jnp.stack(tables[:3])),
        jnp.stack(tables[3:6]),
        jnp.stack(vectors[4:7]),
        flip(a_out),
        b_out,
        vectors[2],
        flip(jnp.stack([a_gate, a_up])),
        jnp.stack([b_gate, b_up]),
        jnp.stack([dense(v) for v in vectors[7:]]),
        flip(a_down),
        b_down,
        vectors[3],
    )


def solution(mesh):
    rows, none = P(("dp", "blk"), None), P()
    in_specs = (
        rows,
        rows,
        P("dp", None),
        none,
        none,
        P(None, None, "blk"),
        none,
        none,
        none,
        P(None, "blk"),
        none,
        none,
        none,
        P(None, None, "blk"),
        none,
        none,
        none,
        P(None, "blk"),
        none,
        none,
        none,
    )
    out_specs = (rows, rows) + (none,) * 14
    return jax.shard_map(
        per_device, mesh=mesh, in_specs=in_specs, out_specs=out_specs, check_vma=False
    )
```
